32 devices in a mesh: fsdp: 8 (over z, core), seq: 4 (over y, x).
Axes of the slice: x: 2, y: 2, z: 4, core: 2. Of those that a mesh axis runs over, the one named last changes fastest.
Arguments:
- tokens: bfloat16 [3, 32, 320, 1024], P(None, ('fsdp', 'seq')), may hold values from -6 to 6
- counts: int32 [3, 32], P(None, 'fsdp'), may hold values from 64 to 320, as said below
- ln1_gain: bfloat16 [1024], P('fsdp'), may hold values from 0.5 to 1.5
- ln1_shift: bfloat16 [1024], P('fsdp'), may hold values from -1.75 to 1.75
- w_qkv: bfloat16 [1024, 3072], P('fsdp'), may hold values from -0.1875 to 0.1875
- b_qv: bfloat16 [2048], P('fsdp'), may hold values from -1.75 to 1.75
- w_out: bfloat16 [1024, 1024], P('fsdp'), may hold values from -1.5 to 1.5
- b_out: bfloat16 [1024], P('fsdp'), may hold values from -1.75 to 1.75
- ln2_gain: bfloat16 [1024], P('fsdp'), may hold values from 0.5 to 1.5
- ln2_shift: bfloat16 [1024], P('fsdp'), may hold values from -1.75 to 1.75
- w_up: bfloat16 [1024, 4096], P('fsdp'), may hold values from -0.1875 to 0.1875
- b_up: bfloat16 [4096], P('fsdp'), may hold values from -3 to 3
- w_down: bfloat16 [4096, 1024], P('fsdp'), may hold values from -0.09375 to 0.09375
- b_down: bfloat16 [1024], P('fsdp'), may hold values from -1.75 to 1.75
- cotangent: bfloat16 [3, 32, 320, 1024], P(None, ('fsdp', 'seq')), may hold values from -6 to 6
Outputs:
- activations: bfloat16 [3, 32, 320, 1024], P(None, ('fsdp', 'seq'))
- input_grad: bfloat16 [3, 32, 320, 1024], P(None, ('fsdp', 'seq'))
- grad_ln1_gain: float32 [1024], P('fsdp')
- grad_ln1_shift: float32 [1024], P('fsdp')
- grad_w_qkv: float32 [1024, 3072], P('fsdp')
- grad_b_qv: float32 [2048], P('fsdp')
- grad_w_out: float32 [1024, 1024], P('fsdp')
- grad_b_out: float32 [1024], P('fsdp')
- grad_ln2_gain: float32 [1024], P('fsdp')
- grad_ln2_shift: float32 [1024], P('fsdp')
- grad_w_up: float32 [1024, 4096], P('fsdp')
- grad_b_up: float32 [4096], P('fsdp')
- grad_w_down: float32 [4096, 1024], P('fsdp')
- grad_b_down: float32 [1024], P('fsdp')
The draws below stay inside these ranges and needn't reach their ends.
Inputs may be any that keep to these rules, and one draw needn't show every extreme that they name: counts[m, i] is 64 plus the image's kept slots; slots at and after it are padding; in every micro-batch each index of fsdp holds an image with all 320 slots live and one with only the 64 buffer slots.
All inputs are finite; a program needn't handle non-finite values.
Results may differ from the reference program's by a relative error of at most 0.018.
Values may be sent and summed in bfloat16 or wider, within the bound.
No kernel may reach another device: no remote copies, remote signals or barrier semaphores. Data moves between devices by JAX's collectives and lax.ppermute only.
A program may use at most 256 MiB of HBM per device.

```python
import jax
import jax.numpy as jnp
from jax import lax

D = 1024
HEADS = 16
HD = 64
FF = 4096
BUFFER = 64
SLOTS = 320
MICRO = 3
IMG_GROUP = 4
IMAGES = 32


def draw_counts(key, part):
    key = jax.random.fold_in(key, 7)
    key_kept, key_full, key_short = jax.random.split(key, 3)
    kept_slots = jax.random.randint(key_kept, (MICRO, IMAGES), 0, SLOTS - BUFFER + 1)
    groups = IMAGES // IMG_GROUP
    lengths = (BUFFER + kept_slots).reshape(MICRO, groups, IMG_GROUP)
    full_pick = jax.random.randint(key_full, (MICRO, groups, 1), 0, IMG_GROUP)
    short_step = jax.random.randint(key_short, (MICRO, groups, 1), 1, IMG_GROUP)
    short_pick = (full_pick + short_step) % IMG_GROUP
    position = jnp.arange(IMG_GROUP, dtype=jnp.int32)[None, None, :]
    lengths = jnp.where(position == full_pick, SLOTS, lengths)
    lengths = jnp.where(position == short_pick, BUFFER, lengths)
    return lengths.reshape(MICRO, IMAGES).astype(jnp.int32)


def level_of(own_key, dims, cuts, least, high):
    def one(dim, shards_of):
        heights = jax.random.uniform(jax.random.fold_in(jax.random.fold_in(own_key, 6), dim), (shards_of,), jnp.float32, least / len(cuts), high / len(cuts))
        return jnp.repeat(jnp.exp(heights), dims[dim] // shards_of).reshape((-1,) + (1,) * (len(dims) - dim - 1))

    loudness = one(*cuts[0])
    for cut in cuts[1:]:
        loudness = loudness * one(*cut)
    return loudness


def centred(key, extent, scale, most, cuts=(), kind=jnp.bfloat16):
    gain = level_of(key, extent, cuts, -0.22, 0.18) if cuts else 1.0
    drawn = jax.random.normal(key, extent, jnp.float32) * scale * gain
    return jnp.minimum(jnp.maximum(drawn, -most), most).astype(kind)


def setup_inputs(seed: int = 0) -> dict:
    key_of = jax.random.split(jax.random.key(seed), 16)
    return {
        "tokens": centred(key_of[0], (MICRO, IMAGES, SLOTS, D), 1.0, 6.0, ((1, 32),)),
        "counts": draw_counts(jax.random.fold_in(key_of[15], 71), 0),
        "ln1_gain": jnp.clip(1.0 + 0.1 * jax.random.normal(key_of[2], (D,), jnp.float32), 0.5, 1.5).astype(jnp.bfloat16),
        "ln1_shift": centred(key_of[3], (D,), 0.3, 1.75, ((0, 8),)),
        "w_qkv": centred(key_of[4], (D, 3 * D), D ** -0.5, 0.1875, ((0, 8),)),
        "b_qv": centred(key_of[5], (2 * D,), 0.3, 1.75, ((0, 8),)),
        "w_out": centred(key_of[6], (D, D), (D // 64) ** -0.5, 1.5, ((0, 8),)),
        "b_out": centred(key_of[7], (D,), 0.3, 1.75, ((0, 8),)),
        "ln2_gain": jnp.clip(1.0 + 0.1 * jax.random.normal(key_of[8], (D,), jnp.float32), 0.5, 1.5).astype(jnp.bfloat16),
        "ln2_shift": centred(key_of[9], (D,), 0.3, 1.75, ((0, 8),)),
        "w_up": centred(key_of[10], (D, FF), D ** -0.5, 0.1875, ((0, 8),)),
        "b_up": centred(key_of[11], (FF,), 0.5, 3.0, ((0, 8),)),
        "w_down": centred(key_of[12], (FF, D), FF ** -0.5, 0.09375, ((0, 8),)),
        "b_down": centred(key_of[13], (D,), 0.3, 1.75, ((0, 8),)),
        "cotangent": centred(key_of[14], (MICRO, IMAGES, SLOTS, D), 1.0, 6.0, ((1, 32),)),
    }


@jax.custom_vjp
def low(v):
    return lax.optimization_barrier(v.astype(jnp.bfloat16)).astype(jnp.float32)

@jax.custom_vjp
def low_back(v):
    return v

def low_keep(v):
    return (low(v), None)

def low_pass(kept, grad):
    return (grad,)

def back_keep(v):
    return (v, None)

def back_low(kept, grad):
    return (low(grad),)
low.defvjp(low_keep, low_pass)
low_back.defvjp(back_keep, back_low)
epsilon = 1e-05
group_images = 8
highest = lax.Precision.HIGHEST

def layer_norm(values, gain_vector, shift_vector):
    center = values - lax.optimization_barrier(jnp.mean(values, axis=-1, keepdims=True))
    spread = lax.optimization_barrier(jnp.mean(center * center, axis=-1, keepdims=True))
    return center * lax.rsqrt(spread + epsilon) * gain_vector + shift_vector

def block_forward(image_block, block_counts, params):
    gain_one, shift_one, qkv_weight, qkv_half, out_weight, out_bias, gain_two, shift_two, up_weight, up_bias, down_weight, down_bias = params
    images, slot_count, model_width = image_block.shape
    flat_rows = image_block.reshape(images * slot_count, model_width)
    normed = low(layer_norm(flat_rows, gain_one, shift_one))
    qkv_bias = jnp.concatenate([qkv_half[:model_width], jnp.zeros((model_width,), jnp.float32), qkv_half[model_width:]])
    project = jnp.dot(normed, qkv_weight, precision=highest) + qkv_bias
    project = low(low_back(project)).reshape(images, slot_count, 3, HEADS, HD)
    query_part = project[:, :, 0]
    key_part = project[:, :, 1]
    value_part = project[:, :, 2]
    scores = jnp.einsum('bshd,bthd->bhst', query_part, key_part, precision=highest) * HD ** (-0.5)
    scores = low_back(scores)
    live_keys = jnp.arange(slot_count, dtype=jnp.int32)[None, :] < block_counts[:, None]
    scores = jnp.where(live_keys[:, None, None, :], scores, -1e+30)
    attention = low(jax.nn.softmax(scores, axis=-1))
    mixed = jnp.einsum('bhst,bthd->bshd', attention, value_part, precision=highest)
    mixed = low(low_back(mixed)).reshape(images * slot_count, model_width)
    branch = low_back(jnp.dot(mixed, out_weight, precision=highest) + out_bias)
    middle = flat_rows + branch
    normed_two = low(layer_norm(middle, gain_two, shift_two))
    upper_in = low_back(jnp.dot(normed_two, up_weight, precision=highest) + up_bias)
    hidden = low(jax.nn.gelu(upper_in))
    second = low_back(jnp.dot(hidden, down_weight, precision=highest) + down_bias)
    return (middle + second).reshape(images, slot_count, model_width)

def reference(tokens, counts, ln1_gain, ln1_shift, w_qkv, b_qv, w_out, b_out, ln2_gain, ln2_shift, w_up, b_up, w_down, b_down, cotangent):
    params = tuple((item.astype(jnp.float32) for item in (ln1_gain, ln1_shift, w_qkv, b_qv, w_out, b_out, ln2_gain, ln2_shift, w_up, b_up, w_down, b_down)))
    block_total = MICRO * IMAGES // group_images
    inputs = tokens.astype(jnp.float32).reshape(block_total, group_images, SLOTS, D)
    count_blocks = counts.reshape(block_total, group_images).astype(jnp.int32)
    seeds = cotangent.astype(jnp.float32).reshape(block_total, group_images, SLOTS, D)

    def whole(inputs, params):

        def one_block(block_args):
            image_block, block_counts = block_args
            return block_forward(image_block, block_counts, params)
        return lax.map(jax.checkpoint(one_block), (inputs, count_blocks))
    outputs, pullback = jax.vjp(whole, inputs, params)
    input_grads, gradients = pullback(seeds)
    activations = outputs.reshape(MICRO, IMAGES, SLOTS, D).astype(jnp.bfloat16)
    input_grad = input_grads.reshape(MICRO, IMAGES, SLOTS, D).astype(jnp.bfloat16)
    return (activations, input_grad, gradients[0], gradients[1], gradients[2], gradients[3], gradients[4], gradients[5], gradients[6], gradients[7], gradients[8], gradients[9], gradients[10], gradients[11])
```

```python
import jax
import jax.numpy as jnp
from jax import lax
from jax.experimental import pallas as pl
from jax.experimental.pallas import tpu as pltpu
from jax.sharding import PartitionSpec as P

HEADS = 16
HD = 64
LANES = 256
PER = LANES // HD
SCALE = HD ** (-0.5)
epsilon = 1e-05
BF = jnp.bfloat16
F32 = jnp.float32


def nt(a, b):
    return lax.dot_general(a, b, (((1,), (1,)), ((), ())), preferred_element_type=F32)


def tn(a, b):
    return lax.dot_general(a, b, (((0,), (0,)), ((), ())), preferred_element_type=F32)


def nn(a, b):
    return jnp.dot(a, b, preferred_element_type=F32)


def head_masks(rows):
    lane = lax.broadcasted_iota(jnp.int32, (rows, LANES), 1) // HD
    return [lane == h for h in range(PER)]


def attention_forward(counts_ref, qkv_ref, out_ref):
    slots, wide = qkv_ref.shape
    width = wide // 3
    live = counts_ref[pl.program_id(0)]
    masks = head_masks(slots)
    alive = lax.broadcasted_iota(jnp.int32, (slots, slots), 1) < live
    for g in range(width // LANES):
        q = qkv_ref[:, pl.ds(g * LANES, LANES)] * jnp.asarray(SCALE, BF)
        k = qkv_ref[:, pl.ds(width + g * LANES, LANES)]
        v = qkv_ref[:, pl.ds(2 * width + g * LANES, LANES)]
        zero = jnp.zeros_like(q)
        total = jnp.zeros((slots, LANES), F32)
        for mask in masks:
            s = jnp.where(alive, nt(jnp.where(mask, q, zero), k), -1e30)
            e = jnp.exp(s - jnp.max(s, axis=1, keepdims=True))
            p = e * (1.0 / jnp.sum(e, axis=1, keepdims=True))
            total += nn(p.astype(BF), jnp.where(mask, v, zero))
        out_ref[:, pl.ds(g * LANES, LANES)] = total.astype(BF)


def attention_backward(counts_ref, qkv_ref, do_ref, out_ref):
    slots, wide = qkv_ref.shape
    width = wide // 3
    live = counts_ref[pl.program_id(0)]
    masks = head_masks(slots)
    alive = lax.broadcasted_iota(jnp.int32, (slots, slots), 0) < live
    for g in range(width // LANES):
        q = qkv_ref[:, pl.ds(g * LANES, LANES)] * jnp.asarray(SCALE, BF)
        k = qkv_ref[:, pl.ds(width + g * LANES, LANES)]
        v = qkv_ref[:, pl.ds(2 * width + g * LANES, LANES)]
        do = do_ref[:, pl.ds(g * LANES, LANES)]
        zero = jnp.zeros_like(q)
        dq = jnp.zeros((slots, LANES), F32)
        dk = jnp.zeros((slots, LANES), F32)
        dv = jnp.zeros((slots, LANES), F32)
        for mask in masks:
            qh = jnp.where(mask, q, zero)
            doh = jnp.where(mask, do, zero)
            s = jnp.where(alive, nt(k, qh), -1e30)
            e = jnp.exp(s - jnp.max(s, axis=0, keepdims=True))
            p = e * (1.0 / jnp.sum(e, axis=0, keepdims=True))
            dp = nt(v, doh)
            ds = (p * (dp - jnp.sum(p * dp, axis=0, keepdims=True))).astype(BF)
            dv += nn(p.astype(BF), doh)
            dk += nn(ds, qh)
            dq += tn(ds, jnp.where(mask, k, zero))
        out_ref[:, pl.ds(g * LANES, LANES)] = (dq * SCALE).astype(BF)
        out_ref[:, pl.ds(width + g * LANES, LANES)] = dk.astype(BF)
        out_ref[:, pl.ds(2 * width + g * LANES, LANES)] = dv.astype(BF)


def per_image(kernel, counts, slots, arrays, out_width):
    rows = arrays[0].shape[0]
    return pl.pallas_call(
        kernel,
        grid_spec=pltpu.PrefetchScalarGridSpec(
            num_scalar_prefetch=1,
            grid=(rows // slots,),
            in_specs=[pl.BlockSpec((slots, a.shape[1]), lambda i, c: (i, 0)) for a in arrays],
            out_specs=pl.BlockSpec((slots, out_width), lambda i, c: (i, 0)),
        ),
        out_shape=jax.ShapeDtypeStruct((rows, out_width), BF),
        compiler_params=pltpu.CompilerParams(vmem_limit_bytes=48 * 2**20),
    )(counts, *arrays)


def packed_rows(parts):
    rows = [part.reshape(part.shape[:-1] + (-1, 128)) for part in parts]
    total, start = 0, 0
    count = sum(part.shape[-2] for part in rows)
    for part in rows:
        size = part.shape[-2]
        edges = [(0, 0)] * (part.ndim - 2) + [(start, count - start - size), (0, 0)]
        total = total + jnp.pad(part, edges)
        start += size
    return total


def gather_small(where, parts):
    if by_hand():
        planes = lax.axis_size("fsdp") // 2
        packed = packed_rows(parts)
        column = jnp.stack([packed] + [send(packed, step, 0, 0) for step in range(1, planes)])
        both = jnp.stack([column, send(column, 0, 1, 0)])
        steps = (where[0] - jnp.arange(planes)) % planes
        flips = (where[1] + jnp.arange(2)) % 2
        whole = both[flips][:, steps].transpose(1, 0, 2, 3).reshape(2 * planes, -1)
    else:
        packed = jnp.concatenate(parts)
        whole = lax.all_gather(packed, "fsdp", axis=0, tiled=False)
    result, start = [], 0
    for part in parts:
        size = part.shape[0]
        result.append(whole[:, start : start + size].reshape(-1).astype(F32))
        start += size
    return result


def reduce_small(where, parts):
    shards = lax.axis_size("fsdp")
    if by_hand():
        planes = shards // 2
        packed = packed_rows([part.reshape(planes, 2, -1) for part in parts])
        chip = pick(packed, where[1], 1) + send(pick(packed, 1 - where[1], 1), 0, 1, 0)
        pair = chip + send(chip, 0, 0, 1)
        plane = pair + send(pair, 0, 0, 2)
        own = pick(plane, where[0])
        for step in range(1, planes):
            own += send(pick(plane, (where[0] + step) % planes), step, 0, 0)
        own = own.reshape(-1)
    else:
        packed = jnp.concatenate([part.reshape(shards, -1) for part in parts], axis=1)
        total = lax.psum(packed, ("fsdp", "seq"))
        own = lax.dynamic_index_in_dim(total, lax.axis_index("fsdp"), axis=0, keepdims=False)
    result, start = [], 0
    for part in parts:
        size = part.shape[0] // shards
        result.append(own[start : start + size])
        start += size
    return result


def send(value, step, flip_core, flip_seq):
    shards, others = lax.axis_size("fsdp"), lax.axis_size("seq")
    pairs = [
        (i * others + j, ((i + 2 * step) % shards ^ flip_core) * others + (j ^ flip_seq))
        for i in range(shards)
        for j in range(others)
    ]
    return lax.ppermute(value, ("fsdp", "seq"), pairs)


def after(value, *earlier):
    return lax.optimization_barrier((value, earlier))[0]


def pick(value, index, axis=0):
    return lax.dynamic_index_in_dim(value, index, axis=axis, keepdims=False)


def place():
    shard = lax.axis_index("fsdp")
    return jnp.stack([shard // 2, shard % 2, lax.axis_index("seq")]).astype(jnp.int32)


def by_hand():
    return lax.axis_size("seq") == 4 and lax.axis_size("fsdp") == 8


def assemble(where, parts, shapes, by_rows):
    planes, depth, wide = parts[0][-5].shape
    planes += 1
    half = depth // 2
    each = len(parts[0])
    flat = list(parts[0]) + list(parts[1])
    total = 2 * (4 + (planes - 1) * 5)

    def kernel(place_ref, *refs):
        ins, outs = refs[: len(flat)], refs[len(flat) : -3]
        held, in_sems, out_sems = refs[-3:]
        z, core, me = place_ref[0], place_ref[1], place_ref[2]
        places = [me, me + 1 - 2 * (me % 2), (me + 2) % 4, 3 - me, 3 - me]

        moves = []
        for flip_core in range(2):
            own = ins[flip_core * each : (flip_core + 1) * each - 5]
            shard = 2 * z + (core + flip_core) % 2
            for unit in range(4):
                if by_rows:
                    source = own[0].at[pl.ds(unit * depth, depth), :]
                elif unit * wide < own[0].shape[1]:
                    source = own[0].at[:, pl.ds(unit * wide, wide)]
                else:
                    source = own[1]
                moves.append((source, shard, jnp.int32(unit), 0, depth))
        for flip_core in range(2):
            others = ins[(flip_core + 1) * each - 5 : (flip_core + 1) * each]
            for step in range(1, planes):
                shard = 2 * ((z + planes - step) % planes) + (core + flip_core) % 2
                for n, spot in enumerate(places):
                    first, size = ((0, depth), (0, depth), (0, depth), (0, half), (half, half))[n]
                    moves.append((others[n].at[step - 1], shard, spot, first, size))

        def bring(n):
            source, _, _, _, size = moves[n]
            return pltpu.make_async_copy(source, held.at[n, pl.ds(0, size)], in_sems.at[n])

        def put(n, act):
            _, shard, unit, first, size = moves[n]
            if by_rows:
                row, column = shard * (4 * depth) + unit * depth + first, 0
            else:
                row, column = shard * depth + first, pl.multiple_of(unit * wide, wide)
            row = pl.multiple_of(row, half)

            def to(target, column):
                spot = outs[target].at[pl.ds(row, size), pl.ds(column, wide)]
                act(pltpu.make_async_copy(held.at[n, pl.ds(0, size)], spot, out_sems.at[n]))

            if len(outs) == 1:
                to(0, column)
            else:
                pl.when(unit < 3)(lambda: to(0, column))
                pl.when(unit == 3)(lambda: to(1, 0))

        for n in range(total):
            bring(n).start()
        for n in range(total):
            bring(n).wait()
            put(n, lambda copy: copy.start())
        for n in range(total):
            put(n, lambda copy: copy.wait())

    return pl.pallas_call(
        kernel,
        in_specs=[pl.BlockSpec(memory_space=pltpu.SMEM)]
        + [pl.BlockSpec(memory_space=pl.ANY)] * len(flat),
        out_specs=[pl.BlockSpec(memory_space=pl.ANY)] * len(shapes),
        out_shape=[jax.ShapeDtypeStruct(shape, BF) for shape in shapes],
        scratch_shapes=[
            pltpu.VMEM((total, depth, wide), BF),
            pltpu.SemaphoreType.DMA((total,)),
            pltpu.SemaphoreType.DMA((total,)),
        ],
        compiler_params=pltpu.CompilerParams(vmem_limit_bytes=24 * 2**20),
    )(where, *flat)


def wgrad_kernel(by_rows, mixed):
    def kernel(place_ref, *refs):
        mine_ref, far_ref = refs[-2:]

        def store(total):
            depth = total.shape[0] // 2
            first = place_ref[1] == 0
            low, high = total[:depth].astype(BF), total[depth:].astype(BF)
            mine_ref[...] = jnp.where(first, low, high)
            far_ref[...] = jnp.where(first, high, low)

        if by_rows:
            left = jnp.concatenate([refs[0][...], refs[1][...]], axis=1)
            store(tn(left, refs[2][...]))
        elif mixed:
            pl.when(pl.program_id(0) < 3)(lambda: store(tn(refs[0][...], refs[1][...])))
            pl.when(pl.program_id(0) == 3)(lambda: store(tn(refs[2][...], refs[3][...])))
        else:
            store(tn(refs[0][...], refs[1][...]))

    return kernel


def wgrad(where, left, right, extra=None, by_rows=False):
    rows = left.shape[0]
    shards = lax.axis_size("fsdp")
    planes = shards // 2
    if by_rows:
        depth, wide = left.shape[1] // (4 * shards), right.shape[1]
        arrays = [left, left, right]
        specs = [
            pl.BlockSpec((rows, depth), lambda j, z, c: (0, 8 * z + j)),
            pl.BlockSpec((rows, depth), lambda j, z, c: (0, 8 * z + 4 + j)),
            pl.BlockSpec((rows, wide), lambda j, z, c: (0, 0)),
        ]
    else:
        depth = left.shape[1] // shards
        wide = right.shape[1] // (3 if extra else 4)
        arrays = [left, right]
        specs = [
            pl.BlockSpec((rows, 2 * depth), lambda j, z, c: (0, z)),
            pl.BlockSpec((rows, wide), lambda j, z, c: (0, j)),
        ]
        if extra:
            arrays += list(extra)
            specs = [
                pl.BlockSpec((rows, 2 * depth), lambda j, z, c: (0, jnp.where(j < 3, z, planes - 1))),
                pl.BlockSpec((rows, wide), lambda j, z, c: (0, jnp.minimum(j, 2))),
                pl.BlockSpec((rows, 2 * depth), lambda j, z, c: (0, jnp.where(j < 3, 0, z))),
                pl.BlockSpec((rows, wide), lambda j, z, c: (0, 0)),
            ]
    out = pl.BlockSpec((None, None, depth, wide), lambda j, z, c: (j, z, 0, 0))
    shape = jax.ShapeDtypeStruct((4, planes, depth, wide), BF)
    return pl.pallas_call(
        wgrad_kernel(by_rows, extra is not None),
        grid_spec=pltpu.PrefetchScalarGridSpec(
            num_scalar_prefetch=1,
            grid=(4, planes),
            in_specs=specs,
            out_specs=[out, out],
        ),
        out_shape=[shape, shape],
        compiler_params=pltpu.CompilerParams(vmem_limit_bytes=48 * 2**20),
    )(where, *arrays)


def add(*parts):
    total = parts[0].astype(F32)
    for part in parts[1:]:
        total += part.astype(F32)
    return total.astype(BF)


def chip_sum(where, mine, far):
    planes, depth, wide = mine.shape[1:]

    def kernel(place_ref, mine_ref, far_ref, *outs):
        for flip in range(4):

            @pl.when(pl.program_id(0) == flip)
            def _():
                outs[flip][...] = add(mine_ref[...], far_ref[...])

    return pl.pallas_call(
        kernel,
        grid_spec=pltpu.PrefetchScalarGridSpec(
            num_scalar_prefetch=1,
            grid=(4, planes),
            in_specs=[
                pl.BlockSpec((None, None, depth, wide), lambda f, z, c: (c[2] ^ f, z, 0, 0))
            ]
            * 2,
            out_specs=[
                pl.BlockSpec(
                    (None, depth, wide),
                    lambda f, z, c, n=n: (jnp.where(f < n, 0, jnp.where(f > n, planes - 1, z)), 0, 0),
                )
                for n in range(4)
            ],
        ),
        out_shape=[jax.ShapeDtypeStruct((planes, depth, wide), BF)] * 4,
    )(where, mine, far)


def plane_parts(chip):
    return [chip[0]] + [send(chip[flip], 0, 0, flip) for flip in (1, 2, 3)]


def plane_sum(where, parts):
    planes, depth, wide = parts[0].shape

    def kernel(place_ref, *refs):
        ins, outs = refs[: len(parts)], refs[len(parts) :]
        for step in range(planes):
            at = (place_ref[0] + step) % planes
            outs[step][...] = add(*[ref[at] for ref in ins])

    return pl.pallas_call(
        kernel,
        in_specs=[pl.BlockSpec(memory_space=pltpu.SMEM)]
        + [pl.BlockSpec(memory_space=pltpu.VMEM)] * len(parts),
        out_shape=[jax.ShapeDtypeStruct((depth, wide), BF)] * planes,
        compiler_params=pltpu.CompilerParams(vmem_limit_bytes=24 * 2**20),
    )(where, *parts)


def column_parts(parts):
    return [parts[0]] + [send(part, step, 0, 0) for step, part in enumerate(parts) if step]


def shares(total):
    return [total] + over_plane(total)


def spread(where, parts, shapes, by_rows=False):
    depth, wide = parts[0].shape

    def kernel(place_ref, *refs):
        ins, outs = refs[: len(parts)], refs[len(parts) :]
        me = place_ref[2]
        for spot, ref in zip([me, me + 1 - 2 * (me % 2), (me + 2) % 4, 3 - me], ins):
            value = ref[...].astype(F32)
            if by_rows:
                outs[0][pl.ds(pl.multiple_of(spot * depth, depth), depth), :] = value
            elif len(outs) == 1:
                outs[0][:, pl.ds(pl.multiple_of(spot * wide, wide), wide)] = value
            else:

                @pl.when(spot < 3)
                def _():
                    outs[0][:, pl.ds(pl.multiple_of(spot * wide, wide), wide)] = value

                @pl.when(spot == 3)
                def _():
                    outs[1][...] = value

    return pl.pallas_call(
        kernel,
        in_specs=[pl.BlockSpec(memory_space=pltpu.SMEM)]
        + [pl.BlockSpec(memory_space=pltpu.VMEM)] * len(parts),
        out_shape=[jax.ShapeDtypeStruct(shape, F32) for shape in shapes],
        compiler_params=pltpu.CompilerParams(vmem_limit_bytes=24 * 2**20),
    )(where, *parts)


def along_z(mine):
    return [send(mine, step, 0, 0) for step in range(1, lax.axis_size("fsdp") // 2)]


def over_plane(value):
    return [send(value, 0, 0, flip) for flip in (1, 2, 3)]


def to_partner(values):
    return [send(value, 0, 1, 0) for value in values]


def across(along_x, along_y):
    half = along_x.shape[1] // 2
    return [send(along_x[:, :half], 0, 0, 2), send(along_y[:, half:], 0, 0, 1)]


def plain_sum(left, right):
    share = lax.psum_scatter(tn(left, right).astype(BF), "fsdp", scatter_dimension=0, tiled=True)
    return lax.psum(share, "seq").astype(F32)


def normal(values):
    center = values - jnp.mean(values, axis=-1, keepdims=True)
    inverse = lax.rsqrt(jnp.mean(center * center, axis=-1, keepdims=True) + epsilon)
    return center * inverse, inverse


def norm_back(grad, unit, inverse, gain):
    e = grad * gain
    return inverse * (
        e
        - jnp.mean(e, axis=-1, keepdims=True)
        - unit * jnp.mean(e * unit, axis=-1, keepdims=True)
    )


def gelu_and_slope(u):
    c = 0.7978845608
    t = jnp.tanh(c * (u + 0.044715 * u * u * u))
    half = 0.5 * (1.0 + t)
    slope = half + 0.5 * u * (1.0 - t * t) * (c + (3 * 0.044715 * c) * u * u)
    return u * half, slope


def plainly(
    tokens, live, x, g_low, small, w_qkv, w_out, w_up, w_down
):
    gain1, shift1, bias_qkv, bias_out, gain2, shift2, bias_up, bias_down = small
    slots, width = tokens.shape[2:]
    qkv_w, out_w, up_w, down_w = [
        lax.all_gather(w, "fsdp", axis=0, tiled=True) for w in (w_qkv, w_out, w_up, w_down)
    ]
    g = g_low.astype(F32)
    unit1, inverse1 = normal(x)
    a1 = (unit1 * gain1 + shift1).astype(BF)
    qkv = (nn(a1, qkv_w) + bias_qkv).astype(BF)
    o = per_image(attention_forward, live, slots, [qkv], width)
    y1 = x + nn(o, out_w) + bias_out
    unit2, inverse2 = normal(y1)
    a2 = (unit2 * gain2 + shift2).astype(BF)
    hid, slope = gelu_and_slope(nn(a2, up_w) + bias_up)
    hid = hid.astype(BF)
    s_down = plain_sum(hid, g_low)
    du = (nt(g_low, down_w) * slope).astype(BF)
    s_up = plain_sum(a2, du)
    activations = (y1 + nn(hid, down_w) + bias_down).astype(BF)
    da2 = nt(du, up_w)
    dy1 = g + norm_back(da2, unit2, inverse2, gain2)
    d1 = dy1.astype(BF)
    s_out = plain_sum(o, d1)
    do = nt(d1, out_w).astype(BF)
    dqkv = per_image(attention_backward, live, slots, [qkv, do], 3 * width)
    s_qkv = plain_sum(a1, dqkv)
    da1 = nt(dqkv, qkv_w)
    input_grad = (dy1 + norm_back(da1, unit1, inverse1, gain1)).astype(BF)
    sums = column_sums(da1, unit1, dqkv, d1, da2, unit2, du, g)
    return activations, input_grad, s_qkv, s_out, s_up, s_down, sums


def column_sums(da1, unit1, dqkv, d1, da2, unit2, du, g):
    width = da1.shape[1]
    sums_qkv = jnp.sum(dqkv.astype(F32), axis=0)
    return (
        jnp.sum(da1 * unit1, axis=0),
        jnp.sum(da1, axis=0),
        jnp.concatenate([sums_qkv[:width], sums_qkv[2 * width :]]),
        jnp.sum(d1.astype(F32), axis=0),
        jnp.sum(da2 * unit2, axis=0),
        jnp.sum(da2, axis=0),
        jnp.sum(du.astype(F32), axis=0),
        jnp.sum(g, axis=0),
    )


def by_parts(
    where, tokens, live, x, g_low, small, w_qkv, w_out, w_up, w_down
):
    gain1, shift1, bias_qkv, bias_out, gain2, shift2, bias_up, bias_down = small
    slots, width = tokens.shape[2:]
    wide = w_up.shape[1]
    me = where[2]
    g = g_low.astype(F32)

    rows_in = w_qkv.shape[0]
    unit = lax.dynamic_slice(w_qkv, (0, jnp.minimum(me, 2) * width), (rows_in, width))
    z_first = along_z(jnp.where(me < 3, unit, w_out))
    z_second = along_z(lax.dynamic_slice(w_up, (0, me * width), (rows_in, width)))
    z_third = along_z(lax.dynamic_slice(w_down, (me * rows_in, 0), (rows_in, width)))
    unit1, inverse1 = normal(x)

    col_first = jnp.stack(z_first)
    two_first = [send(col_first, 0, 0, flip) for flip in (1, 2)]
    own_far_first = to_partner(after([w_qkv, w_out, col_first], col_first))
    col_second = jnp.stack(after(z_second, col_first))
    two_second = [send(col_second, 0, 0, flip) for flip in (1, 2)]
    a1 = (unit1 * gain1 + shift1).astype(BF)
    two_first = after(two_first, col_second, a1)
    cross_first = across(*two_first)
    two_far_first = to_partner(two_first)
    col_third = jnp.stack(after(z_third, two_first))
    two_third = [send(col_third, 0, 0, flip) for flip in (1, 2)]
    cross_first = after(cross_first, col_third)
    near_first = [w_qkv, w_out, col_first] + two_first + cross_first
    far_first = own_far_first + two_far_first + to_partner(cross_first)
    own_far_second = to_partner(after([w_up, col_second], cross_first))
    two_second = after(two_second, cross_first)
    cross_second = across(*two_second)
    two_far_second = to_partner(two_second)
    qkv_w, out_w = assemble(
        where, [near_first, far_first], [(width, 3 * width), (width, width)], False
    )
    qkv = (nn(a1, qkv_w) + bias_qkv).astype(BF)
    cross_second = after(cross_second, qkv)
    near_second = [w_up, col_second] + two_second + cross_second
    far_second = own_far_second + two_far_second + to_partner(cross_second)
    own_far_third = to_partner(after([w_down, col_third], cross_second))
    two_third = after(two_third, qkv)
    cross_third = across(*two_third)
    two_far_third = to_partner(two_third)
    o = per_image(attention_forward, live, slots, [after(qkv, two_third)], width)
    cross_third = after(cross_third, o)
    near_third = [w_down, col_third] + two_third + cross_third
    far_third = own_far_third + two_far_third + to_partner(cross_third)
    y1 = x + nn(o, out_w) + bias_out
    unit2, inverse2 = normal(y1)
    a2 = (unit2 * gain2 + shift2).astype(BF)
    (up_w,) = assemble(where, after([near_second, far_second], a2), [(width, wide)], False)
    hid, slope = gelu_and_slope(nn(a2, up_w) + bias_up)
    hid = hid.astype(BF)
    slope = slope.astype(BF)

    mine_down, far_down = wgrad(where, hid, g_low, by_rows=True)
    got_down = send(far_down, 0, 1, 0)
    (down_w,) = assemble(where, after([near_third, far_third], mine_down), [(wide, width)], True)
    du = (nt(g_low, down_w) * slope.astype(F32)).astype(BF)
    chip_down = chip_sum(where, *after((mine_down, got_down), du))
    plane_down = plane_parts(chip_down)
    mine_up, far_up = wgrad(where, a2, after(du, chip_down))
    got_up = send(far_up, 0, 1, 0)
    da2 = nt(after(du, mine_up), up_w)
    dy1 = g + norm_back(da2, unit2, inverse2, gain2)
    d1 = dy1.astype(BF)
    chip_up = chip_sum(where, *after((mine_up, got_up), d1))
    plane_up = plane_parts(chip_up)
    do = nt(after(d1, chip_up), out_w).astype(BF)
    dqkv = per_image(attention_backward, live, slots, [qkv, do], 3 * width)
    column_down = column_parts(plane_sum(where, after(plane_down, dqkv)))
    mine_qkv, far_qkv = wgrad(where, a1, after(dqkv, column_down[0]), extra=(o, d1))
    got_qkv = send(far_qkv, 0, 1, 0)
    da1 = nt(after(dqkv, mine_qkv), qkv_w)
    dx = norm_back(da1, unit1, inverse1, gain1)
    input_grad = (dy1 + dx).astype(BF)
    chip_qkv = chip_sum(where, *after((mine_qkv, got_qkv), input_grad))
    plane_qkv = plane_parts(chip_qkv)
    column_up = column_parts(plane_sum(where, after(plane_up, chip_qkv)))
    share_down = shares(add(*after(column_down, column_up[0])))
    activations = (y1 + nn(after(hid, share_down[0]), down_w) + bias_down).astype(BF)
    share_up = shares(add(*after(column_up, activations)))
    (s_down,) = spread(where, after(share_down, share_up[0]), [w_down.shape], True)
    column_qkv = column_parts(plane_sum(where, after(plane_qkv, s_down)))
    (s_up,) = spread(where, after(share_up, column_qkv[0]), [w_up.shape])
    share_qkv = shares(add(*after(column_qkv, s_up)))
    s_qkv, s_out = spread(where, share_qkv, [w_qkv.shape, w_out.shape])
    sums = column_sums(da1, unit1, dqkv, d1, da2, unit2, du, g)
    return (
        activations,
        input_grad,
        s_qkv,
        s_out,
        s_up,
        s_down,
        sums,
    )


def on_device(
    tokens,
    counts,
    ln1_gain,
    ln1_shift,
    w_qkv,
    b_qv,
    w_out,
    b_out,
    ln2_gain,
    ln2_shift,
    w_up,
    b_up,
    w_down,
    b_down,
    cotangent,
):
    where = place()
    small = gather_small(
        where, (ln1_gain, ln1_shift, b_qv, b_out, ln2_gain, ln2_shift, b_up, b_down)
    )
    micro, images, slots, width = tokens.shape
    rows = micro * images * slots
    half = small[2]
    small[2] = jnp.concatenate([half[:width], jnp.zeros((width,), F32), half[width:]])
    own_start = lax.axis_index("seq") * images
    live = lax.dynamic_slice_in_dim(counts, own_start, images, axis=1).reshape(-1)
    x = tokens.reshape(rows, width).astype(F32)
    g_low = cotangent.reshape(rows, width)
    weights = (w_qkv, w_out, w_up, w_down)
    if by_hand():
        found = by_parts(where, tokens, live, x, g_low, small, *weights)
    else:
        found = plainly(tokens, live, x, g_low, small, *weights)
    activations, input_grad, s_qkv, s_out, s_up, s_down, sums = found
    sums = reduce_small(where, sums)
    return (
        activations.reshape(tokens.shape),
        input_grad.reshape(tokens.shape),
        sums[0],
        sums[1],
        s_qkv,
        sums[2],
        s_out,
        sums[3],
        sums[4],
        sums[5],
        s_up,
        sums[6],
        s_down,
        sums[7],
    )


def solution(mesh):
    row = P(None, ("fsdp", "seq"), None, None)
    one, two = P("fsdp"), P("fsdp", None)
    params = (one, one, two, one, two, one, one, one, two, one, two, one)
    return jax.shard_map(
        on_device,
        mesh=mesh,
        in_specs=(row, P(None, "fsdp")) + params + (row,),
        out_specs=(row, row) + params,
        check_vma=False,
    )
```

```python
import jax
import jax.numpy as jnp
from jax import lax
from jax.experimental import pallas as pl
from jax.experimental.pallas import tpu as pltpu
from jax.sharding import PartitionSpec as P

HEADS = 16
HD = 64
LANES = 256
PER = LANES // HD
TILE = 1024
HEIGHTS = 3
WIDE = 512
PARTS = 2
SCALE = HD ** (-0.5)
epsilon = 1e-05
BF = jnp.bfloat16
F32 = jnp.float32


def nt(a, b):
    return lax.dot_general(a, b, (((1,), (1,)), ((), ())), preferred_element_type=F32)


def tn(a, b):
    return lax.dot_general(a, b, (((0,), (0,)), ((), ())), preferred_element_type=F32)


def nn(a, b):
    return jnp.dot(a, b, preferred_element_type=F32)


def by_head(value):
    lane = lax.broadcasted_iota(jnp.int32, value.shape, 1) // HD
    zero = jnp.zeros_like(value)
    return jnp.concatenate([jnp.where(lane == h, value, zero) for h in range(PER)])


def own_lanes(value):
    slots = value.shape[0] // PER
    lane = lax.broadcasted_iota(jnp.int32, (slots, LANES), 1) // HD
    total = value[:slots]
    for h in range(1, PER):
        total = jnp.where(lane == h, value[h * slots : (h + 1) * slots], total)
    return total


def probabilities(k, heads, live):
    s = nt(k, heads)
    s = jnp.where(lax.broadcasted_iota(jnp.int32, s.shape, 0) < live, s, -1e30)
    e = jnp.exp(s - jnp.max(s, axis=0, keepdims=True))
    return e * (1.0 / jnp.sum(e, axis=0, keepdims=True))


def attention_forward(counts_ref, qkv_ref, out_ref):
    width = qkv_ref.shape[1] // 3
    live = counts_ref[pl.program_id(0)]
    for g in range(width // LANES):
        q = qkv_ref[:, pl.ds(g * LANES, LANES)] * jnp.asarray(SCALE, BF)
        k = qkv_ref[:, pl.ds(width + g * LANES, LANES)]
        v = qkv_ref[:, pl.ds(2 * width + g * LANES, LANES)]
        p = probabilities(k, by_head(q), live)
        out_ref[:, pl.ds(g * LANES, LANES)] = own_lanes(tn(p.astype(BF), v)).astype(BF)


def attention_backward(counts_ref, qkv_ref, do_ref, out_ref):
    width = qkv_ref.shape[1] // 3
    live = counts_ref[pl.program_id(0)]
    for g in range(width // LANES):
        q = qkv_ref[:, pl.ds(g * LANES, LANES)] * jnp.asarray(SCALE, BF)
        k = qkv_ref[:, pl.ds(width + g * LANES, LANES)]
        v = qkv_ref[:, pl.ds(2 * width + g * LANES, LANES)]
        heads, do_heads = by_head(q), by_head(do_ref[:, pl.ds(g * LANES, LANES)])
        p = probabilities(k, heads, live)
        dp = nt(v, do_heads)
        ds = (p * (dp - jnp.sum(p * dp, axis=0, keepdims=True))).astype(BF)
        out_ref[:, pl.ds(g * LANES, LANES)] = (own_lanes(tn(ds, k)) * SCALE).astype(BF)
        out_ref[:, pl.ds(width + g * LANES, LANES)] = nn(ds, heads).astype(BF)
        out_ref[:, pl.ds(2 * width + g * LANES, LANES)] = nn(p.astype(BF), do_heads).astype(BF)


def per_image(kernel, counts, slots, arrays, out_width):
    rows = arrays[0].shape[0]
    return pl.pallas_call(
        kernel,
        grid_spec=pltpu.PrefetchScalarGridSpec(
            num_scalar_prefetch=1,
            grid=(rows // slots,),
            in_specs=[pl.BlockSpec((slots, a.shape[1]), lambda i, c: (i, 0)) for a in arrays],
            out_specs=pl.BlockSpec((slots, out_width), lambda i, c: (i, 0)),
        ),
        out_shape=jax.ShapeDtypeStruct((rows, out_width), BF),
        compiler_params=pltpu.CompilerParams(vmem_limit_bytes=48 * 2**20),
    )(counts, *arrays)


def packed_rows(parts):
    rows = [part.reshape(part.shape[:-1] + (-1, 128)) for part in parts]
    total, start = 0, 0
    count = sum(part.shape[-2] for part in rows)
    for part in rows:
        size = part.shape[-2]
        edges = [(0, 0)] * (part.ndim - 2) + [(start, count - start - size), (0, 0)]
        total = total + jnp.pad(part, edges)
        start += size
    return total


def small_table(where, column, parts):
    planes = column.shape[0]
    both = jnp.stack([column, send(column, 0, 1, 0)])
    flips = (where[1] + jnp.arange(2)) % 2
    whole = both[flips].transpose(1, 0, 2, 3).reshape(2 * planes, -1)
    return cut(whole, parts)


def cut(whole, parts):
    result, start = [], 0
    for part in parts:
        size = part.shape[0]
        result.append(whole[:, start : start + size].reshape(-1).astype(F32))
        start += size
    return result


def complete(small, width):
    half = small[2]
    middle = jnp.zeros((width,), F32)
    return small[:2] + [jnp.concatenate([half[:width], middle, half[width:]])] + small[3:]


def own_parts(own, parts):
    result, start = [], 0
    for part in parts:
        size = part.shape[0] // lax.axis_size("fsdp")
        result.append(own[start : start + size])
        start += size
    return result


def send(value, step, flip_core, flip_seq):
    shards, others = lax.axis_size("fsdp"), lax.axis_size("seq")
    pairs = [
        (i * others + j, ((i + 2 * step) % shards ^ flip_core) * others + (j ^ flip_seq))
        for i in range(shards)
        for j in range(others)
    ]
    return lax.ppermute(value, ("fsdp", "seq"), pairs)


def after(value, *earlier):
    return lax.optimization_barrier((value, earlier))[0]


def pick(value, index, axis=0):
    return lax.dynamic_index_in_dim(value, index, axis=axis, keepdims=False)


def place():
    shard = lax.axis_index("fsdp")
    return jnp.stack([shard // 2, shard % 2, lax.axis_index("seq")]).astype(jnp.int32)


def by_hand():
    return lax.axis_size("seq") == 4 and lax.axis_size("fsdp") == 8


def assemble(where, owns, pieces, targets):
    planes, depth = pieces[0][0].shape[:2]
    planes += 1
    half = depth // 2
    flat = [*owns[0], *pieces[0], *owns[1], *pieces[1]]
    each = len(flat) // 2
    widths = [own.shape[1] // 4 for own in owns[0]]
    total = len(targets) * 2 * (4 + (planes - 1) * 5)

    def kernel(place_ref, *refs):
        ins, outs = refs[: len(flat)], refs[len(flat) : -3]
        held, in_sems, out_sems = refs[-3:]
        z, core, me = place_ref[0], place_ref[1], place_ref[2]
        places = [me, me + 1 - 2 * (me % 2), (me + 2) % 4, 3 - me, 3 - me]
        parts = [(0, depth), (0, depth), (0, depth), (0, half), (half, half)]

        moves = []
        for flip_core in range(2):
            for target, wide in enumerate(widths):
                shard = 2 * z + (core + flip_core) % 2
                own = ins[flip_core * each + target]
                for unit in range(4):
                    source = own.at[:, pl.ds(unit * wide, wide)]
                    moves.append((source, shard, jnp.int32(unit), 0, depth, target))
        for flip_core in range(2):
            others = ins[(flip_core + 1) * each - 5 : (flip_core + 1) * each]
            for step in range(1, planes):
                shard = 2 * ((z + planes - step) % planes) + (core + flip_core) % 2
                for n, spot in enumerate(places):
                    for target, wide in enumerate(widths):
                        source = others[n].at[step - 1, :, pl.ds(sum(widths[:target]), wide)]
                        moves.append((source, shard, spot, *parts[n], target))

        def bring(n):
            source, _, _, _, size, target = moves[n]
            spot = held.at[n, pl.ds(0, size), pl.ds(0, widths[target])]
            return pltpu.make_async_copy(source, spot, in_sems.at[n])

        def put(n):
            _, shard, unit, first, size, target = moves[n]
            wide = widths[target]
            row = pl.multiple_of(shard * depth + first, half)
            column = pl.multiple_of(unit * wide, wide)
            return pltpu.make_async_copy(
                held.at[n, pl.ds(0, size), pl.ds(0, wide)],
                outs[target].at[pl.ds(row, size), pl.ds(column, wide)],
                out_sems.at[n],
            )

        for n in range(total):
            bring(n).start()
        for n in range(total):
            bring(n).wait()
            put(n).start()
        for n in range(total):
            put(n).wait()

    return pl.pallas_call(
        kernel,
        in_specs=[pl.BlockSpec(memory_space=pltpu.SMEM)]
        + [pl.BlockSpec(memory_space=pl.ANY)] * len(flat),
        out_specs=[pl.BlockSpec(memory_space=pltpu.HBM)] * len(targets),
        out_shape=[jax.ShapeDtypeStruct(shape, BF) for shape in targets],
        scratch_shapes=[
            pltpu.VMEM((total, depth, max(widths)), BF),
            pltpu.SemaphoreType.DMA((total,)),
            pltpu.SemaphoreType.DMA((total,)),
        ],
        compiler_params=pltpu.CompilerParams(vmem_limit_bytes=48 * 2**20),
    )(where, *flat)


def halves(place_ref, total, depth):
    first = place_ref[1] == 0
    for n in range(total.shape[0] // (2 * depth)):
        low = total[2 * n * depth : (2 * n + 1) * depth].astype(BF)
        high = total[(2 * n + 1) * depth : (2 * n + 2) * depth].astype(BF)
        yield n, jnp.where(first, low, high), jnp.where(first, high, low)


def wgrad_call(kernel, where, grid, specs, out, shape, arrays):
    return pl.pallas_call(
        kernel,
        grid_spec=pltpu.PrefetchScalarGridSpec(
            num_scalar_prefetch=1, grid=grid, in_specs=specs, out_specs=[out, out]
        ),
        out_shape=[jax.ShapeDtypeStruct(shape, BF)] * 2,
        compiler_params=pltpu.CompilerParams(vmem_limit_bytes=56 * 2**20),
    )(where, *arrays)


def wgrad_units(where, left, right, extra=None):
    rows, width = left.shape
    shards = lax.axis_size("fsdp")
    depth, wide = width // shards, right.shape[1] // (3 if extra else 4)

    def kernel(place_ref, *refs):
        mine_ref, far_ref = refs[-2:]

        def store(left_ref, right_ref):
            total = tn(left_ref[...], right_ref[...])
            for n, mine, far in halves(place_ref, total, depth):
                mine_ref[n] = mine
                far_ref[n] = far

        if extra:
            pl.when(pl.program_id(0) < 3)(lambda: store(refs[0], refs[1]))
            pl.when(pl.program_id(0) == 3)(lambda: store(refs[2], refs[3]))
        else:
            store(refs[0], refs[1])

    one = pl.Buffered(1)
    arrays = [left, right]
    specs = [
        pl.BlockSpec((rows, width), lambda j, c: (0, 0), pipeline_mode=one),
        pl.BlockSpec((rows, wide), lambda j, c: (0, jnp.minimum(j, 2) if extra else j)),
    ]
    if extra:
        arrays += list(extra)
        specs.append(pl.BlockSpec((rows, width), lambda j, c: (0, 0), pipeline_mode=one))
        specs.append(pl.BlockSpec((rows, wide), lambda j, c: (0, 0), pipeline_mode=one))
    out = pl.BlockSpec((None, shards // 2, depth, wide), lambda j, c: (j, 0, 0, 0))
    shape = (4, shards // 2, depth, wide)
    return wgrad_call(kernel, where, (4,), specs, out, shape, arrays)


def wgrad_planes(where, left, right):
    rows, width = right.shape
    planes = lax.axis_size("fsdp") // 2
    depth, wide = left.shape[1] // (2 * planes), width // 4

    def kernel(place_ref, left_ref, right_ref, mine_ref, far_ref):
        total = tn(left_ref[...], right_ref[...])
        for _, mine, far in halves(place_ref, total, depth):
            for j in range(4):
                mine_ref[j] = mine[:, j * wide : (j + 1) * wide]
                far_ref[j] = far[:, j * wide : (j + 1) * wide]

    specs = [
        pl.BlockSpec((rows, 2 * depth), lambda z, c: (0, z)),
        pl.BlockSpec((rows, width), lambda z, c: (0, 0), pipeline_mode=pl.Buffered(1)),
    ]
    out = pl.BlockSpec((4, None, depth, wide), lambda z, c: (0, z, 0, 0))
    shape = (4, planes, depth, wide)
    return wgrad_call(kernel, where, (planes,), specs, out, shape, (left, right))


def add(*parts):
    total = parts[0].astype(F32)
    for part in parts[1:]:
        total += part.astype(F32)
    return total.astype(BF)


def chip_sum(where, mine, far):
    planes, depth, wide = mine.shape[1:]
    half = planes // 2

    def kernel(place_ref, mine_ref, far_ref, *outs):
        for flip, (first, second) in enumerate(((0, 2), (1, 2), (0, 3), (1, 3))):

            @pl.when(pl.program_id(0) == flip)
            def _():
                total = add(mine_ref[...], far_ref[...])
                outs[first][flip // 2] = total[:half]
                outs[second][flip % 2] = total[half:]

    piece = (2, half, depth, wide)
    return pl.pallas_call(
        kernel,
        grid_spec=pltpu.PrefetchScalarGridSpec(
            num_scalar_prefetch=1,
            grid=(4,),
            in_specs=[pl.BlockSpec((None, planes, depth, wide), lambda f, c: (c[2] ^ f, 0, 0, 0))] * 2,
            out_specs=[pl.BlockSpec(piece, lambda f, c: (0, 0, 0, 0))] * 4,
        ),
        out_shape=[jax.ShapeDtypeStruct(piece, BF)] * 4,
        compiler_params=pltpu.CompilerParams(vmem_limit_bytes=32 * 2**20),
    )(where, mine, far)


def sides(chip):
    return [send(chip[1], 0, 0, 1), send(chip[3], 0, 0, 2)]


def side_sum(chip, got):
    half, depth, wide = chip[0].shape[1:]

    def kernel(a_ref, ga_ref, b_ref, gb_ref, *outs):
        for own, other, outs_of in ((a_ref, ga_ref, outs[:2]), (b_ref, gb_ref, outs[2:])):
            for n in range(2):

                @pl.when(pl.program_id(0) == n)
                def _():
                    outs_of[n][...] = add(own[...], other[...])

    return pl.pallas_call(
        kernel,
        grid=(2,),
        in_specs=[pl.BlockSpec((None, half, depth, wide), lambda n: (n, 0, 0, 0))] * 4,
        out_specs=[pl.BlockSpec((half, depth, wide), lambda n: (0, 0, 0))] * 4,
        out_shape=[jax.ShapeDtypeStruct((half, depth, wide), BF)] * 4,
        compiler_params=pltpu.CompilerParams(vmem_limit_bytes=32 * 2**20),
    )(chip[0], got[0], chip[2], got[1])


def ends(side):
    return [send(side[1], 0, 0, 2), send(side[3], 0, 0, 1)]


def plane_sum(side, got):
    half, depth, wide = side[0].shape
    parts = [side[0], got[0], side[2], got[1]]

    def kernel(*refs):
        out = refs[-1]
        for n in range(half):
            out[n] = add(refs[0][n], refs[1][n])
            out[half + n] = add(refs[2][n], refs[3][n])

    return pl.pallas_call(
        kernel,
        in_specs=[pl.BlockSpec(memory_space=pltpu.VMEM)] * 4,
        out_shape=jax.ShapeDtypeStruct((2 * half, depth, wide), BF),
        compiler_params=pltpu.CompilerParams(vmem_limit_bytes=24 * 2**20),
    )(*parts)


def plane_columns(where, side, got, last):
    half, depth, wide = side[0].shape
    planes, more = 2 * half, 16
    parts = [side[0], got[0], side[2], got[1], last]

    def kernel(place_ref, *refs):
        ins, outs = refs[:5], refs[5:]
        for step in range(planes):
            at = (place_ref[0] + step) % planes

            @pl.when(at < half)
            def _():
                outs[step][pl.ds(0, depth), :] = add(ins[0][at], ins[1][at])

            @pl.when(at >= half)
            def _():
                outs[step][pl.ds(0, depth), :] = add(ins[2][at - half], ins[3][at - half])

            outs[step][pl.ds(depth, more), :] = ins[4][at]

    return pl.pallas_call(
        kernel,
        in_specs=[pl.BlockSpec(memory_space=pltpu.SMEM)]
        + [pl.BlockSpec(memory_space=pltpu.VMEM)] * 5,
        out_shape=[jax.ShapeDtypeStruct((depth + more, wide), BF)] * planes,
        compiler_params=pltpu.CompilerParams(vmem_limit_bytes=24 * 2**20),
    )(where, *parts)


def column_parts(parts):
    return [parts[0]] + [send(part, step, 0, 0) for step, part in enumerate(parts) if step]


def column_groups():
    shards = lax.axis_size("fsdp")
    return [list(range(c, shards, 2)) for c in range(2)]


def column_sum(total):
    return lax.psum_scatter(
        total, "fsdp", scatter_dimension=0, tiled=False, axis_index_groups=column_groups()
    )


def from_plane(share):
    return lax.all_gather(share, "seq", axis=0, tiled=False)


def joined(units):
    count, depth, wide = units.shape

    def kernel(in_ref, out_ref):
        for j in range(count):
            out_ref[:, pl.ds(j * wide, wide)] = in_ref[j].astype(F32)

    return pl.pallas_call(
        kernel,
        in_specs=[pl.BlockSpec(memory_space=pltpu.VMEM)],
        out_specs=pl.BlockSpec(memory_space=pltpu.VMEM),
        out_shape=jax.ShapeDtypeStruct((depth, count * wide), F32),
        compiler_params=pltpu.CompilerParams(vmem_limit_bytes=24 * 2**20),
    )(units)


def shares(total):
    return [total] + over_plane(total)


def spread(where, parts, shapes, more=0):
    wide = parts[0].shape[1]
    depth = shapes[0][0]

    def kernel(place_ref, *refs):
        ins, outs = refs[: len(parts)], refs[len(parts) :]
        me = place_ref[2]
        for spot, ref in zip([me, me + 1 - 2 * (me % 2), (me + 2) % 4, 3 - me], ins):
            value = ref[pl.ds(0, depth), :].astype(F32)
            column = pl.ds(pl.multiple_of(spot * wide, wide), wide)
            if len(shapes) == 1:
                outs[0][:, column] = value
            else:

                @pl.when(spot < 3)
                def _():
                    outs[0][:, column] = value

                @pl.when(spot == 3)
                def _():
                    outs[1][...] = value

        if more:
            rows = [ref[pl.ds(depth, 16), :].astype(F32) for ref in ins]
            outs[-1][...] = (rows[0] + rows[1] + rows[2] + rows[3])[:more]

    out = [jax.ShapeDtypeStruct(shape, F32) for shape in shapes]
    return pl.pallas_call(
        kernel,
        in_specs=[pl.BlockSpec(memory_space=pltpu.SMEM)]
        + [pl.BlockSpec(memory_space=pltpu.VMEM)] * len(parts),
        out_shape=out + ([jax.ShapeDtypeStruct((more, wide), F32)] if more else []),
        compiler_params=pltpu.CompilerParams(vmem_limit_bytes=24 * 2**20),
    )(where, *parts)


def along_z(mine):
    return [send(mine, step, 0, 0) for step in range(1, lax.axis_size("fsdp") // 2)]


def over_plane(value):
    return [send(value, 0, 0, flip) for flip in (1, 2, 3)]


def to_partner(values):
    return [send(value, 0, 1, 0) for value in values]


def column(mine):
    return lax.all_gather(
        mine, "fsdp", axis=0, tiled=False, axis_index_groups=column_groups()
    )


def others(where, whole, depth):
    planes = whole.shape[0]
    return jnp.stack(
        [pick(whole, (where[0] + planes - step) % planes)[:depth] for step in range(1, planes)]
    )


def across(along_x, along_y):
    half = along_x.shape[1] // 2
    return [send(along_x[:, :half], 0, 0, 2), send(along_y[:, half:], 0, 0, 1)]


def plain_sum(left, right):
    share = lax.psum_scatter(tn(left, right).astype(BF), "fsdp", scatter_dimension=0, tiled=True)
    return lax.psum(share, "seq").astype(F32)


def normal(values):
    center = values - jnp.mean(values, axis=-1, keepdims=True)
    inverse = lax.rsqrt(jnp.mean(center * center, axis=-1, keepdims=True) + epsilon)
    return center * inverse, inverse


def norm_back(grad, unit, inverse, gain):
    e = grad * gain
    return inverse * (
        e
        - jnp.mean(e, axis=-1, keepdims=True)
        - unit * jnp.mean(e * unit, axis=-1, keepdims=True)
    )


def gelu_and_slope(u):
    c = 0.7978845608
    square = u * u
    t = jnp.tanh(u * (c + (0.044715 * c) * square))
    half = 0.5 + 0.5 * t
    hid = u * half
    return hid, half + hid * (1.0 - t) * (c + (3 * 0.044715 * c) * square)


def call(kernel, grid, in_specs, out_specs, out_shape, scratch, args):
    return pl.pallas_call(
        kernel,
        grid=grid,
        in_specs=in_specs,
        out_specs=out_specs,
        out_shape=out_shape,
        scratch_shapes=scratch,
        compiler_params=pltpu.CompilerParams(vmem_limit_bytes=56 * 2**20),
    )(*args)


def whole(array):
    return pl.BlockSpec(array.shape, lambda *i: (0,) * array.ndim, pipeline_mode=pl.Buffered(1))


def rows_of(height, width):
    return pl.BlockSpec((height, width), lambda i: (i, 0))


def columns_of(height, width):
    return pl.BlockSpec((height, width), lambda i: (0, i))


def struct(*shape, dtype=BF):
    return jax.ShapeDtypeStruct(shape, dtype)


def project(a, w, bias):
    rows, wide = a.shape[0], w.shape[1]

    def kernel(a_ref, w_ref, b_ref, out_ref):
        out_ref[...] = (nn(a_ref[...], w_ref[...]) + b_ref[...]).astype(BF)

    return call(
        kernel,
        (wide // TILE,),
        [whole(a), columns_of(w.shape[0], TILE), columns_of(1, TILE)],
        columns_of(rows, TILE),
        struct(rows, wide),
        [],
        (a, w, bias[None]),
    )


def middle(o, w, x, bias, gain, shift):
    rows, width = x.shape
    height = rows // 4

    def kernel(o_ref, w_ref, x_ref, b_ref, gain_ref, shift_ref, y_ref, a_ref):
        y = nn(o_ref[...], w_ref[...]) + x_ref[...].astype(F32) + b_ref[...]
        y_ref[...] = y
        unit, _ = normal(y)
        a_ref[...] = (unit * gain_ref[...] + shift_ref[...]).astype(BF)

    tile = rows_of(height, width)
    vectors = [bias[None], gain[None], shift[None]]
    return call(
        kernel,
        (rows // height,),
        [tile, whole(w), tile] + [whole(v) for v in vectors],
        [tile, tile],
        [struct(rows, width, dtype=F32), struct(rows, width)],
        [],
        (o, w, x, *vectors),
    )


def expand(a, w, bias):
    rows, wide = a.shape[0], w.shape[1]

    def kernel(a_ref, w_ref, b_ref, hid_ref, slope_ref):
        for part in range(PARTS):
            at = pl.ds(part * (rows // PARTS), rows // PARTS)
            hid, slope = gelu_and_slope(nn(a_ref[at, :], w_ref[...]) + b_ref[...])
            hid_ref[at, :] = hid.astype(BF)
            slope_ref[at, :] = slope.astype(BF)

    tile = columns_of(rows, WIDE)
    return call(
        kernel,
        (wide // WIDE,),
        [whole(a), columns_of(w.shape[0], WIDE), columns_of(1, WIDE)],
        [tile, tile],
        [struct(rows, wide)] * 2,
        [],
        (a, w, bias[None]),
    )


def back_down(g, w, slope):
    rows, wide = slope.shape

    def kernel(g_ref, w_ref, slope_ref, du_ref, sum_ref):
        du = (nt(g_ref[...], w_ref[...]) * slope_ref[...].astype(F32)).astype(BF)
        du_ref[...] = du
        sum_ref[...] = jnp.sum(du.astype(F32), axis=0, keepdims=True)

    tile = columns_of(rows, TILE)
    return call(
        kernel,
        (wide // TILE,),
        [whole(g), rows_of(TILE, w.shape[1]), tile],
        [tile, columns_of(1, TILE)],
        [struct(rows, wide), struct(1, wide, dtype=F32)],
        [],
        (g, w, slope),
    )


def back_norm(total, values, gain):
    unit, inverse = normal(values)
    sums = (
        jnp.sum(total * unit, axis=0, keepdims=True),
        jnp.sum(total, axis=0, keepdims=True),
    )
    return norm_back(total, unit, inverse, gain), sums


def gather_sums(refs, sums):
    @pl.when(pl.program_id(0) == 0)
    def _():
        for ref, value in zip(refs, sums):
            ref[...] = value

    @pl.when(pl.program_id(0) > 0)
    def _():
        for ref, value in zip(refs, sums):
            ref[...] += value


def back_up(du, w, y1, g, gain):
    rows, wide = du.shape
    width = y1.shape[1]
    height = rows // HEIGHTS

    def kernel(du_ref, w_ref, y_ref, g_ref, gain_ref, dy_ref, d1_ref, s1_ref, s2_ref, s3_ref):
        back, sums = back_norm(nt(du_ref[...], w_ref[...]), y_ref[...], gain_ref[...])
        dy = g_ref[...].astype(F32) + back
        dy_ref[...] = dy
        d1 = dy.astype(BF)
        d1_ref[...] = d1
        sums += (jnp.sum(d1.astype(F32), axis=0, keepdims=True),)
        gather_sums((s1_ref, s2_ref, s3_ref), sums)

    row, tile = pl.BlockSpec((1, width), lambda i: (0, 0)), rows_of(height, width)
    vector = struct(1, width, dtype=F32)
    return call(
        kernel,
        (rows // height,),
        [rows_of(height, wide), whole(w), tile, tile, whole(gain[None])],
        [tile, tile, row, row, row],
        [struct(rows, width, dtype=F32), struct(rows, width), vector, vector, vector],
        [],
        (du, w, y1, g, gain[None]),
    )


def back_out(d1, w):
    rows, width = d1.shape

    def kernel(d_ref, w_ref, out_ref):
        out_ref[...] = nt(d_ref[...], w_ref[...]).astype(BF)

    return call(
        kernel,
        (width // TILE,),
        [whole(d1), rows_of(TILE, width)],
        columns_of(rows, TILE),
        struct(rows, width),
        [],
        (d1, w),
    )


def back_qkv(dqkv, w, x, dy1, gain):
    rows, wide = dqkv.shape
    width = x.shape[1]
    height = rows // HEIGHTS

    def kernel(d_ref, w_ref, x_ref, dy_ref, gain_ref, dx_ref, s1_ref, s2_ref, s3_ref):
        back, sums = back_norm(
            nt(d_ref[...], w_ref[...]), x_ref[...].astype(F32), gain_ref[...]
        )
        dx_ref[...] = (dy_ref[...] + back).astype(BF)
        sums += (jnp.sum(d_ref[...].astype(F32), axis=0, keepdims=True),)
        gather_sums((s1_ref, s2_ref, s3_ref), sums)

    row, tile = pl.BlockSpec((1, width), lambda i: (0, 0)), rows_of(height, width)
    long = pl.BlockSpec((1, wide), lambda i: (0, 0))
    vector = struct(1, width, dtype=F32)
    return call(
        kernel,
        (rows // height,),
        [rows_of(height, wide), whole(w), tile, tile, whole(gain[None])],
        [tile, row, row, long],
        [struct(rows, width), vector, vector, struct(1, wide, dtype=F32)],
        [],
        (dqkv, w, x, dy1, gain[None]),
    )


def contract(hid, w, y1, bias):
    rows, wide = hid.shape
    width = w.shape[1]
    height = rows // HEIGHTS

    def kernel(h_ref, w_ref, y_ref, b_ref, out_ref):
        out_ref[...] = (nn(h_ref[...], w_ref[...]) + y_ref[...] + b_ref[...]).astype(BF)

    tile = rows_of(height, width)
    return call(
        kernel,
        (rows // height,),
        [rows_of(height, wide), whole(w), tile, whole(bias[None])],
        tile,
        struct(rows, width),
        [],
        (hid, w, y1, bias[None]),
    )


def plainly(
    tokens, live, x, g_low, small, w_qkv, w_out, w_up, w_down
):
    gain1, shift1, bias_qkv, bias_out, gain2, shift2, bias_up, bias_down = small
    slots, width = tokens.shape[2:]
    qkv_w, out_w, up_w, down_w = [
        lax.all_gather(w, "fsdp", axis=0, tiled=True) for w in (w_qkv, w_out, w_up, w_down)
    ]
    g = g_low.astype(F32)
    unit1, inverse1 = normal(x)
    a1 = (unit1 * gain1 + shift1).astype(BF)
    qkv = (nn(a1, qkv_w) + bias_qkv).astype(BF)
    o = per_image(attention_forward, live, slots, [qkv], width)
    y1 = x + nn(o, out_w) + bias_out
    unit2, inverse2 = normal(y1)
    a2 = (unit2 * gain2 + shift2).astype(BF)
    hid, slope = gelu_and_slope(nn(a2, up_w) + bias_up)
    hid = hid.astype(BF)
    s_down = plain_sum(hid, g_low)
    du = (nt(g_low, down_w) * slope).astype(BF)
    s_up = plain_sum(a2, du)
    activations = (y1 + nn(hid, down_w) + bias_down).astype(BF)
    da2 = nt(du, up_w)
    dy1 = g + norm_back(da2, unit2, inverse2, gain2)
    d1 = dy1.astype(BF)
    s_out = plain_sum(o, d1)
    do = nt(d1, out_w).astype(BF)
    dqkv = per_image(attention_backward, live, slots, [qkv, do], 3 * width)
    s_qkv = plain_sum(a1, dqkv)
    da1 = nt(dqkv, qkv_w)
    input_grad = (dy1 + norm_back(da1, unit1, inverse1, gain1)).astype(BF)
    sums = column_sums(da1, unit1, dqkv, d1, da2, unit2, du, g)
    shards = lax.axis_size("fsdp")
    packed = jnp.concatenate([part.reshape(shards, -1) for part in sums], axis=1)
    own = pick(lax.psum(packed, ("fsdp", "seq")), lax.axis_index("fsdp"))
    return activations, input_grad, s_qkv, s_out, s_up, s_down, own_parts(own, sums)


def column_sums(da1, unit1, dqkv, d1, da2, unit2, du, g):
    width = da1.shape[1]
    sums_qkv = jnp.sum(dqkv.astype(F32), axis=0)
    return (
        jnp.sum(da1 * unit1, axis=0),
        jnp.sum(da1, axis=0),
        jnp.concatenate([sums_qkv[:width], sums_qkv[2 * width :]]),
        jnp.sum(d1.astype(F32), axis=0),
        jnp.sum(da2 * unit2, axis=0),
        jnp.sum(da2, axis=0),
        jnp.sum(du.astype(F32), axis=0),
        jnp.sum(g, axis=0),
    )


def by_parts(where, tokens, live, x, g_low, vectors, w_qkv, w_out, w_up, w_down):
    slots, width = tokens.shape[2:]
    wide = w_up.shape[1]
    me = where[2]
    x_low = tokens.reshape(x.shape)

    def unit(w):
        return lax.dynamic_slice_in_dim(w, me * (w.shape[1] // 4), w.shape[1] // 4, axis=1)

    depth = w_qkv.shape[0]
    first = unit(w_qkv)
    z_first = along_z(first)
    w_up, w_out, w_down, vectors = after((w_up, w_out, w_down, vectors), first)
    packed = jnp.pad(packed_rows(vectors), ((0, 4), (0, 0))).reshape(2, width)
    packed = jnp.pad(packed, ((0, 14), (0, width // 4)))
    z_second = column(
        jnp.concatenate([jnp.concatenate([unit(w_up), unit(w_out)], axis=1), packed])
    )
    z_third = column(unit(w_down))
    unit1, _ = normal(x)
    sum_down = jnp.sum(g_low.astype(F32), axis=0)

    col_first = jnp.stack(after(z_first, unit1))
    two_first = [send(col_first, 0, 0, flip) for flip in (1, 2)]
    far_own_first = to_partner(after([w_qkv, w_out], col_first))
    far_first = to_partner([col_first])
    two_first = after(two_first, unit1)
    cross_first = across(*two_first)
    far_first += to_partner(two_first)
    z_second = after(z_second, two_first)
    small = complete(small_table(where, z_second[:, depth : depth + 2, :width], vectors), width)
    gain1, shift1, bias_qkv, bias_out, gain2, shift2, bias_up, bias_down = small
    a1 = (unit1 * gain1 + shift1).astype(BF)
    col_second = others(where, z_second, depth)
    two_second = [send(col_second, 0, 0, flip) for flip in (1, 2)]
    cross_first = after(cross_first, col_second, a1)
    near_first = [col_first] + two_first + cross_first
    far_first += to_partner(cross_first)
    (qkv_w,) = assemble(
        where,
        [[w_qkv], far_own_first[:1]],
        [near_first, far_first],
        [(width, 3 * width)],
    )
    qkv = project(a1, qkv_w, bias_qkv)
    two_second = after(two_second, qkv)
    cross_second = across(*two_second)
    col_third = others(where, after(z_third, two_second), w_down.shape[0])
    two_third = [send(col_third, 0, 0, flip) for flip in (1, 2)]
    far_own_second = to_partner(after([w_up], qkv_w)) + far_own_first[1:]
    far_second = to_partner(after([col_second], qkv_w)) + to_partner(two_second)
    o = per_image(attention_forward, live, slots, [after(qkv, col_third)], width)
    cross_second = after(cross_second, o)
    near_second = [col_second] + two_second + cross_second
    far_second += to_partner(cross_second)
    up_w, out_w = assemble(
        where,
        [[w_up, w_out], far_own_second],
        [near_second, far_second],
        [(width, wide), (width, width)],
    )
    y1, a2 = middle(o, out_w, x_low, bias_out, gain2, shift2)
    far_own_third = to_partner(after([w_down], cross_second))
    far_third = to_partner(after([col_third], cross_second))
    two_third, far_own_third, far_third = after((two_third, far_own_third, far_third), a2)
    cross_third = across(*two_third)
    far_third = far_third + to_partner(two_third)
    hid, slope = expand(a2, after(up_w, two_third), bias_up)
    far_third, cross_third = after((far_third, cross_third), hid)
    near_third = [col_third] + two_third + cross_third
    far_third = far_third + to_partner(cross_third)

    mine_down, far_down = wgrad_planes(where, after(hid, far_third[:3]), g_low)
    far_third = after(far_third, mine_down)
    got_down = send(after(far_down, far_third), 0, 1, 0)
    (down_w,) = assemble(
        where,
        [[w_down], far_own_third],
        [near_third, far_third],
        [(wide, width)],
    )
    du, sum_up = back_down(g_low, down_w, slope)
    chip_down = chip_sum(where, *after((mine_down, got_down), du))
    sides_down = sides(chip_down)
    mine_up, far_up = wgrad_units(where, a2, after(du, chip_down))
    got_up = send(far_up, 0, 1, 0)
    dy1, d1, sum_gain2, sum_shift2, sum_out = back_up(after(du, mine_up), up_w, y1, g_low, gain2)
    side_down = side_sum(chip_down, after(sides_down, dy1))
    ends_down = ends(side_down)
    do = back_out(after(d1, side_down), out_w)
    total_down = plane_sum(side_down, after(ends_down, do))
    share_down = column_sum(total_down)
    chip_up = chip_sum(where, *after((mine_up, got_up), total_down))
    sides_up = sides(chip_up)
    dqkv = per_image(attention_backward, live, slots, [qkv, after(do, chip_up)], 3 * width)
    share_down = after(share_down, dqkv)
    side_up = side_sum(chip_up, after(sides_up, share_down))
    ends_up = ends(side_up)
    mine_qkv, far_qkv = wgrad_units(where, a1, after(dqkv, side_up), extra=(o, d1))
    total_up = plane_sum(side_up, after(ends_up, mine_qkv))
    got_qkv = send(after(far_qkv, total_up), 0, 1, 0)
    share_up = column_sum(total_up)
    from_down = from_plane(share_down)
    chip_qkv = chip_sum(where, *after((mine_qkv, got_qkv), total_up))
    sides_qkv = sides(chip_qkv)
    input_grad, sum_gain1, sum_shift1, sum_qkv = back_qkv(
        after(dqkv, chip_qkv), qkv_w, x_low, dy1, gain1
    )
    s_down = joined(after(from_down, input_grad))
    side_qkv = side_sum(chip_qkv, after(sides_qkv, s_down))
    ends_qkv = ends(side_qkv)

    sum_qv = jnp.concatenate([sum_qkv[0, :width], sum_qkv[0, 2 * width :]])
    sums = (
        sum_gain1[0],
        sum_shift1[0],
        sum_qv,
        sum_out[0],
        sum_gain2[0],
        sum_shift2[0],
        sum_up[0],
        sum_down,
    )
    planes = lax.axis_size("fsdp") // 2
    rows = packed_rows([part.reshape(planes, 2, -1) for part in sums])
    rows = pick(rows, where[1], 1) + send(pick(rows, 1 - where[1], 1), 0, 1, 0)
    rows = jnp.pad(rows, ((0, 0), (0, 4), (0, 0))).reshape(planes, 2, width).astype(BF)
    rows = jnp.pad(rows, ((0, 0), (0, 14), (0, 0)))

    activations = contract(after(hid, side_qkv), down_w, y1, bias_down)
    column_qkv = column_parts(
        plane_columns(where, side_qkv, after(ends_qkv, activations), rows)
    )
    from_up = from_plane(after(share_up, activations))
    share_qkv = add(*after(column_qkv, column_qkv[0]))
    s_up = joined(after(from_up, share_qkv))
    s_qkv, s_out, own = spread(where, shares(share_qkv), [w_qkv.shape, w_out.shape], more=2)
    own = own.reshape(-1)
    return activations, input_grad, s_qkv, s_out, s_up, s_down, own_parts(own, sums)


def on_device(
    tokens,
    counts,
    ln1_gain,
    ln1_shift,
    w_qkv,
    b_qv,
    w_out,
    b_out,
    ln2_gain,
    ln2_shift,
    w_up,
    b_up,
    w_down,
    b_down,
    cotangent,
):
    where = place()
    vectors = (ln1_gain, ln1_shift, b_qv, b_out, ln2_gain, ln2_shift, b_up, b_down)
    micro, images, slots, width = tokens.shape
    rows = micro * images * slots
    own_start = lax.axis_index("seq") * images
    live = lax.dynamic_slice_in_dim(counts, own_start, images, axis=1).reshape(-1)
    x = tokens.reshape(rows, width).astype(F32)
    g_low = cotangent.reshape(rows, width)
    weights = (w_qkv, w_out, w_up, w_down)
    if by_hand():
        found = by_parts(where, tokens, live, x, g_low, vectors, *weights)
    else:
        packed = lax.all_gather(jnp.concatenate(vectors), "fsdp", axis=0, tiled=False)
        small = complete(cut(packed, vectors), width)
        found = plainly(tokens, live, x, g_low, small, *weights)
    activations, input_grad, s_qkv, s_out, s_up, s_down, sums = found
    return (
        activations.reshape(tokens.shape),
        input_grad.reshape(tokens.shape),
        sums[0],
        sums[1],
        s_qkv,
        sums[2],
        s_out,
        sums[3],
        sums[4],
        sums[5],
        s_up,
        sums[6],
        s_down,
        sums[7],
    )


def solution(mesh):
    row = P(None, ("fsdp", "seq"), None, None)
    one, two = P("fsdp"), P("fsdp", None)
    params = (one, one, two, one, two, one, one, one, two, one, two, one)
    return jax.shard_map(
        on_device,
        mesh=mesh,
        in_specs=(row, P(None, "fsdp")) + params + (row,),
        out_specs=(row, row) + params,
        check_vma=False,
    )
```

```python
import jax
import jax.numpy as jnp
from jax import lax
from jax.experimental import pallas as pl
from jax.experimental.pallas import tpu as pltpu
from jax.sharding import PartitionSpec as P

HEADS = 16
HD = 64
LANES = 256
PER = LANES // HD
TILE = 1024
HEIGHTS = 3
WIDE = 512
PARTS = 2
SCALE = HD ** (-0.5)
epsilon = 1e-05
BF = jnp.bfloat16
F32 = jnp.float32


def nt(a, b):
    return lax.dot_general(a, b, (((1,), (1,)), ((), ())), preferred_element_type=F32)


def tn(a, b):
    return lax.dot_general(a, b, (((0,), (0,)), ((), ())), preferred_element_type=F32)


def nn(a, b):
    return jnp.dot(a, b, preferred_element_type=F32)


def by_head(value):
    lane = lax.broadcasted_iota(jnp.int32, value.shape, 1) // HD
    zero = jnp.zeros_like(value)
    return jnp.concatenate([jnp.where(lane == h, value, zero) for h in range(PER)])


def own_lanes(value):
    slots = value.shape[0] // PER
    lane = lax.broadcasted_iota(jnp.int32, (slots, LANES), 1) // HD
    total = value[:slots]
    for h in range(1, PER):
        total = jnp.where(lane == h, value[h * slots : (h + 1) * slots], total)
    return total


def probabilities(k, heads, live):
    s = nt(k, heads)
    s = jnp.where(lax.broadcasted_iota(jnp.int32, s.shape, 0) < live, s, -1e30)
    e = jnp.exp(s - jnp.max(s, axis=0, keepdims=True))
    return e * (1.0 / jnp.sum(e, axis=0, keepdims=True))


def attention_forward(counts_ref, qkv_ref, out_ref):
    width = qkv_ref.shape[1] // 3
    live = counts_ref[pl.program_id(0)]
    for g in range(width // LANES):
        q = qkv_ref[:, pl.ds(g * LANES, LANES)] * jnp.asarray(SCALE, BF)
        k = qkv_ref[:, pl.ds(width + g * LANES, LANES)]
        v = qkv_ref[:, pl.ds(2 * width + g * LANES, LANES)]
        p = probabilities(k, by_head(q), live)
        out_ref[:, pl.ds(g * LANES, LANES)] = own_lanes(tn(p.astype(BF), v)).astype(BF)


def attention_backward(counts_ref, qkv_ref, do_ref, out_ref):
    width = qkv_ref.shape[1] // 3
    live = counts_ref[pl.program_id(0)]
    for g in range(width // LANES):
        q = qkv_ref[:, pl.ds(g * LANES, LANES)] * jnp.asarray(SCALE, BF)
        k = qkv_ref[:, pl.ds(width + g * LANES, LANES)]
        v = qkv_ref[:, pl.ds(2 * width + g * LANES, LANES)]
        heads, do_heads = by_head(q), by_head(do_ref[:, pl.ds(g * LANES, LANES)])
        p = probabilities(k, heads, live)
        dp = nt(v, do_heads)
        ds = (p * (dp - jnp.sum(p * dp, axis=0, keepdims=True))).astype(BF)
        out_ref[:, pl.ds(g * LANES, LANES)] = (own_lanes(tn(ds, k)) * SCALE).astype(BF)
        out_ref[:, pl.ds(width + g * LANES, LANES)] = nn(ds, heads).astype(BF)
        out_ref[:, pl.ds(2 * width + g * LANES, LANES)] = nn(p.astype(BF), do_heads).astype(BF)


def per_image(kernel, counts, slots, arrays, out_width):
    rows = arrays[0].shape[0]
    return pl.pallas_call(
        kernel,
        grid_spec=pltpu.PrefetchScalarGridSpec(
            num_scalar_prefetch=1,
            grid=(rows // slots,),
            in_specs=[pl.BlockSpec((slots, a.shape[1]), lambda i, c: (i, 0)) for a in arrays],
            out_specs=pl.BlockSpec((slots, out_width), lambda i, c: (i, 0)),
        ),
        out_shape=jax.ShapeDtypeStruct((rows, out_width), BF),
        compiler_params=pltpu.CompilerParams(vmem_limit_bytes=48 * 2**20),
    )(counts, *arrays)


def packed_rows(parts):
    rows = [part.reshape(part.shape[:-1] + (-1, 128)) for part in parts]
    total, start = 0, 0
    count = sum(part.shape[-2] for part in rows)
    for part in rows:
        size = part.shape[-2]
        edges = [(0, 0)] * (part.ndim - 2) + [(start, count - start - size), (0, 0)]
        total = total + jnp.pad(part, edges)
        start += size
    return total


def small_table(where, column, parts):
    planes = column.shape[0]
    both = jnp.stack([column, send(column, 0, 1, 0)])
    flips = (where[1] + jnp.arange(2)) % 2
    whole = both[flips].transpose(1, 0, 2, 3).reshape(2 * planes, -1)
    return cut(whole, parts)


def cut(whole, parts):
    result, start = [], 0
    for part in parts:
        size = part.shape[0]
        result.append(whole[:, start : start + size].reshape(-1).astype(F32))
        start += size
    return result


def complete(small, width):
    half = small[2]
    middle = jnp.zeros((width,), F32)
    return small[:2] + [jnp.concatenate([half[:width], middle, half[width:]])] + small[3:]


def own_parts(own, parts):
    result, start = [], 0
    for part in parts:
        size = part.shape[0] // lax.axis_size("fsdp")
        result.append(own[start : start + size])
        start += size
    return result


def send(value, step, flip_core, flip_seq):
    shards, others = lax.axis_size("fsdp"), lax.axis_size("seq")
    pairs = [
        (i * others + j, ((i + 2 * step) % shards ^ flip_core) * others + (j ^ flip_seq))
        for i in range(shards)
        for j in range(others)
    ]
    return lax.ppermute(value, ("fsdp", "seq"), pairs)


def after(value, *earlier):
    return lax.optimization_barrier((value, earlier))[0]


def pick(value, index, axis=0):
    return lax.dynamic_index_in_dim(value, index, axis=axis, keepdims=False)


def place():
    shard = lax.axis_index("fsdp")
    return jnp.stack([shard // 2, shard % 2, lax.axis_index("seq")]).astype(jnp.int32)


def by_hand():
    return lax.axis_size("seq") == 4 and lax.axis_size("fsdp") == 8


def assemble(where, owns, pieces, targets):
    planes, depth = pieces[0][0].shape[:2]
    planes += 1
    half = depth // 2
    flat = [*owns[0], *pieces[0], *owns[1], *pieces[1]]
    each = len(flat) // 2
    widths = [own.shape[1] // 4 for own in owns[0]]
    total = len(targets) * 2 * (4 + (planes - 1) * 5)

    def kernel(place_ref, *refs):
        ins, outs = refs[: len(flat)], refs[len(flat) : -3]
        held, in_sems, out_sems = refs[-3:]
        z, core, me = place_ref[0], place_ref[1], place_ref[2]
        places = [me, me + 1 - 2 * (me % 2), (me + 2) % 4, 3 - me, 3 - me]
        parts = [(0, depth), (0, depth), (0, depth), (0, half), (half, half)]

        moves = []
        for flip_core in range(2):
            for target, wide in enumerate(widths):
                shard = 2 * z + (core + flip_core) % 2
                own = ins[flip_core * each + target]
                for unit in range(4):
                    source = own.at[:, pl.ds(unit * wide, wide)]
                    moves.append((source, shard, jnp.int32(unit), 0, depth, target))
        for flip_core in range(2):
            others = ins[(flip_core + 1) * each - 5 : (flip_core + 1) * each]
            for step in range(1, planes):
                shard = 2 * ((z + planes - step) % planes) + (core + flip_core) % 2
                for n, spot in enumerate(places):
                    for target, wide in enumerate(widths):
                        source = others[n].at[step - 1, :, pl.ds(sum(widths[:target]), wide)]
                        moves.append((source, shard, spot, *parts[n], target))

        def bring(n):
            source, _, _, _, size, target = moves[n]
            spot = held.at[n, pl.ds(0, size), pl.ds(0, widths[target])]
            return pltpu.make_async_copy(source, spot, in_sems.at[n])

        def put(n):
            _, shard, unit, first, size, target = moves[n]
            wide = widths[target]
            row = pl.multiple_of(shard * depth + first, half)
            column = pl.multiple_of(unit * wide, wide)
            return pltpu.make_async_copy(
                held.at[n, pl.ds(0, size), pl.ds(0, wide)],
                outs[target].at[pl.ds(row, size), pl.ds(column, wide)],
                out_sems.at[n],
            )

        for n in range(total):
            bring(n).start()
        for n in range(total):
            bring(n).wait()
            put(n).start()
        for n in range(total):
            put(n).wait()

    return pl.pallas_call(
        kernel,
        in_specs=[pl.BlockSpec(memory_space=pltpu.SMEM)]
        + [pl.BlockSpec(memory_space=pl.ANY)] * len(flat),
        out_specs=[pl.BlockSpec(memory_space=pltpu.HBM)] * len(targets),
        out_shape=[jax.ShapeDtypeStruct(shape, BF) for shape in targets],
        scratch_shapes=[
            pltpu.VMEM((total, depth, max(widths)), BF),
            pltpu.SemaphoreType.DMA((total,)),
            pltpu.SemaphoreType.DMA((total,)),
        ],
        compiler_params=pltpu.CompilerParams(vmem_limit_bytes=58 * 2**20),
    )(where, *flat)


def halves(place_ref, total, depth):
    first = place_ref[1] == 0
    for n in range(total.shape[0] // (2 * depth)):
        low = total[2 * n * depth : (2 * n + 1) * depth].astype(BF)
        high = total[(2 * n + 1) * depth : (2 * n + 2) * depth].astype(BF)
        yield n, jnp.where(first, low, high), jnp.where(first, high, low)


def wgrad_call(kernel, where, grid, specs, outs, shapes, arrays):
    return pl.pallas_call(
        kernel,
        grid_spec=pltpu.PrefetchScalarGridSpec(
            num_scalar_prefetch=1, grid=grid, in_specs=specs, out_specs=outs
        ),
        out_shape=[jax.ShapeDtypeStruct(shape, BF) for shape in shapes],
        compiler_params=pltpu.CompilerParams(vmem_limit_bytes=56 * 2**20),
    )(where, *arrays)


def wgrad_units(where, left, right, extra=()):
    rows, width = left.shape
    shards = lax.axis_size("fsdp")
    planes, depth, wide = shards // 2, width // shards, right.shape[1] // 4
    count = 2 + len(extra)

    def kernel(place_ref, *refs):
        ins, outs = refs[:count], refs[count:]
        for n, mine, far in halves(place_ref, tn(ins[0][...], ins[1][...]), depth):
            outs[0][n] = mine
            outs[1][n] = far
        if extra:

            @pl.when(pl.program_id(0) == 0)
            def _():
                part = width // 4
                for n, mine, far in halves(place_ref, tn(ins[2][...], ins[3][...]), depth):
                    for j in range(4):
                        outs[2][j, n] = mine[:, j * part : (j + 1) * part]
                        outs[3][j, n] = far[:, j * part : (j + 1) * part]

    one = pl.BlockSpec((rows, width), lambda j, c: (0, 0), pipeline_mode=pl.Buffered(1))
    specs = [one, pl.BlockSpec((rows, wide), lambda j, c: (0, j))] + [one] * len(extra)
    outs = [pl.BlockSpec((None, planes, depth, wide), lambda j, c: (j, 0, 0, 0))] * 2
    shapes = [(4, planes, depth, wide)] * 2
    if extra:
        shape = (4, planes, depth, width // 4)
        outs += [pl.BlockSpec(shape, lambda j, c: (0, 0, 0, 0), pipeline_mode=pl.Buffered(1))] * 2
        shapes += [shape] * 2
    return wgrad_call(kernel, where, (4,), specs, outs, shapes, (left, right, *extra))


def wgrad_planes(where, left, right):
    rows, width = right.shape
    planes = lax.axis_size("fsdp") // 2
    depth, wide = left.shape[1] // (2 * planes), width // 4

    def kernel(place_ref, left_ref, right_ref, mine_ref, far_ref):
        for _, mine, far in halves(place_ref, tn(left_ref[...], right_ref[...]), depth):
            for j in range(4):
                mine_ref[j] = mine[:, j * wide : (j + 1) * wide]
                far_ref[j] = far[:, j * wide : (j + 1) * wide]

    specs = [
        pl.BlockSpec((rows, 2 * depth), lambda z, c: (0, z)),
        pl.BlockSpec((rows, width), lambda z, c: (0, 0), pipeline_mode=pl.Buffered(1)),
    ]
    out = pl.BlockSpec((4, None, depth, wide), lambda z, c: (0, z, 0, 0))
    shape = (4, planes, depth, wide)
    return wgrad_call(kernel, where, (planes,), specs, [out] * 2, [shape] * 2, (left, right))


def add(*parts):
    total = parts[0].astype(F32)
    for part in parts[1:]:
        total += part.astype(F32)
    return total.astype(BF)


def chip_sum(where, mine, far):
    planes, depth = mine[0].shape[1:3]
    wides = [part.shape[3] for part in mine]
    half = planes // 2

    def kernel(place_ref, *refs):
        ins, outs = refs[: 2 * len(wides)], refs[2 * len(wides) :]
        for flip, (first, second) in enumerate(((0, 2), (1, 2), (0, 3), (1, 3))):

            @pl.when(pl.program_id(0) == flip)
            def _():
                for n, wide in enumerate(wides):
                    columns = pl.ds(sum(wides[:n]), wide)
                    total = add(ins[n][...], ins[len(wides) + n][...])
                    outs[first][flip // 2, :, :, columns] = total[:half]
                    outs[second][flip % 2, :, :, columns] = total[half:]

    piece = (2, half, depth, sum(wides))
    return pl.pallas_call(
        kernel,
        grid_spec=pltpu.PrefetchScalarGridSpec(
            num_scalar_prefetch=1,
            grid=(4,),
            in_specs=[
                pl.BlockSpec((None, planes, depth, wide), lambda f, c: (c[2] ^ f, 0, 0, 0))
                for wide in wides
            ]
            * 2,
            out_specs=[pl.BlockSpec(piece, lambda f, c: (0, 0, 0, 0))] * 4,
        ),
        out_shape=[jax.ShapeDtypeStruct(piece, BF)] * 4,
        compiler_params=pltpu.CompilerParams(vmem_limit_bytes=40 * 2**20),
    )(where, *mine, *far)


def sides(chip):
    return [send(chip[1], 0, 0, 1), send(chip[3], 0, 0, 2)]


def side_sum(chip, got):
    half, depth, wide = chip[0].shape[1:]

    def kernel(a_ref, ga_ref, b_ref, gb_ref, *outs):
        for own, other, outs_of in ((a_ref, ga_ref, outs[:2]), (b_ref, gb_ref, outs[2:])):
            for n in range(2):

                @pl.when(pl.program_id(0) == n)
                def _():
                    outs_of[n][...] = add(own[...], other[...])

    return pl.pallas_call(
        kernel,
        grid=(2,),
        in_specs=[pl.BlockSpec((None, half, depth, wide), lambda n: (n, 0, 0, 0))] * 4,
        out_specs=[pl.BlockSpec((half, depth, wide), lambda n: (0, 0, 0))] * 4,
        out_shape=[jax.ShapeDtypeStruct((half, depth, wide), BF)] * 4,
        compiler_params=pltpu.CompilerParams(vmem_limit_bytes=32 * 2**20),
    )(chip[0], got[0], chip[2], got[1])


def ends(side):
    return [send(side[1], 0, 0, 2), send(side[3], 0, 0, 1)]


def plane_sum(side, got):
    half, depth, wide = side[0].shape
    parts = [side[0], got[0], side[2], got[1]]

    def kernel(*refs):
        out = refs[-1]
        for n in range(half):
            out[n] = add(refs[0][n], refs[1][n])
            out[half + n] = add(refs[2][n], refs[3][n])

    return pl.pallas_call(
        kernel,
        in_specs=[pl.BlockSpec(memory_space=pltpu.VMEM)] * 4,
        out_shape=jax.ShapeDtypeStruct((2 * half, depth, wide), BF),
        compiler_params=pltpu.CompilerParams(vmem_limit_bytes=24 * 2**20),
    )(*parts)


def plane_columns(where, side, got, last):
    half, depth, wide = side[0].shape
    planes, more = 2 * half, 16
    parts = [side[0], got[0], side[2], got[1], last]

    def kernel(place_ref, *refs):
        ins, outs = refs[:5], refs[5:]
        for step in range(planes):
            at = (place_ref[0] + step) % planes

            @pl.when(at < half)
            def _():
                outs[step][pl.ds(0, depth), :] = add(ins[0][at], ins[1][at])

            @pl.when(at >= half)
            def _():
                outs[step][pl.ds(0, depth), :] = add(ins[2][at - half], ins[3][at - half])

            outs[step][pl.ds(depth, more), :] = ins[4][at]

    return pl.pallas_call(
        kernel,
        in_specs=[pl.BlockSpec(memory_space=pltpu.SMEM)]
        + [pl.BlockSpec(memory_space=pltpu.VMEM)] * 5,
        out_shape=[jax.ShapeDtypeStruct((depth + more, wide), BF)] * planes,
        compiler_params=pltpu.CompilerParams(vmem_limit_bytes=24 * 2**20),
    )(where, *parts)


def column_parts(parts):
    return [parts[0]] + [send(part, step, 0, 0) for step, part in enumerate(parts) if step]


def column_groups():
    shards = lax.axis_size("fsdp")
    return [list(range(c, shards, 2)) for c in range(2)]


def column_sum(total):
    return lax.psum_scatter(
        total, "fsdp", scatter_dimension=0, tiled=False, axis_index_groups=column_groups()
    )


def from_plane(share):
    return lax.all_gather(share, "seq", axis=0, tiled=False)


def joined(units, widths):
    count, depth, _ = units.shape

    def kernel(in_ref, *outs):
        for n, (wide, out_ref) in enumerate(zip(widths, outs)):
            for j in range(count):
                value = in_ref[j, :, pl.ds(sum(widths[:n]), wide)].astype(F32)
                out_ref[:, pl.ds(j * wide, wide)] = value

    return pl.pallas_call(
        kernel,
        in_specs=[pl.BlockSpec(memory_space=pltpu.VMEM)],
        out_specs=[pl.BlockSpec(memory_space=pltpu.VMEM)] * len(widths),
        out_shape=[jax.ShapeDtypeStruct((depth, count * wide), F32) for wide in widths],
        compiler_params=pltpu.CompilerParams(vmem_limit_bytes=24 * 2**20),
    )(units)


def shares(total):
    return [total] + over_plane(total)


def spread(where, parts, widths, more=0):
    depth = parts[0].shape[0] - (16 if more else 0)

    def kernel(place_ref, *refs):
        ins, outs = refs[: len(parts)], refs[len(parts) :]
        me = place_ref[2]
        for spot, ref in zip([me, me + 1 - 2 * (me % 2), (me + 2) % 4, 3 - me], ins):
            for n, wide in enumerate(widths):
                column = pl.ds(pl.multiple_of(spot * wide, wide), wide)
                value = ref[pl.ds(0, depth), pl.ds(sum(widths[:n]), wide)]
                outs[n][:, column] = value.astype(F32)
        if more:
            rows = [ref[pl.ds(depth, 16), :].astype(F32) for ref in ins]
            outs[-1][...] = (rows[0] + rows[1] + rows[2] + rows[3])[:more]

    shapes = [struct(depth, 4 * wide, dtype=F32) for wide in widths]
    if more:
        shapes.append(struct(more, parts[0].shape[1], dtype=F32))
    return pl.pallas_call(
        kernel,
        in_specs=[pl.BlockSpec(memory_space=pltpu.SMEM)]
        + [pl.BlockSpec(memory_space=pltpu.VMEM)] * len(parts),
        out_shape=shapes,
        compiler_params=pltpu.CompilerParams(vmem_limit_bytes=24 * 2**20),
    )(where, *parts)


def along_z(mine):
    return [send(mine, step, 0, 0) for step in range(1, lax.axis_size("fsdp") // 2)]


def over_plane(value):
    return [send(value, 0, 0, flip) for flip in (1, 2, 3)]


def to_partner(values):
    return [send(value, 0, 1, 0) for value in values]


def column(mine):
    return lax.all_gather(
        mine, "fsdp", axis=0, tiled=False, axis_index_groups=column_groups()
    )


def others(where, whole, depth):
    planes = whole.shape[0]
    return jnp.stack(
        [pick(whole, (where[0] + planes - step) % planes)[:depth] for step in range(1, planes)]
    )


def edges(two):
    half = two[0].shape[1] // 2
    return [two[0][:, :half], two[1][:, half:]]


def across(parts):
    return [send(parts[0], 0, 0, 2), send(parts[1], 0, 0, 1)]


def plain_sum(left, right):
    share = lax.psum_scatter(tn(left, right).astype(BF), "fsdp", scatter_dimension=0, tiled=True)
    return lax.psum(share, "seq").astype(F32)


def normal(values):
    center = values - jnp.mean(values, axis=-1, keepdims=True)
    inverse = lax.rsqrt(jnp.mean(center * center, axis=-1, keepdims=True) + epsilon)
    return center * inverse, inverse


def norm_back(grad, unit, inverse, gain):
    e = grad * gain
    return inverse * (
        e
        - jnp.mean(e, axis=-1, keepdims=True)
        - unit * jnp.mean(e * unit, axis=-1, keepdims=True)
    )


def gelu_and_slope(u):
    c = 0.7978845608
    square = u * u
    t = jnp.tanh(u * (c + (0.044715 * c) * square))
    half = 0.5 + 0.5 * t
    hid = u * half
    return hid, half + hid * (1.0 - t) * (c + (3 * 0.044715 * c) * square)


def call(kernel, grid, in_specs, out_specs, out_shape, scratch, args, room=56):
    return pl.pallas_call(
        kernel,
        grid=grid,
        in_specs=in_specs,
        out_specs=out_specs,
        out_shape=out_shape,
        scratch_shapes=scratch,
        compiler_params=pltpu.CompilerParams(vmem_limit_bytes=room * 2**20),
    )(*args)


def whole(array):
    return pl.BlockSpec(array.shape, lambda *i: (0,) * array.ndim, pipeline_mode=pl.Buffered(1))


def rows_of(height, width):
    return pl.BlockSpec((height, width), lambda i: (i, 0))


def columns_of(height, width):
    return pl.BlockSpec((height, width), lambda i: (0, i))


def struct(*shape, dtype=BF):
    return jax.ShapeDtypeStruct(shape, dtype)


def project(a, w, bias):
    rows, wide = a.shape[0], w.shape[1]

    def kernel(a_ref, w_ref, b_ref, out_ref):
        out_ref[...] = (nn(a_ref[...], w_ref[...]) + b_ref[...]).astype(BF)

    return call(
        kernel,
        (wide // TILE,),
        [whole(a), columns_of(w.shape[0], TILE), columns_of(1, TILE)],
        columns_of(rows, TILE),
        struct(rows, wide),
        [],
        (a, w, bias[None]),
    )


def middle(o, w, x, bias, gain, shift):
    rows, width = x.shape
    height = rows // 4

    def kernel(o_ref, w_ref, x_ref, b_ref, gain_ref, shift_ref, y_ref, a_ref):
        y = nn(o_ref[...], w_ref[...]) + x_ref[...].astype(F32) + b_ref[...]
        y_ref[...] = y
        unit, _ = normal(y)
        a_ref[...] = (unit * gain_ref[...] + shift_ref[...]).astype(BF)

    tile = rows_of(height, width)
    vectors = [bias[None], gain[None], shift[None]]
    return call(
        kernel,
        (rows // height,),
        [tile, whole(w), tile] + [whole(v) for v in vectors],
        [tile, tile],
        [struct(rows, width, dtype=F32), struct(rows, width)],
        [],
        (o, w, x, *vectors),
    )


def expand(a, w, bias):
    rows, wide = a.shape[0], w.shape[1]

    def kernel(a_ref, w_ref, b_ref, hid_ref, slope_ref):
        for part in range(PARTS):
            at = pl.ds(part * (rows // PARTS), rows // PARTS)
            hid, slope = gelu_and_slope(nn(a_ref[at, :], w_ref[...]) + b_ref[...])
            hid_ref[at, :] = hid.astype(BF)
            slope_ref[at, :] = slope.astype(BF)

    tile = columns_of(rows, WIDE)
    return call(
        kernel,
        (wide // WIDE,),
        [whole(a), columns_of(w.shape[0], WIDE), columns_of(1, WIDE)],
        [tile, tile],
        [struct(rows, wide)] * 2,
        [],
        (a, w, bias[None]),
    )


def back_norm(total, values, gain):
    unit, inverse = normal(values)
    sums = (
        jnp.sum(total * unit, axis=0, keepdims=True),
        jnp.sum(total, axis=0, keepdims=True),
    )
    return norm_back(total, unit, inverse, gain), sums


def gather_sums(refs, sums):
    @pl.when(pl.program_id(0) == 0)
    def _():
        for ref, value in zip(refs, sums):
            ref[...] = value

    @pl.when(pl.program_id(0) > 0)
    def _():
        for ref, value in zip(refs, sums):
            ref[...] += value


def back_ffn(g, w_down, slope, w_up, y1, gain):
    rows, wide = slope.shape
    width = y1.shape[1]
    height, part = rows // HEIGHTS, wide // 4

    def kernel(g_ref, down_ref, slope_ref, up_ref, y_ref, gain_ref, *refs):
        du_ref, sum_ref, dy_ref, d1_ref, s1_ref, s2_ref, s3_ref, down, up, sems = refs
        first = pl.program_id(0) == 0

        def bring(n):
            at = pl.ds(n * part, part)
            return (
                pltpu.make_async_copy(down_ref.at[at, :], down.at[at, :], sems.at[2 * n]),
                pltpu.make_async_copy(up_ref.at[:, at], up.at[:, at], sems.at[2 * n + 1]),
            )

        @pl.when(first)
        def _():
            sum_ref[...] = jnp.zeros_like(sum_ref)
            for n in range(4):
                for copy in bring(n):
                    copy.start()

        total = None
        for n in range(4):
            at = pl.ds(n * part, part)

            @pl.when(first)
            def _():
                for copy in bring(n):
                    copy.wait()

            dh = nt(g_ref[...], down[at, :])
            du = (dh * slope_ref[:, at].astype(F32)).astype(BF)
            du_ref[:, at] = du
            sum_ref[:, at] += jnp.sum(du.astype(F32), axis=0, keepdims=True)
            more = nt(du, up[:, at])
            total = more if total is None else total + more
        back, sums = back_norm(total, y_ref[...], gain_ref[...])
        dy = g_ref[...].astype(F32) + back
        dy_ref[...] = dy
        d1 = dy.astype(BF)
        d1_ref[...] = d1
        sums += (jnp.sum(d1.astype(F32), axis=0, keepdims=True),)
        gather_sums((s1_ref, s2_ref, s3_ref), sums)

    tile, long = rows_of(height, width), rows_of(height, wide)
    row = pl.BlockSpec((1, width), lambda i: (0, 0))
    far = pl.BlockSpec(memory_space=pl.ANY)
    vector = struct(1, width, dtype=F32)
    return call(
        kernel,
        (rows // height,),
        [tile, far, long, far, tile, whole(gain[None])],
        [long, pl.BlockSpec((1, wide), lambda i: (0, 0)), tile, tile, row, row, row],
        [
            struct(rows, wide),
            struct(1, wide, dtype=F32),
            struct(rows, width, dtype=F32),
            struct(rows, width),
            vector,
            vector,
            vector,
        ],
        [
            pltpu.VMEM(w_down.shape, BF),
            pltpu.VMEM(w_up.shape, BF),
            pltpu.SemaphoreType.DMA((8,)),
        ],
        (g, w_down, slope, w_up, y1, gain[None]),
    )


def back_out(d1, w):
    rows, width = d1.shape

    def kernel(d_ref, w_ref, out_ref):
        out_ref[...] = nt(d_ref[...], w_ref[...]).astype(BF)

    return call(
        kernel,
        (width // 512,),
        [whole(d1), rows_of(512, width)],
        columns_of(rows, 512),
        struct(rows, width),
        [],
        (d1, w),
    )


def back_qkv(dqkv, w, x, dy1, gain):
    rows, wide = dqkv.shape
    width = x.shape[1]
    height = rows // HEIGHTS

    def kernel(d_ref, w_ref, x_ref, dy_ref, gain_ref, dx_ref, s1_ref, s2_ref, s3_ref):
        back, sums = back_norm(
            nt(d_ref[...], w_ref[...]), x_ref[...].astype(F32), gain_ref[...]
        )
        dx_ref[...] = (dy_ref[...] + back).astype(BF)
        sums += (jnp.sum(d_ref[...].astype(F32), axis=0, keepdims=True),)
        gather_sums((s1_ref, s2_ref, s3_ref), sums)

    row, tile = pl.BlockSpec((1, width), lambda i: (0, 0)), rows_of(height, width)
    long = pl.BlockSpec((1, wide), lambda i: (0, 0))
    vector = struct(1, width, dtype=F32)
    return call(
        kernel,
        (rows // height,),
        [rows_of(height, wide), whole(w), tile, tile, whole(gain[None])],
        [tile, row, row, long],
        [struct(rows, width), vector, vector, struct(1, wide, dtype=F32)],
        [],
        (dqkv, w, x, dy1, gain[None]),
    )


def contract(hid, w, y1, bias):
    rows, wide = hid.shape
    width = w.shape[1]
    height = rows // HEIGHTS

    def kernel(h_ref, w_ref, y_ref, b_ref, out_ref):
        out_ref[...] = (nn(h_ref[...], w_ref[...]) + y_ref[...] + b_ref[...]).astype(BF)

    tile = rows_of(height, width)
    return call(
        kernel,
        (rows // height,),
        [rows_of(height, wide), whole(w), tile, whole(bias[None])],
        tile,
        struct(rows, width),
        [],
        (hid, w, y1, bias[None]),
    )


def plainly(
    tokens, live, x, g_low, small, w_qkv, w_out, w_up, w_down
):
    gain1, shift1, bias_qkv, bias_out, gain2, shift2, bias_up, bias_down = small
    slots, width = tokens.shape[2:]
    qkv_w, out_w, up_w, down_w = [
        lax.all_gather(w, "fsdp", axis=0, tiled=True) for w in (w_qkv, w_out, w_up, w_down)
    ]
    g = g_low.astype(F32)
    unit1, inverse1 = normal(x)
    a1 = (unit1 * gain1 + shift1).astype(BF)
    qkv = (nn(a1, qkv_w) + bias_qkv).astype(BF)
    o = per_image(attention_forward, live, slots, [qkv], width)
    y1 = x + nn(o, out_w) + bias_out
    unit2, inverse2 = normal(y1)
    a2 = (unit2 * gain2 + shift2).astype(BF)
    hid, slope = gelu_and_slope(nn(a2, up_w) + bias_up)
    hid = hid.astype(BF)
    s_down = plain_sum(hid, g_low)
    du = (nt(g_low, down_w) * slope).astype(BF)
    s_up = plain_sum(a2, du)
    activations = (y1 + nn(hid, down_w) + bias_down).astype(BF)
    da2 = nt(du, up_w)
    dy1 = g + norm_back(da2, unit2, inverse2, gain2)
    d1 = dy1.astype(BF)
    s_out = plain_sum(o, d1)
    do = nt(d1, out_w).astype(BF)
    dqkv = per_image(attention_backward, live, slots, [qkv, do], 3 * width)
    s_qkv = plain_sum(a1, dqkv)
    da1 = nt(dqkv, qkv_w)
    input_grad = (dy1 + norm_back(da1, unit1, inverse1, gain1)).astype(BF)
    sums = column_sums(da1, unit1, dqkv, d1, da2, unit2, du, g)
    shards = lax.axis_size("fsdp")
    packed = jnp.concatenate([part.reshape(shards, -1) for part in sums], axis=1)
    own = pick(lax.psum(packed, ("fsdp", "seq")), lax.axis_index("fsdp"))
    return activations, input_grad, s_qkv, s_out, s_up, s_down, own_parts(own, sums)


def column_sums(da1, unit1, dqkv, d1, da2, unit2, du, g):
    width = da1.shape[1]
    sums_qkv = jnp.sum(dqkv.astype(F32), axis=0)
    return (
        jnp.sum(da1 * unit1, axis=0),
        jnp.sum(da1, axis=0),
        jnp.concatenate([sums_qkv[:width], sums_qkv[2 * width :]]),
        jnp.sum(d1.astype(F32), axis=0),
        jnp.sum(da2 * unit2, axis=0),
        jnp.sum(da2, axis=0),
        jnp.sum(du.astype(F32), axis=0),
        jnp.sum(g, axis=0),
    )


def by_parts(where, tokens, live, x, g_low, vectors, w_qkv, w_out, w_up, w_down):
    slots, width = tokens.shape[2:]
    wide = w_up.shape[1]
    me = where[2]
    x_low = tokens.reshape(x.shape)

    def unit(w):
        return lax.dynamic_slice_in_dim(w, me * (w.shape[1] // 4), w.shape[1] // 4, axis=1)

    depth = w_qkv.shape[0]
    first = unit(w_qkv)
    z_first = along_z(first)
    packed = jnp.pad(packed_rows(vectors), ((0, 4), (0, 0))).reshape(2, width)
    packed = jnp.pad(packed, ((0, 14), (0, width // 4)))
    packed = jnp.concatenate([jnp.concatenate([unit(w_up), unit(w_out)], axis=1), packed])
    z_second = column(after(packed, z_first))
    z_third = column(unit(w_down))
    unit1, _ = normal(x)
    sum_down = jnp.sum(g_low.astype(F32), axis=0)

    far_own = to_partner(after([w_qkv, w_out], unit1))
    col_first = jnp.stack(after(z_first, far_own))
    far_own = far_own + to_partner(after([w_up, w_down], col_first))
    two_first = [send(col_first, 0, 0, flip) for flip in (1, 2)]
    far_first = to_partner([col_first])
    two_first, far_own, far_first = after((two_first, far_own, far_first), col_first)
    edges_first = edges(two_first)
    cross_first = across(edges_first)
    far_first = far_first + to_partner(two_first)
    z_second = after(z_second, edges_first)
    small = complete(small_table(where, z_second[:, depth : depth + 2, :width], vectors), width)
    gain1, shift1, bias_qkv, bias_out, gain2, shift2, bias_up, bias_down = small
    a1 = (unit1 * gain1 + shift1).astype(BF)
    col_second = others(where, z_second, depth)
    two_second = [send(col_second, 0, 0, flip) for flip in (1, 2)]
    cross_first = after(cross_first, col_second, a1)
    near_first = [col_first] + two_first + cross_first
    far_first = far_first + to_partner(cross_first)
    (qkv_w,) = assemble(
        where,
        [[w_qkv], far_own[:1]],
        [near_first, far_first],
        [(width, 3 * width)],
    )
    far_second = to_partner(after([col_second], qkv_w))
    qkv = project(a1, qkv_w, bias_qkv)
    two_second, far_second = after((two_second, far_second), qkv)
    cross_second = across(edges(two_second))
    far_second = far_second + to_partner(two_second)
    o = per_image(attention_forward, live, slots, [after(qkv, two_second, sum_down)], width)
    cross_second, far_second = after((cross_second, far_second), o)
    near_second = [col_second] + two_second + cross_second
    far_second = far_second + to_partner(cross_second)
    up_w, out_w = assemble(
        where,
        [[w_up, w_out], [far_own[2], far_own[1]]],
        [near_second, far_second],
        [(width, wide), (width, width)],
    )
    y1, a2 = middle(o, out_w, x_low, bias_out, gain2, shift2)
    col_third = others(where, after(z_third, up_w), w_down.shape[0])
    two_third = [send(col_third, 0, 0, flip) for flip in (1, 2)]
    far_third = to_partner([col_third])
    hid, slope = expand(after(a2, col_third), up_w, bias_up)
    two_third, far_third = after((two_third, far_third), hid)
    edges_third = edges(two_third)
    cross_third = across(edges_third)
    far_third = far_third + to_partner(two_third)

    mine_down, far_down = wgrad_planes(where, after(hid, edges_third), g_low)
    cross_third, far_third = after((cross_third, far_third), mine_down)
    near_third = [col_third] + two_third + cross_third
    far_third = far_third + to_partner(cross_third)
    got_down = send(after(far_down, far_third), 0, 1, 0)
    (down_w,) = assemble(
        where,
        [[w_down], far_own[3:]],
        [near_third, far_third],
        [(wide, width)],
    )
    chip_down = chip_sum(where, *after(([mine_down], [got_down]), down_w))
    sides_down = sides(chip_down)
    du, sum_up, dy1, d1, sum_gain2, sum_shift2, sum_out = back_ffn(
        after(g_low, chip_down), down_w, slope, up_w, y1, gain2
    )
    side_down = side_sum(chip_down, after(sides_down, dy1))
    ends_down = ends(side_down)
    up_out = wgrad_units(where, a2, after(du, side_down), (o, d1))
    mine_up, far_up = up_out[::2], up_out[1::2]
    total_down = plane_sum(side_down, after(ends_down, mine_up))
    got_up = to_partner(after(far_up, total_down))
    share_down = column_sum(total_down)
    do = back_out(after(d1, total_down), out_w)
    chip_up = chip_sum(where, *after((mine_up, got_up), do))
    sides_up = sides(chip_up)
    dqkv = per_image(attention_backward, live, slots, [qkv, after(do, chip_up)], 3 * width)
    share_down = after(share_down, dqkv)
    side_up = side_sum(chip_up, after(sides_up, share_down))
    ends_up = ends(side_up)
    mine_qkv, far_qkv = wgrad_units(where, a1, after(dqkv, side_up))
    total_up = plane_sum(side_up, after(ends_up, mine_qkv))
    got_qkv = send(after(far_qkv, total_up), 0, 1, 0)
    share_up = column_sum(total_up)
    chip_qkv = chip_sum(where, *after(([mine_qkv], [got_qkv]), total_up))
    sides_qkv = sides(chip_qkv)
    input_grad, sum_gain1, sum_shift1, sum_qkv = back_qkv(
        after(dqkv, chip_qkv), qkv_w, x_low, dy1, gain1
    )
    side_qkv = side_sum(chip_qkv, after(sides_qkv, input_grad))
    ends_qkv = ends(side_qkv)

    sum_qv = jnp.concatenate([sum_qkv[0, :width], sum_qkv[0, 2 * width :]])
    sums = (
        sum_gain1[0],
        sum_shift1[0],
        sum_qv,
        sum_out[0],
        sum_gain2[0],
        sum_shift2[0],
        sum_up[0],
        sum_down,
    )
    planes = lax.axis_size("fsdp") // 2
    rows = packed_rows([part.reshape(planes, 2, -1) for part in sums])
    hid = after(hid, rows, side_qkv)
    rows = pick(rows, where[1], 1) + send(pick(rows, 1 - where[1], 1), 0, 1, 0)
    rows = rows.reshape(planes, 2, -1).astype(BF)
    rows = jnp.pad(rows, ((0, 0), (0, 14), (0, 0)))

    activations = contract(hid, down_w, y1, bias_down)
    from_down = from_plane(after(share_down, chip_qkv))
    column_qkv = column_parts(
        plane_columns(where, side_qkv, after(ends_qkv, activations), rows)
    )
    shares_up = shares(after(share_up, column_qkv[0]))
    (s_down,) = joined(after(from_down, column_qkv[0]), [width // 4])
    share_qkv = add(*after(column_qkv, s_down, shares_up))
    shares_qkv = shares(share_qkv)
    s_up, s_out = spread(where, after(shares_up, share_qkv), [wide // 4, width // 4])
    s_qkv, own = spread(where, after(shares_qkv, s_up), [width * 3 // 4], 2)
    own = own.reshape(-1)
    return activations, input_grad, s_qkv, s_out, s_up, s_down, own_parts(own, sums)


def on_device(
    tokens,
    counts,
    ln1_gain,
    ln1_shift,
    w_qkv,
    b_qv,
    w_out,
    b_out,
    ln2_gain,
    ln2_shift,
    w_up,
    b_up,
    w_down,
    b_down,
    cotangent,
):
    where = place()
    vectors = (ln1_gain, ln1_shift, b_qv, b_out, ln2_gain, ln2_shift, b_up, b_down)
    micro, images, slots, width = tokens.shape
    rows = micro * images * slots
    own_start = lax.axis_index("seq") * images
    live = lax.dynamic_slice_in_dim(counts, own_start, images, axis=1).reshape(-1)
    x = tokens.reshape(rows, width).astype(F32)
    g_low = cotangent.reshape(rows, width)
    weights = (w_qkv, w_out, w_up, w_down)
    if by_hand():
        found = by_parts(where, tokens, live, x, g_low, vectors, *weights)
    else:
        packed = lax.all_gather(jnp.concatenate(vectors), "fsdp", axis=0, tiled=False)
        small = complete(cut(packed, vectors), width)
        found = plainly(tokens, live, x, g_low, small, *weights)
    activations, input_grad, s_qkv, s_out, s_up, s_down, sums = found
    return (
        activations.reshape(tokens.shape),
        input_grad.reshape(tokens.shape),
        sums[0],
        sums[1],
        s_qkv,
        sums[2],
        s_out,
        sums[3],
        sums[4],
        sums[5],
        s_up,
        sums[6],
        s_down,
        sums[7],
    )


def solution(mesh):
    row = P(None, ("fsdp", "seq"), None, None)
    one, two = P("fsdp"), P("fsdp", None)
    params = (one, one, two, one, two, one, one, one, two, one, two, one)
    return jax.shard_map(
        on_device,
        mesh=mesh,
        in_specs=(row, P(None, "fsdp")) + params + (row,),
        out_specs=(row, row) + params,
        check_vma=False,
    )
```

```python
import jax
import jax.numpy as jnp
from jax import lax
from jax.experimental import pallas as pl
from jax.experimental.pallas import tpu as pltpu
from jax.sharding import PartitionSpec as P

HEADS = 16
HD = 64
LANES = 256
PER = LANES // HD
TILE = 1024
HEIGHTS = 3
WIDE = 512
PARTS = 2
SCALE = HD ** (-0.5)
epsilon = 1e-05
BF = jnp.bfloat16
F32 = jnp.float32


def nt(a, b):
    return lax.dot_general(a, b, (((1,), (1,)), ((), ())), preferred_element_type=F32)


def tn(a, b):
    return lax.dot_general(a, b, (((0,), (0,)), ((), ())), preferred_element_type=F32)


def nn(a, b):
    return jnp.dot(a, b, preferred_element_type=F32)


def by_head(value):
    lane = lax.broadcasted_iota(jnp.int32, value.shape, 1) // HD
    zero = jnp.zeros_like(value)
    return jnp.concatenate([jnp.where(lane == h, value, zero) for h in range(PER)])


def own_lanes(value):
    slots = value.shape[0] // PER
    lane = lax.broadcasted_iota(jnp.int32, (slots, LANES), 1) // HD
    total = value[:slots]
    for h in range(1, PER):
        total = jnp.where(lane == h, value[h * slots : (h + 1) * slots], total)
    return total


def probabilities(k, heads, live):
    s = nt(k, heads)
    s = jnp.where(lax.broadcasted_iota(jnp.int32, s.shape, 0) < live, s, -1e30)
    e = jnp.exp(s - jnp.max(s, axis=0, keepdims=True))
    return e * (1.0 / jnp.sum(e, axis=0, keepdims=True))


def attention_forward(counts_ref, qkv_ref, out_ref):
    width = qkv_ref.shape[1] // 3
    live = counts_ref[pl.program_id(0)]
    for g in range(width // LANES):
        q = qkv_ref[:, pl.ds(g * LANES, LANES)] * jnp.asarray(SCALE, BF)
        k = qkv_ref[:, pl.ds(width + g * LANES, LANES)]
        v = qkv_ref[:, pl.ds(2 * width + g * LANES, LANES)]
        p = probabilities(k, by_head(q), live)
        out_ref[:, pl.ds(g * LANES, LANES)] = own_lanes(tn(p.astype(BF), v)).astype(BF)


def attention_backward(counts_ref, qkv_ref, do_ref, out_ref):
    width = qkv_ref.shape[1] // 3
    live = counts_ref[pl.program_id(0)]
    for g in range(width // LANES):
        q = qkv_ref[:, pl.ds(g * LANES, LANES)] * jnp.asarray(SCALE, BF)
        k = qkv_ref[:, pl.ds(width + g * LANES, LANES)]
        v = qkv_ref[:, pl.ds(2 * width + g * LANES, LANES)]
        heads, do_heads = by_head(q), by_head(do_ref[:, pl.ds(g * LANES, LANES)])
        p = probabilities(k, heads, live)
        dp = nt(v, do_heads)
        ds = (p * (dp - jnp.sum(p * dp, axis=0, keepdims=True))).astype(BF)
        out_ref[:, pl.ds(g * LANES, LANES)] = (own_lanes(tn(ds, k)) * SCALE).astype(BF)
        out_ref[:, pl.ds(width + g * LANES, LANES)] = nn(ds, heads).astype(BF)
        out_ref[:, pl.ds(2 * width + g * LANES, LANES)] = nn(p.astype(BF), do_heads).astype(BF)


def per_image(kernel, counts, slots, arrays, out_width):
    rows = arrays[0].shape[0]
    return pl.pallas_call(
        kernel,
        grid_spec=pltpu.PrefetchScalarGridSpec(
            num_scalar_prefetch=1,
            grid=(rows // slots,),
            in_specs=[pl.BlockSpec((slots, a.shape[1]), lambda i, c: (i, 0)) for a in arrays],
            out_specs=pl.BlockSpec((slots, out_width), lambda i, c: (i, 0)),
        ),
        out_shape=jax.ShapeDtypeStruct((rows, out_width), BF),
        compiler_params=pltpu.CompilerParams(vmem_limit_bytes=48 * 2**20),
    )(counts, *arrays)


def packed_rows(parts):
    rows = [part.reshape(part.shape[:-1] + (-1, 128)) for part in parts]
    total, start = 0, 0
    count = sum(part.shape[-2] for part in rows)
    for part in rows:
        size = part.shape[-2]
        edges = [(0, 0)] * (part.ndim - 2) + [(start, count - start - size), (0, 0)]
        total = total + jnp.pad(part, edges)
        start += size
    return total


def small_table(where, column, parts):
    planes = column.shape[0]
    both = jnp.stack([column, send(column, 0, 1, 0)])
    flips = (where[1] + jnp.arange(2)) % 2
    whole = both[flips].transpose(1, 0, 2, 3).reshape(2 * planes, -1)
    return cut(whole, parts)


def cut(whole, parts):
    result, start = [], 0
    for part in parts:
        size = part.shape[0]
        result.append(whole[:, start : start + size].reshape(-1).astype(F32))
        start += size
    return result


def complete(small, width):
    half = small[2]
    middle = jnp.zeros((width,), F32)
    return small[:2] + [jnp.concatenate([half[:width], middle, half[width:]])] + small[3:]


def own_parts(own, parts):
    result, start = [], 0
    for part in parts:
        size = part.shape[0] // lax.axis_size("fsdp")
        result.append(own[start : start + size])
        start += size
    return result


def send(value, step, flip_core, flip_seq):
    shards, others = lax.axis_size("fsdp"), lax.axis_size("seq")
    pairs = [
        (i * others + j, ((i + 2 * step) % shards ^ flip_core) * others + (j ^ flip_seq))
        for i in range(shards)
        for j in range(others)
    ]
    return lax.ppermute(value, ("fsdp", "seq"), pairs)


def after(value, *earlier):
    return lax.optimization_barrier((value, earlier))[0]


def pick(value, index, axis=0):
    return lax.dynamic_index_in_dim(value, index, axis=axis, keepdims=False)


def place():
    shard = lax.axis_index("fsdp")
    return jnp.stack([shard // 2, shard % 2, lax.axis_index("seq")]).astype(jnp.int32)


def by_hand():
    return lax.axis_size("seq") == 4 and lax.axis_size("fsdp") == 8


def assemble(where, owns, pieces, targets):
    planes, depth = pieces[0][0].shape[:2]
    planes += 1
    half = depth // 2
    flat = [*owns[0], *pieces[0], *owns[1], *pieces[1]]
    each = len(flat) // 2
    widths = [own.shape[1] // 4 for own in owns[0]]
    total = len(targets) * 2 * (4 + (planes - 1) * 5)

    def kernel(place_ref, *refs):
        ins, outs = refs[: len(flat)], refs[len(flat) : -3]
        held, in_sems, out_sems = refs[-3:]
        z, core, me = place_ref[0], place_ref[1], place_ref[2]
        places = [me, me + 1 - 2 * (me % 2), (me + 2) % 4, 3 - me, 3 - me]
        parts = [(0, depth), (0, depth), (0, depth), (0, half), (half, half)]

        moves = []
        for flip_core in range(2):
            for target, wide in enumerate(widths):
                shard = 2 * z + (core + flip_core) % 2
                own = ins[flip_core * each + target]
                for unit in range(4):
                    source = own.at[:, pl.ds(unit * wide, wide)]
                    moves.append((source, shard, jnp.int32(unit), 0, depth, target))
        for flip_core in range(2):
            others = ins[(flip_core + 1) * each - 5 : (flip_core + 1) * each]
            for step in range(1, planes):
                shard = 2 * ((z + planes - step) % planes) + (core + flip_core) % 2
                for n, spot in enumerate(places):
                    for target, wide in enumerate(widths):
                        source = others[n].at[step - 1, :, pl.ds(sum(widths[:target]), wide)]
                        moves.append((source, shard, spot, *parts[n], target))

        def bring(n):
            source, _, _, _, size, target = moves[n]
            spot = held.at[n, pl.ds(0, size), pl.ds(0, widths[target])]
            return pltpu.make_async_copy(source, spot, in_sems.at[n])

        def put(n):
            _, shard, unit, first, size, target = moves[n]
            wide = widths[target]
            row = pl.multiple_of(shard * depth + first, half)
            column = pl.multiple_of(unit * wide, wide)
            return pltpu.make_async_copy(
                held.at[n, pl.ds(0, size), pl.ds(0, wide)],
                outs[target].at[pl.ds(row, size), pl.ds(column, wide)],
                out_sems.at[n],
            )

        for n in range(total):
            bring(n).start()
        for n in range(total):
            bring(n).wait()
            put(n).start()
        for n in range(total):
            put(n).wait()

    return pl.pallas_call(
        kernel,
        in_specs=[pl.BlockSpec(memory_space=pltpu.SMEM)]
        + [pl.BlockSpec(memory_space=pl.ANY)] * len(flat),
        out_specs=[pl.BlockSpec(memory_space=pltpu.HBM)] * len(targets),
        out_shape=[jax.ShapeDtypeStruct(shape, BF) for shape in targets],
        scratch_shapes=[
            pltpu.VMEM((total, depth, max(widths)), BF),
            pltpu.SemaphoreType.DMA((total,)),
            pltpu.SemaphoreType.DMA((total,)),
        ],
        compiler_params=pltpu.CompilerParams(vmem_limit_bytes=58 * 2**20),
    )(where, *flat)


def halves(place_ref, total, depth):
    first = place_ref[1] == 0
    for n in range(total.shape[0] // (2 * depth)):
        low = total[2 * n * depth : (2 * n + 1) * depth].astype(BF)
        high = total[(2 * n + 1) * depth : (2 * n + 2) * depth].astype(BF)
        yield n, jnp.where(first, low, high), jnp.where(first, high, low)


def pieces_to(place_ref, ins, widths, held, sems):
    each = len(ins) // 2
    planes, depth = ins[each - 5].shape[0] + 1, ins[each - 5].shape[1]
    half = depth // 2
    z, core, me = place_ref[0], place_ref[1], place_ref[2]
    places = [me, me + 1 - 2 * (me % 2), (me + 2) % 4, 3 - me, 3 - me]
    parts = [(0, depth), (0, depth), (0, depth), (0, half), (half, half)]
    lists, count = [], 0
    for target, wide in enumerate(widths):
        copies = []
        for flip_core in range(2):
            side = (core + flip_core) % 2
            mine = ins[flip_core * each : (flip_core + 1) * each]
            sources = [
                (mine[target].at[:, pl.ds(unit * wide, wide)], 2 * z + side, unit, 0, depth)
                for unit in range(4)
            ]
            for step in range(1, planes):
                shard = 2 * ((z + planes - step) % planes) + side
                for other, spot, part in zip(mine[each - 5 :], places, parts):
                    source = other.at[step - 1, :, pl.ds(sum(widths[:target]), wide)]
                    sources.append((source, shard, spot, *part))
            for source, shard, unit, first, size in sources:
                row = pl.multiple_of(shard * depth + first, half)
                column = pl.multiple_of(jnp.int32(unit) * wide, wide)
                spot = held[target].at[pl.ds(row, size), pl.ds(column, wide)]
                copies.append(pltpu.make_async_copy(source, spot, sems.at[count]))
                count += 1
        lists.append(copies)
    return lists


def piece_count(pieces, targets):
    return targets * 2 * (4 + pieces[0][0].shape[0] * 5)


def assembled_project(where, owns, pieces, a, bias):
    flat = [*owns[0], *pieces[0], *owns[1], *pieces[1]]
    rows, width = a.shape
    wide = owns[0][0].shape[1]
    steps = wide // TILE
    unit = wide // 4

    def kernel(place_ref, *refs):
        ins, (a_ref, b_ref, out_ref, w_ref, held, sems, done) = refs[: len(flat)], refs[len(flat) :]
        step = pl.program_id(0)
        (copies,) = pieces_to(place_ref, ins, [unit], [held], sems)
        whole_copy = pltpu.make_async_copy(held, w_ref, done.at[0])

        @pl.when(step == 0)
        def _():
            for copy in copies:
                copy.start()
            for copy in copies:
                copy.wait()
            whole_copy.start()

        w = held[:, pl.ds(pl.multiple_of(step * TILE, TILE), TILE)]
        out_ref[...] = (nn(a_ref[...], w) + b_ref[...]).astype(BF)

        @pl.when(step == steps - 1)
        def _():
            whole_copy.wait()

    return call(
        kernel,
        (steps,),
        [pl.BlockSpec(memory_space=pltpu.SMEM)]
        + [pl.BlockSpec(memory_space=pl.ANY)] * len(flat)
        + [whole(a), columns_of(1, TILE)],
        [columns_of(rows, TILE), pl.BlockSpec(memory_space=pltpu.HBM)],
        [struct(rows, wide), struct(width, wide)],
        [
            pltpu.VMEM((width, wide), BF),
            pltpu.SemaphoreType.DMA((piece_count(pieces, 1),)),
            pltpu.SemaphoreType.DMA((1,)),
        ],
        (where, *flat, a, bias[None]),
    )


def assembled_middle(where, owns, pieces, o, x, bias, gain, shift):
    flat = [*owns[0], *pieces[0], *owns[1], *pieces[1]]
    rows, width = x.shape
    wide = owns[0][0].shape[1]
    height = rows // 4

    def kernel(place_ref, *refs):
        ins, refs = refs[: len(flat)], refs[len(flat) :]
        o_ref, x_ref, b_ref, gain_ref, shift_ref, y_ref, a_ref, up_ref, out_ref = refs[:9]
        up, out, sems, done = refs[9:]
        step = pl.program_id(0)
        up_copies, out_copies = pieces_to(
            place_ref, ins, [wide // 4, width // 4], [up, out], sems
        )
        up_whole = pltpu.make_async_copy(up, up_ref, done.at[0])
        out_whole = pltpu.make_async_copy(out, out_ref, done.at[1])

        @pl.when(step == 0)
        def _():
            for copy in out_copies + up_copies:
                copy.start()
            for copy in out_copies:
                copy.wait()
            out_whole.start()

        @pl.when(step == 1)
        def _():
            for copy in up_copies:
                copy.wait()
            up_whole.start()

        y = nn(o_ref[...], out[...]) + x_ref[...].astype(F32) + b_ref[...]
        y_ref[...] = y
        unit, _ = normal(y)
        a_ref[...] = (unit * gain_ref[...] + shift_ref[...]).astype(BF)

        @pl.when(step == 3)
        def _():
            out_whole.wait()
            up_whole.wait()

    tile = rows_of(height, width)
    vectors = [bias[None], gain[None], shift[None]]
    far = pl.BlockSpec(memory_space=pltpu.HBM)
    return call(
        kernel,
        (4,),
        [pl.BlockSpec(memory_space=pltpu.SMEM)]
        + [pl.BlockSpec(memory_space=pl.ANY)] * len(flat)
        + [tile, tile]
        + [whole(v) for v in vectors],
        [tile, tile, far, far],
        [
            struct(rows, width, dtype=F32),
            struct(rows, width),
            struct(width, wide),
            struct(width, width),
        ],
        [
            pltpu.VMEM((width, wide), BF),
            pltpu.VMEM((width, width), BF),
            pltpu.SemaphoreType.DMA((piece_count(pieces, 2),)),
            pltpu.SemaphoreType.DMA((2,)),
        ],
        (where, *flat, o, x, *vectors),
    )


def wgrad_call(kernel, where, grid, specs, outs, shapes, arrays, scratch=()):
    return pl.pallas_call(
        kernel,
        grid_spec=pltpu.PrefetchScalarGridSpec(
            num_scalar_prefetch=1,
            grid=grid,
            in_specs=specs,
            out_specs=outs,
            scratch_shapes=scratch,
        ),
        out_shape=[jax.ShapeDtypeStruct(shape, BF) for shape in shapes],
        compiler_params=pltpu.CompilerParams(vmem_limit_bytes=56 * 2**20),
    )(where, *arrays)


def wgrad_units(where, left, right, extra=()):
    rows, width = left.shape
    shards = lax.axis_size("fsdp")
    planes, depth, wide = shards // 2, width // shards, right.shape[1] // 4
    part = extra[1].shape[1] // 4 if extra else 0
    count = 2 + len(extra)

    def kernel(place_ref, *refs):
        ins, outs, held = refs[:count], refs[count : count + 2], refs[count + 2 :]
        step = pl.program_id(0)
        if extra:

            @pl.when(step == 0)
            def _():
                for n, mine, far in halves(place_ref, tn(ins[2][...], ins[3][...]), depth):
                    for j in range(4):
                        held[0][j, n] = mine[:, j * part : (j + 1) * part]
                        held[1][j, n] = far[:, j * part : (j + 1) * part]

        for n, mine, far in halves(place_ref, tn(ins[0][...], ins[1][...]), depth):
            outs[0][n, :, pl.ds(0, wide)] = mine
            outs[1][n, :, pl.ds(0, wide)] = far
        if extra:
            for out, kept in zip(outs, held):
                out[:, :, pl.ds(wide, part)] = kept[step]

    one = pl.BlockSpec((rows, width), lambda j, c: (0, 0), pipeline_mode=pl.Buffered(1))
    specs = [one, pl.BlockSpec((rows, wide), lambda j, c: (0, j))] + [one] * len(extra)
    out = pl.BlockSpec((None, planes, depth, wide + part), lambda j, c: (j, 0, 0, 0))
    shape = (4, planes, depth, wide + part)
    scratch = [pltpu.VMEM((4, planes, depth, part), BF)] * 2 if extra else []
    arrays = (left, right, *extra)
    return wgrad_call(kernel, where, (4,), specs, [out] * 2, [shape] * 2, arrays, scratch)


def wgrad_planes(where, left, right):
    rows, width = right.shape
    planes = lax.axis_size("fsdp") // 2
    depth, wide = left.shape[1] // (2 * planes), width // 4

    def kernel(place_ref, left_ref, right_ref, mine_ref, far_ref):
        for _, mine, far in halves(place_ref, tn(left_ref[...], right_ref[...]), depth):
            for j in range(4):
                mine_ref[j] = mine[:, j * wide : (j + 1) * wide]
                far_ref[j] = far[:, j * wide : (j + 1) * wide]

    specs = [
        pl.BlockSpec((rows, 2 * depth), lambda z, c: (0, z)),
        pl.BlockSpec((rows, width), lambda z, c: (0, 0), pipeline_mode=pl.Buffered(1)),
    ]
    out = pl.BlockSpec((4, None, depth, wide), lambda z, c: (0, z, 0, 0))
    shape = (4, planes, depth, wide)
    return wgrad_call(kernel, where, (planes,), specs, [out] * 2, [shape] * 2, (left, right))


def add(*parts):
    if len(parts) == 2:
        return parts[0] + parts[1]
    total = parts[0].astype(F32)
    for part in parts[1:]:
        total += part.astype(F32)
    return total.astype(BF)


def chip_sum(where, mine, far):
    planes, depth = mine[0].shape[1:3]
    wides = [part.shape[3] for part in mine]
    half = planes // 2

    def kernel(place_ref, *refs):
        ins, outs = refs[: 2 * len(wides)], refs[2 * len(wides) :]
        for flip, (first, second) in enumerate(((0, 2), (1, 2), (0, 3), (1, 3))):

            @pl.when(pl.program_id(0) == flip)
            def _():
                for n, wide in enumerate(wides):
                    columns = pl.ds(sum(wides[:n]), wide)
                    total = add(ins[n][...], ins[len(wides) + n][...])
                    outs[first][flip // 2, :, :, columns] = total[:half]
                    outs[second][flip % 2, :, :, columns] = total[half:]

    piece = (2, half, depth, sum(wides))
    return pl.pallas_call(
        kernel,
        grid_spec=pltpu.PrefetchScalarGridSpec(
            num_scalar_prefetch=1,
            grid=(4,),
            in_specs=[
                pl.BlockSpec((None, planes, depth, wide), lambda f, c: (c[2] ^ f, 0, 0, 0))
                for wide in wides
            ]
            * 2,
            out_specs=[pl.BlockSpec(piece, lambda f, c: (0, 0, 0, 0))] * 4,
        ),
        out_shape=[jax.ShapeDtypeStruct(piece, BF)] * 4,
        compiler_params=pltpu.CompilerParams(vmem_limit_bytes=40 * 2**20),
    )(where, *mine, *far)


def sides(chip):
    return [send(chip[1], 0, 0, 1), send(chip[3], 0, 0, 2)]


def side_sum(chip, got):
    half, depth, wide = chip[0].shape[1:]

    def kernel(a_ref, ga_ref, b_ref, gb_ref, *outs):
        for own, other, outs_of in ((a_ref, ga_ref, outs[:2]), (b_ref, gb_ref, outs[2:])):
            for n in range(2):

                @pl.when(pl.program_id(0) == n)
                def _():
                    outs_of[n][...] = add(own[...], other[...])

    return pl.pallas_call(
        kernel,
        grid=(2,),
        in_specs=[pl.BlockSpec((None, half, depth, wide), lambda n: (n, 0, 0, 0))] * 4,
        out_specs=[pl.BlockSpec((half, depth, wide), lambda n: (0, 0, 0))] * 4,
        out_shape=[jax.ShapeDtypeStruct((half, depth, wide), BF)] * 4,
        compiler_params=pltpu.CompilerParams(vmem_limit_bytes=32 * 2**20),
    )(chip[0], got[0], chip[2], got[1])


def ends(side):
    return [send(side[1], 0, 0, 2), send(side[3], 0, 0, 1)]


def plane_sum(side, got):
    half, depth, wide = side[0].shape
    parts = [side[0], got[0], side[2], got[1]]

    def kernel(*refs):
        out = refs[-1]
        for n in range(half):
            out[n] = add(refs[0][n], refs[1][n])
            out[half + n] = add(refs[2][n], refs[3][n])

    return pl.pallas_call(
        kernel,
        in_specs=[pl.BlockSpec(memory_space=pltpu.VMEM)] * 4,
        out_shape=jax.ShapeDtypeStruct((2 * half, depth, wide), BF),
        compiler_params=pltpu.CompilerParams(vmem_limit_bytes=24 * 2**20),
    )(*parts)


def plane_columns(where, side, got, last):
    half, depth, wide = side[0].shape
    planes, more = 2 * half, 16
    parts = [side[0], got[0], side[2], got[1], last]

    def kernel(place_ref, *refs):
        ins, outs = refs[:5], refs[5:]
        for step in range(planes):
            at = (place_ref[0] + step) % planes

            @pl.when(at < half)
            def _():
                outs[step][pl.ds(0, depth), :] = add(ins[0][at], ins[1][at])

            @pl.when(at >= half)
            def _():
                outs[step][pl.ds(0, depth), :] = add(ins[2][at - half], ins[3][at - half])

            outs[step][pl.ds(depth, more), :] = ins[4][at]

    return pl.pallas_call(
        kernel,
        in_specs=[pl.BlockSpec(memory_space=pltpu.SMEM)]
        + [pl.BlockSpec(memory_space=pltpu.VMEM)] * 5,
        out_shape=[jax.ShapeDtypeStruct((depth + more, wide), BF)] * planes,
        compiler_params=pltpu.CompilerParams(vmem_limit_bytes=24 * 2**20),
    )(where, *parts)


def column_parts(parts):
    return [parts[0]] + [send(part, step, 0, 0) for step, part in enumerate(parts) if step]


def column_groups():
    shards = lax.axis_size("fsdp")
    return [list(range(c, shards, 2)) for c in range(2)]


def column_sum(total):
    return lax.psum_scatter(
        total, "fsdp", scatter_dimension=0, tiled=False, axis_index_groups=column_groups()
    )


def from_plane(share):
    return lax.all_gather(share, "seq", axis=0, tiled=False)


def joined(units, widths):
    count, depth, _ = units.shape

    def kernel(in_ref, *outs):
        for n, (wide, out_ref) in enumerate(zip(widths, outs)):
            for j in range(count):
                value = in_ref[j, :, pl.ds(sum(widths[:n]), wide)].astype(F32)
                out_ref[:, pl.ds(j * wide, wide)] = value

    return pl.pallas_call(
        kernel,
        in_specs=[pl.BlockSpec(memory_space=pltpu.VMEM)],
        out_specs=[pl.BlockSpec(memory_space=pltpu.VMEM)] * len(widths),
        out_shape=[jax.ShapeDtypeStruct((depth, count * wide), F32) for wide in widths],
        compiler_params=pltpu.CompilerParams(vmem_limit_bytes=24 * 2**20),
    )(units)


def shares(total):
    return [total] + over_plane(total)


def spread(where, parts, widths, more=0):
    depth = parts[0].shape[0] - (16 if more else 0)

    def kernel(place_ref, *refs):
        ins, outs = refs[: len(parts)], refs[len(parts) :]
        me = place_ref[2]
        for spot, ref in zip([me, me + 1 - 2 * (me % 2), (me + 2) % 4, 3 - me], ins):
            for n, wide in enumerate(widths):
                column = pl.ds(pl.multiple_of(spot * wide, wide), wide)
                value = ref[pl.ds(0, depth), pl.ds(sum(widths[:n]), wide)]
                outs[n][:, column] = value.astype(F32)
        if more:
            rows = [ref[pl.ds(depth, 16), :].astype(F32) for ref in ins]
            outs[-1][...] = (rows[0] + rows[1] + rows[2] + rows[3])[:more]

    shapes = [struct(depth, 4 * wide, dtype=F32) for wide in widths]
    if more:
        shapes.append(struct(more, parts[0].shape[1], dtype=F32))
    return pl.pallas_call(
        kernel,
        in_specs=[pl.BlockSpec(memory_space=pltpu.SMEM)]
        + [pl.BlockSpec(memory_space=pltpu.VMEM)] * len(parts),
        out_shape=shapes,
        compiler_params=pltpu.CompilerParams(vmem_limit_bytes=24 * 2**20),
    )(where, *parts)


def along_z(mine):
    return [send(mine, step, 0, 0) for step in range(1, lax.axis_size("fsdp") // 2)]


def over_plane(value):
    return [send(value, 0, 0, flip) for flip in (1, 2, 3)]


def to_partner(values):
    return [send(value, 0, 1, 0) for value in values]


def column(mine):
    return lax.all_gather(
        mine, "fsdp", axis=0, tiled=False, axis_index_groups=column_groups()
    )


def others(where, whole, depth):
    planes = whole.shape[0]
    return jnp.stack(
        [pick(whole, (where[0] + planes - step) % planes)[:depth] for step in range(1, planes)]
    )


def edges(two):
    half = two[0].shape[1] // 2
    return [two[0][:, :half], two[1][:, half:]]


def across(parts):
    return [send(parts[0], 0, 0, 2), send(parts[1], 0, 0, 1)]


def plain_sum(left, right):
    share = lax.psum_scatter(tn(left, right).astype(BF), "fsdp", scatter_dimension=0, tiled=True)
    return lax.psum(share, "seq").astype(F32)


def normal(values):
    center = values - jnp.mean(values, axis=-1, keepdims=True)
    inverse = lax.rsqrt(jnp.mean(center * center, axis=-1, keepdims=True) + epsilon)
    return center * inverse, inverse


def norm_back(grad, unit, inverse, gain):
    e = grad * gain
    return inverse * (
        e
        - jnp.mean(e, axis=-1, keepdims=True)
        - unit * jnp.mean(e * unit, axis=-1, keepdims=True)
    )


def gelu_and_slope(u):
    c = 0.7978845608
    square = u * u
    t = jnp.tanh(u * (c + (0.044715 * c) * square))
    half = 0.5 + 0.5 * t
    hid = u * half
    return hid, half + hid * (1.0 - t) * (c + (3 * 0.044715 * c) * square)


def call(kernel, grid, in_specs, out_specs, out_shape, scratch, args, room=56):
    return pl.pallas_call(
        kernel,
        grid=grid,
        in_specs=in_specs,
        out_specs=out_specs,
        out_shape=out_shape,
        scratch_shapes=scratch,
        compiler_params=pltpu.CompilerParams(vmem_limit_bytes=room * 2**20),
    )(*args)


def whole(array):
    return pl.BlockSpec(array.shape, lambda *i: (0,) * array.ndim, pipeline_mode=pl.Buffered(1))


def rows_of(height, width):
    return pl.BlockSpec((height, width), lambda i: (i, 0))


def columns_of(height, width):
    return pl.BlockSpec((height, width), lambda i: (0, i))


def struct(*shape, dtype=BF):
    return jax.ShapeDtypeStruct(shape, dtype)


def project(a, w, bias):
    rows, wide = a.shape[0], w.shape[1]

    def kernel(a_ref, w_ref, b_ref, out_ref):
        out_ref[...] = (nn(a_ref[...], w_ref[...]) + b_ref[...]).astype(BF)

    return call(
        kernel,
        (wide // TILE,),
        [whole(a), columns_of(w.shape[0], TILE), columns_of(1, TILE)],
        columns_of(rows, TILE),
        struct(rows, wide),
        [],
        (a, w, bias[None]),
    )


def middle(o, w, x, bias, gain, shift):
    rows, width = x.shape
    height = rows // 4

    def kernel(o_ref, w_ref, x_ref, b_ref, gain_ref, shift_ref, y_ref, a_ref):
        y = nn(o_ref[...], w_ref[...]) + x_ref[...].astype(F32) + b_ref[...]
        y_ref[...] = y
        unit, _ = normal(y)
        a_ref[...] = (unit * gain_ref[...] + shift_ref[...]).astype(BF)

    tile = rows_of(height, width)
    vectors = [bias[None], gain[None], shift[None]]
    return call(
        kernel,
        (rows // height,),
        [tile, whole(w), tile] + [whole(v) for v in vectors],
        [tile, tile],
        [struct(rows, width, dtype=F32), struct(rows, width)],
        [],
        (o, w, x, *vectors),
    )


def expand(a, w, bias):
    rows, wide = a.shape[0], w.shape[1]

    def kernel(a_ref, w_ref, b_ref, hid_ref, slope_ref):
        for part in range(PARTS):
            at = pl.ds(part * (rows // PARTS), rows // PARTS)
            hid, slope = gelu_and_slope(nn(a_ref[at, :], w_ref[...]) + b_ref[...])
            hid_ref[at, :] = hid.astype(BF)
            slope_ref[at, :] = slope.astype(BF)

    tile = columns_of(rows, WIDE)
    return call(
        kernel,
        (wide // WIDE,),
        [whole(a), columns_of(w.shape[0], WIDE), columns_of(1, WIDE)],
        [tile, tile],
        [struct(rows, wide)] * 2,
        [],
        (a, w, bias[None]),
    )


def back_norm(total, values, gain):
    unit, inverse = normal(values)
    sums = (
        jnp.sum(total * unit, axis=0, keepdims=True),
        jnp.sum(total, axis=0, keepdims=True),
    )
    return norm_back(total, unit, inverse, gain), sums


def gather_sums(refs, sums):
    @pl.when(pl.program_id(0) == 0)
    def _():
        for ref, value in zip(refs, sums):
            ref[...] = value

    @pl.when(pl.program_id(0) > 0)
    def _():
        for ref, value in zip(refs, sums):
            ref[...] += value


def back_ffn(g, w_down, slope, w_up, y1, gain):
    rows, wide = slope.shape
    width = y1.shape[1]
    height, part = rows // HEIGHTS, wide // 4

    def kernel(g_ref, down_ref, slope_ref, up_ref, y_ref, gain_ref, *refs):
        du_ref, sum_ref, dy_ref, d1_ref, s1_ref, s2_ref, s3_ref, down, up, sems = refs
        first = pl.program_id(0) == 0

        def bring(n):
            at = pl.ds(n * part, part)
            return (
                pltpu.make_async_copy(down_ref.at[at, :], down.at[at, :], sems.at[2 * n]),
                pltpu.make_async_copy(up_ref.at[:, at], up.at[:, at], sems.at[2 * n + 1]),
            )

        @pl.when(first)
        def _():
            sum_ref[...] = jnp.zeros_like(sum_ref)
            for n in range(4):
                for copy in bring(n):
                    copy.start()

        total = None
        for n in range(4):
            at = pl.ds(n * part, part)

            @pl.when(first)
            def _():
                for copy in bring(n):
                    copy.wait()

            dh = nt(g_ref[...], down[at, :])
            du = (dh * slope_ref[:, at].astype(F32)).astype(BF)
            du_ref[:, at] = du
            sum_ref[:, at] += jnp.sum(du.astype(F32), axis=0, keepdims=True)
            more = nt(du, up[:, at])
            total = more if total is None else total + more
        back, sums = back_norm(total, y_ref[...], gain_ref[...])
        dy = g_ref[...].astype(F32) + back
        dy_ref[...] = dy
        d1 = dy.astype(BF)
        d1_ref[...] = d1
        sums += (jnp.sum(d1.astype(F32), axis=0, keepdims=True),)
        gather_sums((s1_ref, s2_ref, s3_ref), sums)

    tile, long = rows_of(height, width), rows_of(height, wide)
    row = pl.BlockSpec((1, width), lambda i: (0, 0))
    far = pl.BlockSpec(memory_space=pl.ANY)
    vector = struct(1, width, dtype=F32)
    return call(
        kernel,
        (rows // height,),
        [tile, far, long, far, tile, whole(gain[None])],
        [long, pl.BlockSpec((1, wide), lambda i: (0, 0)), tile, tile, row, row, row],
        [
            struct(rows, wide),
            struct(1, wide, dtype=F32),
            struct(rows, width, dtype=F32),
            struct(rows, width),
            vector,
            vector,
            vector,
        ],
        [
            pltpu.VMEM(w_down.shape, BF),
            pltpu.VMEM(w_up.shape, BF),
            pltpu.SemaphoreType.DMA((8,)),
        ],
        (g, w_down, slope, w_up, y1, gain[None]),
    )


def back_out(d1, w):
    rows, width = d1.shape

    def kernel(d_ref, w_ref, out_ref):
        out_ref[...] = nt(d_ref[...], w_ref[...]).astype(BF)

    return call(
        kernel,
        (width // 512,),
        [whole(d1), rows_of(512, width)],
        columns_of(rows, 512),
        struct(rows, width),
        [],
        (d1, w),
    )


def back_qkv(dqkv, w, x, dy1, gain):
    rows, wide = dqkv.shape
    width = x.shape[1]
    height = rows // HEIGHTS

    def kernel(d_ref, w_ref, x_ref, dy_ref, gain_ref, dx_ref, s1_ref, s2_ref, s3_ref):
        back, sums = back_norm(
            nt(d_ref[...], w_ref[...]), x_ref[...].astype(F32), gain_ref[...]
        )
        dx_ref[...] = (dy_ref[...] + back).astype(BF)
        sums += (jnp.sum(d_ref[...].astype(F32), axis=0, keepdims=True),)
        gather_sums((s1_ref, s2_ref, s3_ref), sums)

    row, tile = pl.BlockSpec((1, width), lambda i: (0, 0)), rows_of(height, width)
    long = pl.BlockSpec((1, wide), lambda i: (0, 0))
    vector = struct(1, width, dtype=F32)
    return call(
        kernel,
        (rows // height,),
        [rows_of(height, wide), whole(w), tile, tile, whole(gain[None])],
        [tile, row, row, long],
        [struct(rows, width), vector, vector, struct(1, wide, dtype=F32)],
        [],
        (dqkv, w, x, dy1, gain[None]),
    )


def contract(hid, w, y1, bias):
    rows, wide = hid.shape
    width = w.shape[1]
    height = rows // HEIGHTS

    def kernel(h_ref, w_ref, y_ref, b_ref, out_ref):
        out_ref[...] = (nn(h_ref[...], w_ref[...]) + y_ref[...] + b_ref[...]).astype(BF)

    tile = rows_of(height, width)
    return call(
        kernel,
        (rows // height,),
        [rows_of(height, wide), whole(w), tile, whole(bias[None])],
        tile,
        struct(rows, width),
        [],
        (hid, w, y1, bias[None]),
    )


def plainly(
    tokens, live, x, g_low, small, w_qkv, w_out, w_up, w_down
):
    gain1, shift1, bias_qkv, bias_out, gain2, shift2, bias_up, bias_down = small
    slots, width = tokens.shape[2:]
    qkv_w, out_w, up_w, down_w = [
        lax.all_gather(w, "fsdp", axis=0, tiled=True) for w in (w_qkv, w_out, w_up, w_down)
    ]
    g = g_low.astype(F32)
    unit1, inverse1 = normal(x)
    a1 = (unit1 * gain1 + shift1).astype(BF)
    qkv = (nn(a1, qkv_w) + bias_qkv).astype(BF)
    o = per_image(attention_forward, live, slots, [qkv], width)
    y1 = x + nn(o, out_w) + bias_out
    unit2, inverse2 = normal(y1)
    a2 = (unit2 * gain2 + shift2).astype(BF)
    hid, slope = gelu_and_slope(nn(a2, up_w) + bias_up)
    hid = hid.astype(BF)
    s_down = plain_sum(hid, g_low)
    du = (nt(g_low, down_w) * slope).astype(BF)
    s_up = plain_sum(a2, du)
    activations = (y1 + nn(hid, down_w) + bias_down).astype(BF)
    da2 = nt(du, up_w)
    dy1 = g + norm_back(da2, unit2, inverse2, gain2)
    d1 = dy1.astype(BF)
    s_out = plain_sum(o, d1)
    do = nt(d1, out_w).astype(BF)
    dqkv = per_image(attention_backward, live, slots, [qkv, do], 3 * width)
    s_qkv = plain_sum(a1, dqkv)
    da1 = nt(dqkv, qkv_w)
    input_grad = (dy1 + norm_back(da1, unit1, inverse1, gain1)).astype(BF)
    sums = column_sums(da1, unit1, dqkv, d1, da2, unit2, du, g)
    shards = lax.axis_size("fsdp")
    packed = jnp.concatenate([part.reshape(shards, -1) for part in sums], axis=1)
    own = pick(lax.psum(packed, ("fsdp", "seq")), lax.axis_index("fsdp"))
    return activations, input_grad, s_qkv, s_out, s_up, s_down, own_parts(own, sums)


def column_sums(da1, unit1, dqkv, d1, da2, unit2, du, g):
    width = da1.shape[1]
    sums_qkv = jnp.sum(dqkv.astype(F32), axis=0)
    return (
        jnp.sum(da1 * unit1, axis=0),
        jnp.sum(da1, axis=0),
        jnp.concatenate([sums_qkv[:width], sums_qkv[2 * width :]]),
        jnp.sum(d1.astype(F32), axis=0),
        jnp.sum(da2 * unit2, axis=0),
        jnp.sum(da2, axis=0),
        jnp.sum(du.astype(F32), axis=0),
        jnp.sum(g, axis=0),
    )


def by_parts(where, tokens, live, x, g_low, vectors, w_qkv, w_out, w_up, w_down):
    slots, width = tokens.shape[2:]
    wide = w_up.shape[1]
    me = where[2]
    x_low = tokens.reshape(x.shape)

    def unit(w):
        return lax.dynamic_slice_in_dim(w, me * (w.shape[1] // 4), w.shape[1] // 4, axis=1)

    depth = w_qkv.shape[0]
    first = unit(w_qkv)
    z_first = along_z(first)
    packed = jnp.pad(packed_rows(vectors), ((0, 4), (0, 0))).reshape(2, width)
    packed = jnp.pad(packed, ((0, 14), (0, width // 4)))
    packed = jnp.concatenate([jnp.concatenate([unit(w_up), unit(w_out)], axis=1), packed])
    z_second = column(after(packed, z_first))
    z_third = column(unit(w_down))
    unit1, _ = normal(x)
    sum_down = jnp.sum(g_low.astype(F32), axis=0)

    far_own = to_partner(after([w_qkv, w_out], unit1))
    col_first = jnp.stack(after(z_first, far_own))
    far_own = far_own + to_partner(after([w_up, w_down], col_first))
    two_first = [send(col_first, 0, 0, flip) for flip in (1, 2)]
    far_first = to_partner([col_first])
    two_first, far_own, far_first = after((two_first, far_own, far_first), col_first)
    edges_first = edges(two_first)
    cross_first = across(edges_first)
    far_first = far_first + to_partner(two_first)
    z_second = after(z_second, edges_first)
    small = complete(small_table(where, z_second[:, depth : depth + 2, :width], vectors), width)
    gain1, shift1, bias_qkv, bias_out, gain2, shift2, bias_up, bias_down = small
    a1 = (unit1 * gain1 + shift1).astype(BF)
    col_second = others(where, z_second, depth)
    two_second = [send(col_second, 0, 0, flip) for flip in (1, 2)]
    cross_first = after(cross_first, col_second, a1)
    near_first = [col_first] + two_first + cross_first
    far_first = far_first + to_partner(cross_first)
    far_second = to_partner(after([col_second], far_first))
    qkv, qkv_w = assembled_project(
        where, [[w_qkv], far_own[:1]], [near_first, far_first], a1, bias_qkv
    )
    two_second, far_second = after((two_second, far_second), qkv)
    cross_second = across(edges(two_second))
    far_second = far_second + to_partner(two_second)
    o = per_image(attention_forward, live, slots, [after(qkv, two_second, sum_down)], width)
    cross_second, far_second = after((cross_second, far_second), o)
    near_second = [col_second] + two_second + cross_second
    far_second = far_second + to_partner(cross_second)
    y1, a2, up_w, out_w = assembled_middle(
        where,
        [[w_up, w_out], [far_own[2], far_own[1]]],
        [near_second, far_second],
        o,
        x_low,
        bias_out,
        gain2,
        shift2,
    )
    col_third = others(where, after(z_third, far_second), w_down.shape[0])
    two_third = [send(col_third, 0, 0, flip) for flip in (1, 2)]
    far_third = to_partner([col_third])
    hid, slope = expand(after(a2, col_third), up_w, bias_up)
    two_third, far_third = after((two_third, far_third), hid)
    edges_third = edges(two_third)
    cross_third = across(edges_third)
    far_third = far_third + to_partner(two_third)

    mine_down, far_down = wgrad_planes(where, after(hid, edges_third), g_low)
    cross_third, far_third = after((cross_third, far_third), mine_down)
    near_third = [col_third] + two_third + cross_third
    far_third = far_third + to_partner(cross_third)
    got_down = send(after(far_down, far_third), 0, 1, 0)
    (down_w,) = assemble(
        where,
        [[w_down], far_own[3:]],
        [near_third, far_third],
        [(wide, width)],
    )
    chip_down = chip_sum(where, *after(([mine_down], [got_down]), down_w))
    sides_down = sides(chip_down)
    du, sum_up, dy1, d1, sum_gain2, sum_shift2, sum_out = back_ffn(
        after(g_low, chip_down), down_w, slope, up_w, y1, gain2
    )
    side_down = side_sum(chip_down, after(sides_down, dy1))
    ends_down = ends(side_down)
    mine_up, far_up = wgrad_units(where, a2, after(du, side_down), (o, d1))
    total_down = plane_sum(side_down, after(ends_down, mine_up))
    got_up = send(after(far_up, total_down), 0, 1, 0)
    share_down = column_sum(total_down)
    do = back_out(after(d1, total_down), out_w)
    chip_up = chip_sum(where, *after(([mine_up], [got_up]), do))
    sides_up = sides(chip_up)
    dqkv = per_image(attention_backward, live, slots, [qkv, after(do, chip_up)], 3 * width)
    share_down = after(share_down, dqkv)
    side_up = side_sum(chip_up, after(sides_up, share_down))
    ends_up = ends(side_up)
    mine_qkv, far_qkv = wgrad_units(where, a1, after(dqkv, side_up))
    total_up = plane_sum(side_up, after(ends_up, mine_qkv))
    got_qkv = send(after(far_qkv, total_up), 0, 1, 0)
    share_up = column_sum(total_up)
    chip_qkv = chip_sum(where, *after(([mine_qkv], [got_qkv]), total_up))
    sides_qkv = sides(chip_qkv)
    input_grad, sum_gain1, sum_shift1, sum_qkv = back_qkv(
        after(dqkv, chip_qkv), qkv_w, x_low, dy1, gain1
    )
    side_qkv = side_sum(chip_qkv, after(sides_qkv, input_grad))
    ends_qkv = ends(side_qkv)

    sum_qv = jnp.concatenate([sum_qkv[0, :width], sum_qkv[0, 2 * width :]])
    sums = (
        sum_gain1[0],
        sum_shift1[0],
        sum_qv,
        sum_out[0],
        sum_gain2[0],
        sum_shift2[0],
        sum_up[0],
        sum_down,
    )
    planes = lax.axis_size("fsdp") // 2
    rows = packed_rows([part.reshape(planes, 2, -1) for part in sums])
    rows = pick(rows, where[1], 1) + send(pick(rows, 1 - where[1], 1), 0, 1, 0)
    rows = rows.reshape(planes, 2, -1).astype(BF)
    rows = jnp.pad(rows, ((0, 0), (0, 14), (0, 0)))

    from_down = from_plane(after(share_down, chip_qkv))
    column_qkv = column_parts(plane_columns(where, side_qkv, ends_qkv, rows))
    activations = contract(after(hid, column_qkv[0]), down_w, y1, bias_down)
    shares_up = shares(after(share_up, column_qkv[0]))
    share_qkv = add(*after(column_qkv, activations))
    shares_qkv = shares(share_qkv)
    (s_down,) = joined(after(from_down, share_qkv), [width // 4])
    s_up, s_out = spread(where, after(shares_up, share_qkv), [wide // 4, width // 4])
    s_qkv, own = spread(where, after(shares_qkv, s_up, s_down), [width * 3 // 4], 2)
    own = own.reshape(-1)
    return activations, input_grad, s_qkv, s_out, s_up, s_down, own_parts(own, sums)


def on_device(
    tokens,
    counts,
    ln1_gain,
    ln1_shift,
    w_qkv,
    b_qv,
    w_out,
    b_out,
    ln2_gain,
    ln2_shift,
    w_up,
    b_up,
    w_down,
    b_down,
    cotangent,
):
    where = place()
    vectors = (ln1_gain, ln1_shift, b_qv, b_out, ln2_gain, ln2_shift, b_up, b_down)
    micro, images, slots, width = tokens.shape
    rows = micro * images * slots
    own_start = lax.axis_index("seq") * images
    live = lax.dynamic_slice_in_dim(counts, own_start, images, axis=1).reshape(-1)
    x = tokens.reshape(rows, width).astype(F32)
    g_low = cotangent.reshape(rows, width)
    weights = (w_qkv, w_out, w_up, w_down)
    if by_hand():
        found = by_parts(where, tokens, live, x, g_low, vectors, *weights)
    else:
        packed = lax.all_gather(jnp.concatenate(vectors), "fsdp", axis=0, tiled=False)
        small = complete(cut(packed, vectors), width)
        found = plainly(tokens, live, x, g_low, small, *weights)
    activations, input_grad, s_qkv, s_out, s_up, s_down, sums = found
    return (
        activations.reshape(tokens.shape),
        input_grad.reshape(tokens.shape),
        sums[0],
        sums[1],
        s_qkv,
        sums[2],
        s_out,
        sums[3],
        sums[4],
        sums[5],
        s_up,
        sums[6],
        s_down,
        sums[7],
    )


def solution(mesh):
    row = P(None, ("fsdp", "seq"), None, None)
    one, two = P("fsdp"), P("fsdp", None)
    params = (one, one, two, one, two, one, one, one, two, one, two, one)
    return jax.shard_map(
        on_device,
        mesh=mesh,
        in_specs=(row, P(None, "fsdp")) + params + (row,),
        out_specs=(row, row) + params,
        check_vma=False,
    )
```

```python
import jax
import jax.numpy as jnp
from jax import lax
from jax.experimental import pallas as pl
from jax.experimental.pallas import tpu as pltpu
from jax.sharding import PartitionSpec as P

HEADS = 16
HD = 64
LANES = 256
PER = LANES // HD
TILE = 1024
HEIGHTS = 3
WIDE = 512
PARTS = 2
SCALE = HD ** (-0.5)
epsilon = 1e-05
BF = jnp.bfloat16
F32 = jnp.float32


def nt(a, b):
    return lax.dot_general(a, b, (((1,), (1,)), ((), ())), preferred_element_type=F32)


def tn(a, b):
    return lax.dot_general(a, b, (((0,), (0,)), ((), ())), preferred_element_type=F32)


def nn(a, b):
    return jnp.dot(a, b, preferred_element_type=F32)


def by_head(value):
    lane = lax.broadcasted_iota(jnp.int32, value.shape, 1) // HD
    zero = jnp.zeros_like(value)
    return jnp.concatenate([jnp.where(lane == h, value, zero) for h in range(PER)])


def own_lanes(value):
    slots = value.shape[0] // PER
    lane = lax.broadcasted_iota(jnp.int32, (slots, LANES), 1) // HD
    total = value[:slots]
    for h in range(1, PER):
        total = jnp.where(lane == h, value[h * slots : (h + 1) * slots], total)
    return total


def probabilities(k, heads, live):
    s = nt(k, heads)
    s = jnp.where(lax.broadcasted_iota(jnp.int32, s.shape, 0) < live, s, -1e30)
    e = jnp.exp(s - jnp.max(s, axis=0, keepdims=True))
    return e * (1.0 / jnp.sum(e, axis=0, keepdims=True))


def attention_forward(counts_ref, qkv_ref, out_ref):
    width = qkv_ref.shape[1] // 3
    live = counts_ref[pl.program_id(0)]
    for g in range(width // LANES):
        q = qkv_ref[:, pl.ds(g * LANES, LANES)] * jnp.asarray(SCALE, BF)
        k = qkv_ref[:, pl.ds(width + g * LANES, LANES)]
        v = qkv_ref[:, pl.ds(2 * width + g * LANES, LANES)]
        p = probabilities(k, by_head(q), live)
        out_ref[:, pl.ds(g * LANES, LANES)] = own_lanes(tn(p.astype(BF), v)).astype(BF)


def attention_backward(counts_ref, qkv_ref, do_ref, out_ref):
    width = qkv_ref.shape[1] // 3
    live = counts_ref[pl.program_id(0)]
    for g in range(width // LANES):
        q = qkv_ref[:, pl.ds(g * LANES, LANES)] * jnp.asarray(SCALE, BF)
        k = qkv_ref[:, pl.ds(width + g * LANES, LANES)]
        v = qkv_ref[:, pl.ds(2 * width + g * LANES, LANES)]
        heads, do_heads = by_head(q), by_head(do_ref[:, pl.ds(g * LANES, LANES)])
        p = probabilities(k, heads, live)
        dp = nt(v, do_heads)
        ds = (p * (dp - jnp.sum(p * dp, axis=0, keepdims=True))).astype(BF)
        out_ref[:, pl.ds(g * LANES, LANES)] = (own_lanes(tn(ds, k)) * SCALE).astype(BF)
        out_ref[:, pl.ds(width + g * LANES, LANES)] = nn(ds, heads).astype(BF)
        out_ref[:, pl.ds(2 * width + g * LANES, LANES)] = nn(p.astype(BF), do_heads).astype(BF)


def per_image(kernel, counts, slots, arrays, out_width):
    rows = arrays[0].shape[0]
    return pl.pallas_call(
        kernel,
        grid_spec=pltpu.PrefetchScalarGridSpec(
            num_scalar_prefetch=1,
            grid=(rows // slots,),
            in_specs=[pl.BlockSpec((slots, a.shape[1]), lambda i, c: (i, 0)) for a in arrays],
            out_specs=pl.BlockSpec((slots, out_width), lambda i, c: (i, 0)),
        ),
        out_shape=jax.ShapeDtypeStruct((rows, out_width), BF),
        compiler_params=pltpu.CompilerParams(vmem_limit_bytes=48 * 2**20),
    )(counts, *arrays)


def packed_rows(parts):
    rows = [part.reshape(part.shape[:-1] + (-1, 128)) for part in parts]
    total, start = 0, 0
    count = sum(part.shape[-2] for part in rows)
    for part in rows:
        size = part.shape[-2]
        edges = [(0, 0)] * (part.ndim - 2) + [(start, count - start - size), (0, 0)]
        total = total + jnp.pad(part, edges)
        start += size
    return total


def small_table(where, column, parts):
    planes = column.shape[0]
    both = jnp.stack([column, send(column, 0, 1, 0)])
    flips = (where[1] + jnp.arange(2)) % 2
    whole = both[flips].transpose(1, 0, 2, 3).reshape(2 * planes, -1)
    return cut(whole, parts)


def cut(whole, parts):
    result, start = [], 0
    for part in parts:
        size = part.shape[0]
        result.append(whole[:, start : start + size].reshape(-1).astype(F32))
        start += size
    return result


def complete(small, width):
    half = small[2]
    middle = jnp.zeros((width,), F32)
    return small[:2] + [jnp.concatenate([half[:width], middle, half[width:]])] + small[3:]


def own_parts(own, parts):
    result, start = [], 0
    for part in parts:
        size = part.shape[0] // lax.axis_size("fsdp")
        result.append(own[start : start + size])
        start += size
    return result


def send(value, step, flip_core, flip_seq):
    shards, others = lax.axis_size("fsdp"), lax.axis_size("seq")
    pairs = [
        (i * others + j, ((i + 2 * step) % shards ^ flip_core) * others + (j ^ flip_seq))
        for i in range(shards)
        for j in range(others)
    ]
    return lax.ppermute(value, ("fsdp", "seq"), pairs)


def after(value, *earlier):
    return lax.optimization_barrier((value, earlier))[0]


def pick(value, index, axis=0):
    return lax.dynamic_index_in_dim(value, index, axis=axis, keepdims=False)


def place():
    shard = lax.axis_index("fsdp")
    return jnp.stack([shard // 2, shard % 2, lax.axis_index("seq")]).astype(jnp.int32)


def by_hand():
    return lax.axis_size("seq") == 4 and lax.axis_size("fsdp") == 8


def assemble(where, owns, pieces, targets):
    planes, depth = pieces[0][0].shape[:2]
    planes += 1
    half = depth // 2
    flat = [*owns[0], *pieces[0], *owns[1], *pieces[1]]
    each = len(flat) // 2
    widths = [own.shape[1] // 4 for own in owns[0]]
    total = len(targets) * 2 * (4 + (planes - 1) * 5)

    def kernel(place_ref, *refs):
        ins, outs = refs[: len(flat)], refs[len(flat) : -3]
        held, in_sems, out_sems = refs[-3:]
        z, core, me = place_ref[0], place_ref[1], place_ref[2]
        places = [me, me + 1 - 2 * (me % 2), (me + 2) % 4, 3 - me, 3 - me]
        parts = [(0, depth), (0, depth), (0, depth), (0, half), (half, half)]

        moves = []
        for flip_core in range(2):
            for target, wide in enumerate(widths):
                shard = 2 * z + (core + flip_core) % 2
                own = ins[flip_core * each + target]
                for unit in range(4):
                    source = own.at[:, pl.ds(unit * wide, wide)]
                    moves.append((source, shard, jnp.int32(unit), 0, depth, target))
        for flip_core in range(2):
            others = ins[(flip_core + 1) * each - 5 : (flip_core + 1) * each]
            for step in range(1, planes):
                shard = 2 * ((z + planes - step) % planes) + (core + flip_core) % 2
                for n, spot in enumerate(places):
                    for target, wide in enumerate(widths):
                        source = others[n].at[step - 1, :, pl.ds(sum(widths[:target]), wide)]
                        moves.append((source, shard, spot, *parts[n], target))

        def bring(n):
            source, _, _, _, size, target = moves[n]
            spot = held.at[n, pl.ds(0, size), pl.ds(0, widths[target])]
            return pltpu.make_async_copy(source, spot, in_sems.at[n])

        def put(n):
            _, shard, unit, first, size, target = moves[n]
            wide = widths[target]
            row = pl.multiple_of(shard * depth + first, half)
            column = pl.multiple_of(unit * wide, wide)
            return pltpu.make_async_copy(
                held.at[n, pl.ds(0, size), pl.ds(0, wide)],
                outs[target].at[pl.ds(row, size), pl.ds(column, wide)],
                out_sems.at[n],
            )

        for n in range(total):
            bring(n).start()
        for n in range(total):
            bring(n).wait()
            put(n).start()
        for n in range(total):
            put(n).wait()

    return pl.pallas_call(
        kernel,
        in_specs=[pl.BlockSpec(memory_space=pltpu.SMEM)]
        + [pl.BlockSpec(memory_space=pl.ANY)] * len(flat),
        out_specs=[pl.BlockSpec(memory_space=pltpu.HBM)] * len(targets),
        out_shape=[jax.ShapeDtypeStruct(shape, BF) for shape in targets],
        scratch_shapes=[
            pltpu.VMEM((total, depth, max(widths)), BF),
            pltpu.SemaphoreType.DMA((total,)),
            pltpu.SemaphoreType.DMA((total,)),
        ],
        compiler_params=pltpu.CompilerParams(vmem_limit_bytes=58 * 2**20),
    )(where, *flat)


def halves(place_ref, total, depth):
    first = place_ref[1] == 0
    for n in range(total.shape[0] // (2 * depth)):
        low = total[2 * n * depth : (2 * n + 1) * depth].astype(BF)
        high = total[(2 * n + 1) * depth : (2 * n + 2) * depth].astype(BF)
        yield n, jnp.where(first, low, high), jnp.where(first, high, low)


def pieces_to(place_ref, ins, widths, held, sems):
    each = len(ins) // 2
    planes, depth = ins[each - 5].shape[0] + 1, ins[each - 5].shape[1]
    half = depth // 2
    z, core, me = place_ref[0], place_ref[1], place_ref[2]
    places = [me, me + 1 - 2 * (me % 2), (me + 2) % 4, 3 - me, 3 - me]
    parts = [(0, depth), (0, depth), (0, depth), (0, half), (half, half)]
    lists, count = [], 0
    for target, wide in enumerate(widths):
        copies = []
        for flip_core in range(2):
            side = (core + flip_core) % 2
            mine = ins[flip_core * each : (flip_core + 1) * each]
            sources = [
                (mine[target].at[:, pl.ds(unit * wide, wide)], 2 * z + side, unit, 0, depth)
                for unit in range(4)
            ]
            for step in range(1, planes):
                shard = 2 * ((z + planes - step) % planes) + side
                for other, spot, part in zip(mine[each - 5 :], places, parts):
                    source = other.at[step - 1, :, pl.ds(sum(widths[:target]), wide)]
                    sources.append((source, shard, spot, *part))
            for source, shard, unit, first, size in sources:
                row = pl.multiple_of(shard * depth + first, half)
                column = pl.multiple_of(jnp.int32(unit) * wide, wide)
                spot = held[target].at[pl.ds(row, size), pl.ds(column, wide)]
                copies.append(pltpu.make_async_copy(source, spot, sems.at[count]))
                count += 1
        lists.append(copies)
    return lists


def piece_count(pieces, targets):
    return targets * 2 * (4 + pieces[0][0].shape[0] * 5)


def assembled_project(where, owns, pieces, a, bias):
    flat = [*owns[0], *pieces[0], *owns[1], *pieces[1]]
    rows, width = a.shape
    wide = owns[0][0].shape[1]
    steps = wide // TILE

    def kernel(place_ref, *refs):
        ins, refs = refs[: len(flat)], refs[len(flat) :]
        a_ref, b_ref, y_ref, qkv_ref, out_ref, qkv, out, sems, done = refs
        step = pl.program_id(0)
        qkv_copies, out_copies = pieces_to(
            place_ref, ins, [wide // 4, width // 4], [qkv, out], sems
        )
        qkv_whole = pltpu.make_async_copy(qkv, qkv_ref, done.at[0])
        out_whole = pltpu.make_async_copy(out, out_ref, done.at[1])

        @pl.when(step == 0)
        def _():
            for copy in qkv_copies + out_copies:
                copy.start()
            for copy in qkv_copies:
                copy.wait()
            qkv_whole.start()

        @pl.when(step == 1)
        def _():
            for copy in out_copies:
                copy.wait()
            out_whole.start()

        w = qkv[:, pl.ds(pl.multiple_of(step * TILE, TILE), TILE)]
        y_ref[...] = (nn(a_ref[...], w) + b_ref[...]).astype(BF)

        @pl.when(step == steps - 1)
        def _():
            qkv_whole.wait()
            out_whole.wait()

    far = pl.BlockSpec(memory_space=pltpu.HBM)
    return call(
        kernel,
        (steps,),
        [pl.BlockSpec(memory_space=pltpu.SMEM)]
        + [pl.BlockSpec(memory_space=pl.ANY)] * len(flat)
        + [whole(a), columns_of(1, TILE)],
        [columns_of(rows, TILE), far, far],
        [struct(rows, wide), struct(width, wide), struct(width, width)],
        [
            pltpu.VMEM((width, wide), BF),
            pltpu.VMEM((width, width), BF),
            pltpu.SemaphoreType.DMA((piece_count(pieces, 2),)),
            pltpu.SemaphoreType.DMA((2,)),
        ],
        (where, *flat, a, bias[None]),
    )


def assembled_middle(where, owns, pieces, o, w, x, bias, gain, shift):
    flat = [*owns[0], *pieces[0], *owns[1], *pieces[1]]
    rows, width = x.shape
    wide = owns[0][0].shape[1]
    height = rows // 4

    def kernel(place_ref, *refs):
        ins, refs = refs[: len(flat)], refs[len(flat) :]
        o_ref, w_ref, x_ref, b_ref, gain_ref, shift_ref, y_ref, a_ref, up_ref = refs[:9]
        up, sems, done = refs[9:]
        step = pl.program_id(0)
        (copies,) = pieces_to(place_ref, ins, [wide // 4], [up], sems)
        up_whole = pltpu.make_async_copy(up, up_ref, done.at[0])

        @pl.when(step == 0)
        def _():
            for copy in copies:
                copy.start()

        @pl.when(step == 1)
        def _():
            for copy in copies:
                copy.wait()
            up_whole.start()

        y = nn(o_ref[...], w_ref[...]) + x_ref[...].astype(F32) + b_ref[...]
        y_ref[...] = y
        unit, _ = normal(y)
        a_ref[...] = (unit * gain_ref[...] + shift_ref[...]).astype(BF)

        @pl.when(step == 3)
        def _():
            up_whole.wait()

    tile = rows_of(height, width)
    vectors = [bias[None], gain[None], shift[None]]
    return call(
        kernel,
        (4,),
        [pl.BlockSpec(memory_space=pltpu.SMEM)]
        + [pl.BlockSpec(memory_space=pl.ANY)] * len(flat)
        + [tile, whole(w), tile]
        + [whole(v) for v in vectors],
        [tile, tile, pl.BlockSpec(memory_space=pltpu.HBM)],
        [struct(rows, width, dtype=F32), struct(rows, width), struct(width, wide)],
        [
            pltpu.VMEM((width, wide), BF),
            pltpu.SemaphoreType.DMA((piece_count(pieces, 1),)),
            pltpu.SemaphoreType.DMA((1,)),
        ],
        (where, *flat, o, w, x, *vectors),
    )


def wgrad_call(kernel, where, grid, specs, outs, shapes, arrays, scratch=()):
    return pl.pallas_call(
        kernel,
        grid_spec=pltpu.PrefetchScalarGridSpec(
            num_scalar_prefetch=1,
            grid=grid,
            in_specs=specs,
            out_specs=outs,
            scratch_shapes=scratch,
        ),
        out_shape=[jax.ShapeDtypeStruct(shape, BF) for shape in shapes],
        compiler_params=pltpu.CompilerParams(vmem_limit_bytes=50 * 2**20),
    )(where, *arrays)


def wgrad_units(where, left, right, extra=()):
    rows, width = left.shape
    shards = lax.axis_size("fsdp")
    planes, depth, wide = shards // 2, width // shards, right.shape[1] // 4
    part = extra[1].shape[1] // 4 if extra else 0
    count = 2 + len(extra)

    def kernel(place_ref, *refs):
        ins, outs, held = refs[:count], refs[count : count + 2], refs[count + 2 :]
        step = pl.program_id(0)
        if extra:

            @pl.when(step == 0)
            def _():
                for n, mine, far in halves(place_ref, tn(ins[2][...], ins[3][...]), depth):
                    for j in range(4):
                        held[0][j, n] = mine[:, j * part : (j + 1) * part]
                        held[1][j, n] = far[:, j * part : (j + 1) * part]

        for n, mine, far in halves(place_ref, tn(ins[0][...], ins[1][...]), depth):
            outs[0][n, :, pl.ds(0, wide)] = mine
            outs[1][n, :, pl.ds(0, wide)] = far
        if extra:
            for out, kept in zip(outs, held):
                out[:, :, pl.ds(wide, part)] = kept[step]

    one = pl.BlockSpec((rows, width), lambda j, c: (0, 0), pipeline_mode=pl.Buffered(1))
    specs = [one, pl.BlockSpec((rows, wide), lambda j, c: (0, j))] + [one] * len(extra)
    out = pl.BlockSpec((None, planes, depth, wide + part), lambda j, c: (j, 0, 0, 0))
    shape = (4, planes, depth, wide + part)
    scratch = [pltpu.VMEM((4, planes, depth, part), BF)] * 2 if extra else []
    arrays = (left, right, *extra)
    return wgrad_call(kernel, where, (4,), specs, [out] * 2, [shape] * 2, arrays, scratch)


def wgrad_planes(where, left, right):
    rows, width = right.shape
    planes = lax.axis_size("fsdp") // 2
    depth, wide = left.shape[1] // (2 * planes), width // 4

    def kernel(place_ref, left_ref, right_ref, mine_ref, far_ref):
        for _, mine, far in halves(place_ref, tn(left_ref[...], right_ref[...]), depth):
            for j in range(4):
                mine_ref[j] = mine[:, j * wide : (j + 1) * wide]
                far_ref[j] = far[:, j * wide : (j + 1) * wide]

    specs = [
        pl.BlockSpec((rows, 2 * depth), lambda z, c: (0, z)),
        pl.BlockSpec((rows, width), lambda z, c: (0, 0), pipeline_mode=pl.Buffered(1)),
    ]
    out = pl.BlockSpec((4, None, depth, wide), lambda z, c: (0, z, 0, 0))
    shape = (4, planes, depth, wide)
    return wgrad_call(kernel, where, (planes,), specs, [out] * 2, [shape] * 2, (left, right))


def add(*parts):
    if len(parts) == 2:
        return parts[0] + parts[1]
    total = parts[0].astype(F32)
    for part in parts[1:]:
        total += part.astype(F32)
    return total.astype(BF)


def chip_sum(where, mine, far):
    planes, depth = mine[0].shape[1:3]
    wides = [part.shape[3] for part in mine]
    half = planes // 2

    def kernel(place_ref, *refs):
        ins, outs = refs[: 2 * len(wides)], refs[2 * len(wides) :]
        for flip, (first, second) in enumerate(((0, 2), (1, 2), (0, 3), (1, 3))):

            @pl.when(pl.program_id(0) == flip)
            def _():
                for n, wide in enumerate(wides):
                    columns = pl.ds(sum(wides[:n]), wide)
                    total = add(ins[n][...], ins[len(wides) + n][...])
                    outs[first][flip // 2, :, :, columns] = total[:half]
                    outs[second][flip % 2, :, :, columns] = total[half:]

    piece = (2, half, depth, sum(wides))
    return pl.pallas_call(
        kernel,
        grid_spec=pltpu.PrefetchScalarGridSpec(
            num_scalar_prefetch=1,
            grid=(4,),
            in_specs=[
                pl.BlockSpec((None, planes, depth, wide), lambda f, c: (c[2] ^ f, 0, 0, 0))
                for wide in wides
            ]
            * 2,
            out_specs=[pl.BlockSpec(piece, lambda f, c: (0, 0, 0, 0))] * 4,
        ),
        out_shape=[jax.ShapeDtypeStruct(piece, BF)] * 4,
        compiler_params=pltpu.CompilerParams(vmem_limit_bytes=40 * 2**20),
    )(where, *mine, *far)


def sides(chip):
    return [send(chip[1], 0, 0, 1), send(chip[3], 0, 0, 2)]


def side_sum(chip, got):
    half, depth, wide = chip[0].shape[1:]

    def kernel(a_ref, ga_ref, b_ref, gb_ref, *outs):
        for own, other, outs_of in ((a_ref, ga_ref, outs[:2]), (b_ref, gb_ref, outs[2:])):
            for n in range(2):

                @pl.when(pl.program_id(0) == n)
                def _():
                    outs_of[n][...] = add(own[...], other[...])

    return pl.pallas_call(
        kernel,
        grid=(2,),
        in_specs=[pl.BlockSpec((None, half, depth, wide), lambda n: (n, 0, 0, 0))] * 4,
        out_specs=[pl.BlockSpec((half, depth, wide), lambda n: (0, 0, 0))] * 4,
        out_shape=[jax.ShapeDtypeStruct((half, depth, wide), BF)] * 4,
        compiler_params=pltpu.CompilerParams(vmem_limit_bytes=32 * 2**20),
    )(chip[0], got[0], chip[2], got[1])


def ends(side):
    return [send(side[1], 0, 0, 2), send(side[3], 0, 0, 1)]


def plane_sum(side, got):
    half, depth, wide = side[0].shape
    parts = [side[0], got[0], side[2], got[1]]

    def kernel(*refs):
        out = refs[-1]
        for n in range(half):
            out[n] = add(refs[0][n], refs[1][n])
            out[half + n] = add(refs[2][n], refs[3][n])

    return pl.pallas_call(
        kernel,
        in_specs=[pl.BlockSpec(memory_space=pltpu.VMEM)] * 4,
        out_shape=jax.ShapeDtypeStruct((2 * half, depth, wide), BF),
        compiler_params=pltpu.CompilerParams(vmem_limit_bytes=24 * 2**20),
    )(*parts)


def plane_columns(where, side, got, last):
    half, depth, wide = side[0].shape
    planes, more = 2 * half, 16
    parts = [side[0], got[0], side[2], got[1], last]

    def kernel(place_ref, *refs):
        ins, outs = refs[:5], refs[5:]
        for step in range(planes):
            at = (place_ref[0] + step) % planes

            @pl.when(at < half)
            def _():
                outs[step][pl.ds(0, depth), :] = add(ins[0][at], ins[1][at])

            @pl.when(at >= half)
            def _():
                outs[step][pl.ds(0, depth), :] = add(ins[2][at - half], ins[3][at - half])

            outs[step][pl.ds(depth, more), :] = ins[4][at]

    return pl.pallas_call(
        kernel,
        in_specs=[pl.BlockSpec(memory_space=pltpu.SMEM)]
        + [pl.BlockSpec(memory_space=pltpu.VMEM)] * 5,
        out_shape=[jax.ShapeDtypeStruct((depth + more, wide), BF)] * planes,
        compiler_params=pltpu.CompilerParams(vmem_limit_bytes=24 * 2**20),
    )(where, *parts)


def column_parts(parts):
    return [parts[0]] + [send(part, step, 0, 0) for step, part in enumerate(parts) if step]


def column_groups():
    shards = lax.axis_size("fsdp")
    return [list(range(c, shards, 2)) for c in range(2)]


def column_sum(total):
    return lax.psum_scatter(
        total, "fsdp", scatter_dimension=0, tiled=False, axis_index_groups=column_groups()
    )


def from_plane(share):
    return lax.all_gather(share, "seq", axis=0, tiled=False)


def joined(units, widths):
    count, depth, _ = units.shape

    def kernel(in_ref, *outs):
        for n, (wide, out_ref) in enumerate(zip(widths, outs)):
            for j in range(count):
                value = in_ref[j, :, pl.ds(sum(widths[:n]), wide)].astype(F32)
                out_ref[:, pl.ds(j * wide, wide)] = value

    return pl.pallas_call(
        kernel,
        in_specs=[pl.BlockSpec(memory_space=pltpu.VMEM)],
        out_specs=[pl.BlockSpec(memory_space=pltpu.VMEM)] * len(widths),
        out_shape=[jax.ShapeDtypeStruct((depth, count * wide), F32) for wide in widths],
        compiler_params=pltpu.CompilerParams(vmem_limit_bytes=24 * 2**20),
    )(units)


def shares(total):
    return [total] + over_plane(total)


def spread(where, parts, widths, more=0):
    depth = parts[0].shape[0] - (16 if more else 0)

    def kernel(place_ref, *refs):
        ins, outs = refs[: len(parts)], refs[len(parts) :]
        me = place_ref[2]
        for spot, ref in zip([me, me + 1 - 2 * (me % 2), (me + 2) % 4, 3 - me], ins):
            for n, wide in enumerate(widths):
                column = pl.ds(pl.multiple_of(spot * wide, wide), wide)
                value = ref[pl.ds(0, depth), pl.ds(sum(widths[:n]), wide)]
                outs[n][:, column] = value.astype(F32)
        if more:
            rows = [ref[pl.ds(depth, 16), :].astype(F32) for ref in ins]
            outs[-1][...] = (rows[0] + rows[1] + rows[2] + rows[3])[:more]

    shapes = [struct(depth, 4 * wide, dtype=F32) for wide in widths]
    if more:
        shapes.append(struct(more, parts[0].shape[1], dtype=F32))
    return pl.pallas_call(
        kernel,
        in_specs=[pl.BlockSpec(memory_space=pltpu.SMEM)]
        + [pl.BlockSpec(memory_space=pltpu.VMEM)] * len(parts),
        out_shape=shapes,
        compiler_params=pltpu.CompilerParams(vmem_limit_bytes=24 * 2**20),
    )(where, *parts)


def along_z(mine):
    return [send(mine, step, 0, 0) for step in range(1, lax.axis_size("fsdp") // 2)]


def over_plane(value):
    return [send(value, 0, 0, flip) for flip in (1, 2, 3)]


def to_partner(values):
    return [send(value, 0, 1, 0) for value in values]


def column(mine):
    return lax.all_gather(
        mine, "fsdp", axis=0, tiled=False, axis_index_groups=column_groups()
    )


def others(where, whole, depth):
    planes = whole.shape[0]
    return jnp.stack(
        [pick(whole, (where[0] + planes - step) % planes)[:depth] for step in range(1, planes)]
    )


def edges(two):
    half = two[0].shape[1] // 2
    return [two[0][:, :half], two[1][:, half:]]


def across(parts):
    return [send(parts[0], 0, 0, 2), send(parts[1], 0, 0, 1)]


def plain_sum(left, right):
    share = lax.psum_scatter(tn(left, right).astype(BF), "fsdp", scatter_dimension=0, tiled=True)
    return lax.psum(share, "seq").astype(F32)


def normal(values):
    center = values - jnp.mean(values, axis=-1, keepdims=True)
    inverse = lax.rsqrt(jnp.mean(center * center, axis=-1, keepdims=True) + epsilon)
    return center * inverse, inverse


def norm_back(grad, unit, inverse, gain):
    e = grad * gain
    return inverse * (
        e
        - jnp.mean(e, axis=-1, keepdims=True)
        - unit * jnp.mean(e * unit, axis=-1, keepdims=True)
    )


def gelu_and_slope(u):
    c = 0.7978845608
    square = u * u
    t = jnp.tanh(u * (c + (0.044715 * c) * square))
    half = 0.5 + 0.5 * t
    hid = u * half
    return hid, half + hid * (1.0 - t) * (c + (3 * 0.044715 * c) * square)


def call(kernel, grid, in_specs, out_specs, out_shape, scratch, args, room=56):
    return pl.pallas_call(
        kernel,
        grid=grid,
        in_specs=in_specs,
        out_specs=out_specs,
        out_shape=out_shape,
        scratch_shapes=scratch,
        compiler_params=pltpu.CompilerParams(vmem_limit_bytes=room * 2**20),
    )(*args)


def whole(array):
    return pl.BlockSpec(array.shape, lambda *i: (0,) * array.ndim, pipeline_mode=pl.Buffered(1))


def rows_of(height, width):
    return pl.BlockSpec((height, width), lambda i: (i, 0))


def columns_of(height, width):
    return pl.BlockSpec((height, width), lambda i: (0, i))


def struct(*shape, dtype=BF):
    return jax.ShapeDtypeStruct(shape, dtype)


def project(a, w, bias):
    rows, wide = a.shape[0], w.shape[1]

    def kernel(a_ref, w_ref, b_ref, out_ref):
        out_ref[...] = (nn(a_ref[...], w_ref[...]) + b_ref[...]).astype(BF)

    return call(
        kernel,
        (wide // TILE,),
        [whole(a), columns_of(w.shape[0], TILE), columns_of(1, TILE)],
        columns_of(rows, TILE),
        struct(rows, wide),
        [],
        (a, w, bias[None]),
    )


def middle(o, w, x, bias, gain, shift):
    rows, width = x.shape
    height = rows // 4

    def kernel(o_ref, w_ref, x_ref, b_ref, gain_ref, shift_ref, y_ref, a_ref):
        y = nn(o_ref[...], w_ref[...]) + x_ref[...].astype(F32) + b_ref[...]
        y_ref[...] = y
        unit, _ = normal(y)
        a_ref[...] = (unit * gain_ref[...] + shift_ref[...]).astype(BF)

    tile = rows_of(height, width)
    vectors = [bias[None], gain[None], shift[None]]
    return call(
        kernel,
        (rows // height,),
        [tile, whole(w), tile] + [whole(v) for v in vectors],
        [tile, tile],
        [struct(rows, width, dtype=F32), struct(rows, width)],
        [],
        (o, w, x, *vectors),
    )


def expand(a, w, bias):
    rows, wide = a.shape[0], w.shape[1]

    def kernel(a_ref, w_ref, b_ref, hid_ref, slope_ref):
        for part in range(PARTS):
            at = pl.ds(part * (rows // PARTS), rows // PARTS)
            hid, slope = gelu_and_slope(nn(a_ref[at, :], w_ref[...]) + b_ref[...])
            hid_ref[at, :] = hid.astype(BF)
            slope_ref[at, :] = slope.astype(BF)

    tile = columns_of(rows, WIDE)
    return call(
        kernel,
        (wide // WIDE,),
        [whole(a), columns_of(w.shape[0], WIDE), columns_of(1, WIDE)],
        [tile, tile],
        [struct(rows, wide)] * 2,
        [],
        (a, w, bias[None]),
    )


def back_norm(total, values, gain):
    unit, inverse = normal(values)
    sums = (
        jnp.sum(total * unit, axis=0, keepdims=True),
        jnp.sum(total, axis=0, keepdims=True),
    )
    return norm_back(total, unit, inverse, gain), sums


def gather_sums(refs, sums):
    @pl.when(pl.program_id(0) == 0)
    def _():
        for ref, value in zip(refs, sums):
            ref[...] = value

    @pl.when(pl.program_id(0) > 0)
    def _():
        for ref, value in zip(refs, sums):
            ref[...] += value


def back_ffn(g, w_down, slope, w_up, y1, gain):
    rows, wide = slope.shape
    width = y1.shape[1]
    height, part = rows // HEIGHTS, wide // 4

    def kernel(g_ref, down_ref, slope_ref, up_ref, y_ref, gain_ref, *refs):
        du_ref, sum_ref, dy_ref, d1_ref, s1_ref, s2_ref, s3_ref, down, up, sems = refs
        first = pl.program_id(0) == 0

        def bring(n):
            at = pl.ds(n * part, part)
            return (
                pltpu.make_async_copy(down_ref.at[at, :], down.at[at, :], sems.at[2 * n]),
                pltpu.make_async_copy(up_ref.at[:, at], up.at[:, at], sems.at[2 * n + 1]),
            )

        @pl.when(first)
        def _():
            sum_ref[...] = jnp.zeros_like(sum_ref)
            for n in range(4):
                for copy in bring(n):
                    copy.start()

        total = None
        for n in range(4):
            at = pl.ds(n * part, part)

            @pl.when(first)
            def _():
                for copy in bring(n):
                    copy.wait()

            dh = nt(g_ref[...], down[at, :])
            du = (dh * slope_ref[:, at].astype(F32)).astype(BF)
            du_ref[:, at] = du
            sum_ref[:, at] += jnp.sum(du.astype(F32), axis=0, keepdims=True)
            more = nt(du, up[:, at])
            total = more if total is None else total + more
        back, sums = back_norm(total, y_ref[...], gain_ref[...])
        dy = g_ref[...].astype(F32) + back
        dy_ref[...] = dy
        d1 = dy.astype(BF)
        d1_ref[...] = d1
        sums += (jnp.sum(d1.astype(F32), axis=0, keepdims=True),)
        gather_sums((s1_ref, s2_ref, s3_ref), sums)

    tile, long = rows_of(height, width), rows_of(height, wide)
    row = pl.BlockSpec((1, width), lambda i: (0, 0))
    far = pl.BlockSpec(memory_space=pl.ANY)
    vector = struct(1, width, dtype=F32)
    return call(
        kernel,
        (rows // height,),
        [tile, far, long, far, tile, whole(gain[None])],
        [long, pl.BlockSpec((1, wide), lambda i: (0, 0)), tile, tile, row, row, row],
        [
            struct(rows, wide),
            struct(1, wide, dtype=F32),
            struct(rows, width, dtype=F32),
            struct(rows, width),
            vector,
            vector,
            vector,
        ],
        [
            pltpu.VMEM(w_down.shape, BF),
            pltpu.VMEM(w_up.shape, BF),
            pltpu.SemaphoreType.DMA((8,)),
        ],
        (g, w_down, slope, w_up, y1, gain[None]),
    )


def back_out(d1, w):
    rows, width = d1.shape

    def kernel(d_ref, w_ref, out_ref):
        out_ref[...] = nt(d_ref[...], w_ref[...]).astype(BF)

    return call(
        kernel,
        (width // 512,),
        [whole(d1), rows_of(512, width)],
        columns_of(rows, 512),
        struct(rows, width),
        [],
        (d1, w),
    )


def back_qkv(dqkv, w, x, dy1, gain):
    rows, wide = dqkv.shape
    width = x.shape[1]
    height = rows // HEIGHTS

    def kernel(d_ref, w_ref, x_ref, dy_ref, gain_ref, dx_ref, s1_ref, s2_ref, s3_ref):
        back, sums = back_norm(
            nt(d_ref[...], w_ref[...]), x_ref[...].astype(F32), gain_ref[...]
        )
        dx_ref[...] = (dy_ref[...] + back).astype(BF)
        sums += (jnp.sum(d_ref[...].astype(F32), axis=0, keepdims=True),)
        gather_sums((s1_ref, s2_ref, s3_ref), sums)

    row, tile = pl.BlockSpec((1, width), lambda i: (0, 0)), rows_of(height, width)
    long = pl.BlockSpec((1, wide), lambda i: (0, 0))
    vector = struct(1, width, dtype=F32)
    return call(
        kernel,
        (rows // height,),
        [rows_of(height, wide), whole(w), tile, tile, whole(gain[None])],
        [tile, row, row, long],
        [struct(rows, width), vector, vector, struct(1, wide, dtype=F32)],
        [],
        (dqkv, w, x, dy1, gain[None]),
    )


def contract(hid, w, y1, bias):
    rows, wide = hid.shape
    width = w.shape[1]
    height = rows // HEIGHTS

    def kernel(h_ref, w_ref, y_ref, b_ref, out_ref):
        out_ref[...] = (nn(h_ref[...], w_ref[...]) + y_ref[...] + b_ref[...]).astype(BF)

    tile = rows_of(height, width)
    return call(
        kernel,
        (rows // height,),
        [rows_of(height, wide), whole(w), tile, whole(bias[None])],
        tile,
        struct(rows, width),
        [],
        (hid, w, y1, bias[None]),
    )


def plainly(
    tokens, live, x, g_low, small, w_qkv, w_out, w_up, w_down
):
    gain1, shift1, bias_qkv, bias_out, gain2, shift2, bias_up, bias_down = small
    slots, width = tokens.shape[2:]
    qkv_w, out_w, up_w, down_w = [
        lax.all_gather(w, "fsdp", axis=0, tiled=True) for w in (w_qkv, w_out, w_up, w_down)
    ]
    g = g_low.astype(F32)
    unit1, inverse1 = normal(x)
    a1 = (unit1 * gain1 + shift1).astype(BF)
    qkv = (nn(a1, qkv_w) + bias_qkv).astype(BF)
    o = per_image(attention_forward, live, slots, [qkv], width)
    y1 = x + nn(o, out_w) + bias_out
    unit2, inverse2 = normal(y1)
    a2 = (unit2 * gain2 + shift2).astype(BF)
    hid, slope = gelu_and_slope(nn(a2, up_w) + bias_up)
    hid = hid.astype(BF)
    s_down = plain_sum(hid, g_low)
    du = (nt(g_low, down_w) * slope).astype(BF)
    s_up = plain_sum(a2, du)
    activations = (y1 + nn(hid, down_w) + bias_down).astype(BF)
    da2 = nt(du, up_w)
    dy1 = g + norm_back(da2, unit2, inverse2, gain2)
    d1 = dy1.astype(BF)
    s_out = plain_sum(o, d1)
    do = nt(d1, out_w).astype(BF)
    dqkv = per_image(attention_backward, live, slots, [qkv, do], 3 * width)
    s_qkv = plain_sum(a1, dqkv)
    da1 = nt(dqkv, qkv_w)
    input_grad = (dy1 + norm_back(da1, unit1, inverse1, gain1)).astype(BF)
    sums = column_sums(da1, unit1, dqkv, d1, da2, unit2, du, g)
    shards = lax.axis_size("fsdp")
    packed = jnp.concatenate([part.reshape(shards, -1) for part in sums], axis=1)
    own = pick(lax.psum(packed, ("fsdp", "seq")), lax.axis_index("fsdp"))
    return activations, input_grad, s_qkv, s_out, s_up, s_down, own_parts(own, sums)


def column_sums(da1, unit1, dqkv, d1, da2, unit2, du, g):
    width = da1.shape[1]
    sums_qkv = jnp.sum(dqkv.astype(F32), axis=0)
    return (
        jnp.sum(da1 * unit1, axis=0),
        jnp.sum(da1, axis=0),
        jnp.concatenate([sums_qkv[:width], sums_qkv[2 * width :]]),
        jnp.sum(d1.astype(F32), axis=0),
        jnp.sum(da2 * unit2, axis=0),
        jnp.sum(da2, axis=0),
        jnp.sum(du.astype(F32), axis=0),
        jnp.sum(g, axis=0),
    )


def by_parts(where, tokens, live, x, g_low, vectors, w_qkv, w_out, w_up, w_down):
    slots, width = tokens.shape[2:]
    wide = w_up.shape[1]
    me = where[2]
    x_low = tokens.reshape(x.shape)

    def unit(w):
        return lax.dynamic_slice_in_dim(w, me * (w.shape[1] // 4), w.shape[1] // 4, axis=1)

    depth = w_qkv.shape[0]
    first = jnp.concatenate([unit(w_qkv), unit(w_out)], axis=1)
    z_first = along_z(first)
    packed = jnp.pad(packed_rows(vectors), ((0, 4), (0, 0))).reshape(2, width)
    packed = jnp.pad(packed, ((0, 14), (0, 0)))
    packed = jnp.concatenate([unit(w_up), packed])
    third = unit(w_down)
    z_second = column(after(packed, z_first, third))
    z_third = column(third)
    unit1, _ = normal(x)
    sum_down = jnp.sum(g_low.astype(F32), axis=0)

    far_own = to_partner(after([w_qkv, w_out], unit1))
    col_first = jnp.stack(after(z_first, far_own))
    far_own = far_own + to_partner(after([w_up, w_down], col_first))
    two_first = [send(col_first, 0, 0, flip) for flip in (1, 2)]
    far_first = to_partner([col_first])
    two_first, far_own, far_first = after((two_first, far_own, far_first), col_first)
    edges_first = edges(two_first)
    cross_first = across(edges_first)
    far_first = far_first + to_partner(two_first)
    z_second = after(z_second, edges_first)
    small = complete(small_table(where, z_second[:, depth : depth + 2, :width], vectors), width)
    gain1, shift1, bias_qkv, bias_out, gain2, shift2, bias_up, bias_down = small
    a1 = (unit1 * gain1 + shift1).astype(BF)
    col_second = others(where, z_second, depth)
    two_second = [send(col_second, 0, 0, flip) for flip in (1, 2)]
    cross_first = after(cross_first, col_second, a1)
    near_first = [col_first] + two_first + cross_first
    far_first = far_first + to_partner(cross_first)
    far_second = to_partner(after([col_second], far_first))
    qkv, qkv_w, out_w = assembled_project(
        where, [[w_qkv, w_out], far_own[:2]], [near_first, far_first], a1, bias_qkv
    )
    two_second, far_second = after((two_second, far_second), qkv)
    cross_second = across(edges(two_second))
    far_second = far_second + to_partner(two_second)
    o = per_image(attention_forward, live, slots, [after(qkv, two_second, sum_down)], width)
    cross_second, far_second = after((cross_second, far_second), o)
    near_second = [col_second] + two_second + cross_second
    far_second = far_second + to_partner(cross_second)
    y1, a2, up_w = assembled_middle(
        where,
        [[w_up], far_own[2:3]],
        [near_second, far_second],
        o,
        out_w,
        x_low,
        bias_out,
        gain2,
        shift2,
    )
    col_third = others(where, after(z_third, far_second), w_down.shape[0])
    two_third = [send(col_third, 0, 0, flip) for flip in (1, 2)]
    far_third = to_partner([col_third])
    hid, slope = expand(after(a2, col_third), up_w, bias_up)
    two_third, far_third = after((two_third, far_third), hid)
    edges_third = edges(two_third)
    cross_third = across(edges_third)
    far_third = far_third + to_partner(two_third)

    mine_down, far_down = wgrad_planes(where, after(hid, edges_third), g_low)
    cross_third, far_third = after((cross_third, far_third), mine_down)
    near_third = [col_third] + two_third + cross_third
    far_third = far_third + to_partner(cross_third)
    got_down = send(after(far_down, far_third), 0, 1, 0)
    (down_w,) = assemble(
        where,
        [[w_down], far_own[3:]],
        [near_third, far_third],
        [(wide, width)],
    )
    chip_down = chip_sum(where, *after(([mine_down], [got_down]), down_w))
    sides_down = sides(chip_down)
    du, sum_up, dy1, d1, sum_gain2, sum_shift2, sum_out = back_ffn(
        after(g_low, chip_down), down_w, slope, up_w, y1, gain2
    )
    side_down = side_sum(chip_down, after(sides_down, dy1))
    ends_down = ends(side_down)
    mine_up, far_up = wgrad_units(where, a2, after(du, side_down), (o, d1))
    total_down = plane_sum(side_down, after(ends_down, mine_up))
    got_up = send(after(far_up, total_down), 0, 1, 0)
    share_down = column_sum(total_down)
    do = back_out(after(d1, total_down), out_w)
    chip_up = chip_sum(where, *after(([mine_up], [got_up]), do))
    sides_up = sides(chip_up)
    dqkv = per_image(attention_backward, live, slots, [qkv, after(do, chip_up)], 3 * width)
    share_down = after(share_down, dqkv)
    side_up = side_sum(chip_up, after(sides_up, share_down))
    ends_up = ends(side_up)
    mine_qkv, far_qkv = wgrad_units(where, a1, after(dqkv, side_up))
    total_up = plane_sum(side_up, after(ends_up, mine_qkv))
    got_qkv = send(after(far_qkv, total_up), 0, 1, 0)
    share_up = column_sum(total_up)
    chip_qkv = chip_sum(where, *after(([mine_qkv], [got_qkv]), total_up))
    sides_qkv = sides(chip_qkv)
    input_grad, sum_gain1, sum_shift1, sum_qkv = back_qkv(
        after(dqkv, chip_qkv), qkv_w, x_low, dy1, gain1
    )
    side_qkv = side_sum(chip_qkv, after(sides_qkv, input_grad))
    ends_qkv = ends(side_qkv)

    sum_qv = jnp.concatenate([sum_qkv[0, :width], sum_qkv[0, 2 * width :]])
    sums = (
        sum_gain1[0],
        sum_shift1[0],
        sum_qv,
        sum_out[0],
        sum_gain2[0],
        sum_shift2[0],
        sum_up[0],
        sum_down,
    )
    planes = lax.axis_size("fsdp") // 2
    rows = packed_rows([part.reshape(planes, 2, -1) for part in sums])
    rows = pick(rows, where[1], 1) + send(pick(rows, 1 - where[1], 1), 0, 1, 0)
    rows = rows.reshape(planes, 2, -1).astype(BF)
    rows = jnp.pad(rows, ((0, 0), (0, 14), (0, 0)))

    from_down = from_plane(after(share_down, chip_qkv))
    column_qkv = column_parts(plane_columns(where, side_qkv, ends_qkv, rows))
    activations = contract(after(hid, column_qkv[0]), down_w, y1, bias_down)
    shares_up = shares(after(share_up, column_qkv[0]))
    share_qkv = add(*after(column_qkv, activations))
    shares_qkv = shares(share_qkv)
    (s_down,) = joined(after(from_down, share_qkv), [width // 4])
    s_up, s_out = spread(where, after(shares_up, s_down), [wide // 4, width // 4])
    s_qkv, own = spread(where, after(shares_qkv, s_up), [width * 3 // 4], 2)
    own = own.reshape(-1)
    return activations, input_grad, s_qkv, s_out, s_up, s_down, own_parts(own, sums)


def on_device(
    tokens,
    counts,
    ln1_gain,
    ln1_shift,
    w_qkv,
    b_qv,
    w_out,
    b_out,
    ln2_gain,
    ln2_shift,
    w_up,
    b_up,
    w_down,
    b_down,
    cotangent,
):
    where = place()
    vectors = (ln1_gain, ln1_shift, b_qv, b_out, ln2_gain, ln2_shift, b_up, b_down)
    micro, images, slots, width = tokens.shape
    rows = micro * images * slots
    own_start = lax.axis_index("seq") * images
    live = lax.dynamic_slice_in_dim(counts, own_start, images, axis=1).reshape(-1)
    x = tokens.reshape(rows, width).astype(F32)
    g_low = cotangent.reshape(rows, width)
    weights = (w_qkv, w_out, w_up, w_down)
    if by_hand():
        found = by_parts(where, tokens, live, x, g_low, vectors, *weights)
    else:
        packed = lax.all_gather(jnp.concatenate(vectors), "fsdp", axis=0, tiled=False)
        small = complete(cut(packed, vectors), width)
        found = plainly(tokens, live, x, g_low, small, *weights)
    activations, input_grad, s_qkv, s_out, s_up, s_down, sums = found
    return (
        activations.reshape(tokens.shape),
        input_grad.reshape(tokens.shape),
        sums[0],
        sums[1],
        s_qkv,
        sums[2],
        s_out,
        sums[3],
        sums[4],
        sums[5],
        s_up,
        sums[6],
        s_down,
        sums[7],
    )


def solution(mesh):
    row = P(None, ("fsdp", "seq"), None, None)
    one, two = P("fsdp"), P("fsdp", None)
    params = (one, one, two, one, two, one, one, one, two, one, two, one)
    return jax.shard_map(
        on_device,
        mesh=mesh,
        in_specs=(row, P(None, "fsdp")) + params + (row,),
        out_specs=(row, row) + params,
        check_vma=False,
    )
```

```python
import jax
import jax.numpy as jnp
from jax import lax
from jax.experimental import pallas as pl
from jax.experimental.pallas import tpu as pltpu
from jax.sharding import PartitionSpec as P

HEADS = 16
HD = 64
LANES = 256
PER = LANES // HD
TILE = 1024
HEIGHTS = 3
WIDE = 512
PARTS = 2
SCALE = HD ** (-0.5)
epsilon = 1e-05
BF = jnp.bfloat16
F32 = jnp.float32


def nt(a, b):
    return lax.dot_general(a, b, (((1,), (1,)), ((), ())), preferred_element_type=F32)


def tn(a, b):
    return lax.dot_general(a, b, (((0,), (0,)), ((), ())), preferred_element_type=F32)


def nn(a, b):
    return jnp.dot(a, b, preferred_element_type=F32)


def by_head(value):
    lane = lax.broadcasted_iota(jnp.int32, value.shape, 1) // HD
    zero = jnp.zeros_like(value)
    return jnp.concatenate([jnp.where(lane == h, value, zero) for h in range(PER)])


def own_lanes(value):
    slots = value.shape[0] // PER
    lane = lax.broadcasted_iota(jnp.int32, (slots, LANES), 1) // HD
    total = value[:slots]
    for h in range(1, PER):
        total = jnp.where(lane == h, value[h * slots : (h + 1) * slots], total)
    return total


def probabilities(k, heads, live):
    s = nt(k, heads)
    s = jnp.where(lax.broadcasted_iota(jnp.int32, s.shape, 0) < live, s, -1e30)
    e = jnp.exp(s - jnp.max(s, axis=0, keepdims=True))
    return e * (1.0 / jnp.sum(e, axis=0, keepdims=True))


def attention_forward(counts_ref, qkv_ref, out_ref):
    width = qkv_ref.shape[1] // 3
    live = counts_ref[pl.program_id(0)]
    for g in range(width // LANES):
        q = qkv_ref[:, pl.ds(g * LANES, LANES)] * jnp.asarray(SCALE, BF)
        k = qkv_ref[:, pl.ds(width + g * LANES, LANES)]
        v = qkv_ref[:, pl.ds(2 * width + g * LANES, LANES)]
        p = probabilities(k, by_head(q), live)
        out_ref[:, pl.ds(g * LANES, LANES)] = own_lanes(tn(p.astype(BF), v)).astype(BF)


def attention_backward(counts_ref, qkv_ref, do_ref, out_ref):
    width = qkv_ref.shape[1] // 3
    live = counts_ref[pl.program_id(0)]
    for g in range(width // LANES):
        q = qkv_ref[:, pl.ds(g * LANES, LANES)] * jnp.asarray(SCALE, BF)
        k = qkv_ref[:, pl.ds(width + g * LANES, LANES)]
        v = qkv_ref[:, pl.ds(2 * width + g * LANES, LANES)]
        heads, do_heads = by_head(q), by_head(do_ref[:, pl.ds(g * LANES, LANES)])
        p = probabilities(k, heads, live)
        dp = nt(v, do_heads)
        ds = (p * (dp - jnp.sum(p * dp, axis=0, keepdims=True))).astype(BF)
        out_ref[:, pl.ds(g * LANES, LANES)] = (own_lanes(tn(ds, k)) * SCALE).astype(BF)
        out_ref[:, pl.ds(width + g * LANES, LANES)] = nn(ds, heads).astype(BF)
        out_ref[:, pl.ds(2 * width + g * LANES, LANES)] = nn(p.astype(BF), do_heads).astype(BF)


def per_image(kernel, counts, slots, arrays, out_width):
    rows = arrays[0].shape[0]
    return pl.pallas_call(
        kernel,
        grid_spec=pltpu.PrefetchScalarGridSpec(
            num_scalar_prefetch=1,
            grid=(rows // slots,),
            in_specs=[pl.BlockSpec((slots, a.shape[1]), lambda i, c: (i, 0)) for a in arrays],
            out_specs=pl.BlockSpec((slots, out_width), lambda i, c: (i, 0)),
        ),
        out_shape=jax.ShapeDtypeStruct((rows, out_width), BF),
        compiler_params=pltpu.CompilerParams(vmem_limit_bytes=48 * 2**20),
    )(counts, *arrays)


def packed_rows(parts):
    rows = [part.reshape(part.shape[:-1] + (-1, 128)) for part in parts]
    total, start = 0, 0
    count = sum(part.shape[-2] for part in rows)
    for part in rows:
        size = part.shape[-2]
        edges = [(0, 0)] * (part.ndim - 2) + [(start, count - start - size), (0, 0)]
        total = total + jnp.pad(part, edges)
        start += size
    return total


def small_table(where, column, parts):
    planes = column.shape[0]
    both = jnp.stack([column, send(column, 0, 1, 0)])
    flips = (where[1] + jnp.arange(2)) % 2
    whole = both[flips].transpose(1, 0, 2, 3).reshape(2 * planes, -1)
    return cut(whole, parts)


def cut(whole, parts):
    result, start = [], 0
    for part in parts:
        size = part.shape[0]
        result.append(whole[:, start : start + size].reshape(-1).astype(F32))
        start += size
    return result


def complete(small, width):
    half = small[2]
    middle = jnp.zeros((width,), F32)
    return small[:2] + [jnp.concatenate([half[:width], middle, half[width:]])] + small[3:]


def own_parts(own, parts):
    result, start = [], 0
    for part in parts:
        size = part.shape[0] // lax.axis_size("fsdp")
        result.append(own[start : start + size])
        start += size
    return result


def send(value, step, flip_core, flip_seq):
    shards, others = lax.axis_size("fsdp"), lax.axis_size("seq")
    pairs = [
        (i * others + j, ((i + 2 * step) % shards ^ flip_core) * others + (j ^ flip_seq))
        for i in range(shards)
        for j in range(others)
    ]
    return lax.ppermute(value, ("fsdp", "seq"), pairs)


def after(value, *earlier):
    return lax.optimization_barrier((value, earlier))[0]


def pick(value, index, axis=0):
    return lax.dynamic_index_in_dim(value, index, axis=axis, keepdims=False)


def place():
    shard = lax.axis_index("fsdp")
    return jnp.stack([shard // 2, shard % 2, lax.axis_index("seq")]).astype(jnp.int32)


def by_hand():
    return lax.axis_size("seq") == 4 and lax.axis_size("fsdp") == 8


def assemble(where, owns, pieces, targets):
    planes, depth = pieces[0][0].shape[:2]
    planes += 1
    half = depth // 2
    flat = [*owns[0], *pieces[0], *owns[1], *pieces[1]]
    each = len(flat) // 2
    widths = [own.shape[1] // 4 for own in owns[0]]
    total = len(targets) * 2 * (4 + (planes - 1) * 5)

    def kernel(place_ref, *refs):
        ins, outs = refs[: len(flat)], refs[len(flat) : -3]
        held, in_sems, out_sems = refs[-3:]
        z, core, me = place_ref[0], place_ref[1], place_ref[2]
        places = [me, me + 1 - 2 * (me % 2), (me + 2) % 4, 3 - me, 3 - me]
        parts = [(0, depth), (0, depth), (0, depth), (0, half), (half, half)]

        moves = []
        for flip_core in range(2):
            for target, wide in enumerate(widths):
                shard = 2 * z + (core + flip_core) % 2
                own = ins[flip_core * each + target]
                for unit in range(4):
                    source = own.at[:, pl.ds(unit * wide, wide)]
                    moves.append((source, shard, jnp.int32(unit), 0, depth, target))
        for flip_core in range(2):
            others = ins[(flip_core + 1) * each - 5 : (flip_core + 1) * each]
            for step in range(1, planes):
                shard = 2 * ((z + planes - step) % planes) + (core + flip_core) % 2
                for n, spot in enumerate(places):
                    for target, wide in enumerate(widths):
                        source = others[n].at[step - 1, :, pl.ds(sum(widths[:target]), wide)]
                        moves.append((source, shard, spot, *parts[n], target))

        def bring(n):
            source, _, _, _, size, target = moves[n]
            spot = held.at[n, pl.ds(0, size), pl.ds(0, widths[target])]
            return pltpu.make_async_copy(source, spot, in_sems.at[n])

        def put(n):
            _, shard, unit, first, size, target = moves[n]
            wide = widths[target]
            row = pl.multiple_of(shard * depth + first, half)
            column = pl.multiple_of(unit * wide, wide)
            return pltpu.make_async_copy(
                held.at[n, pl.ds(0, size), pl.ds(0, wide)],
                outs[target].at[pl.ds(row, size), pl.ds(column, wide)],
                out_sems.at[n],
            )

        for n in range(total):
            bring(n).start()
        for n in range(total):
            bring(n).wait()
            put(n).start()
        for n in range(total):
            put(n).wait()

    return pl.pallas_call(
        kernel,
        in_specs=[pl.BlockSpec(memory_space=pltpu.SMEM)]
        + [pl.BlockSpec(memory_space=pl.ANY)] * len(flat),
        out_specs=[pl.BlockSpec(memory_space=pltpu.HBM)] * len(targets),
        out_shape=[jax.ShapeDtypeStruct(shape, BF) for shape in targets],
        scratch_shapes=[
            pltpu.VMEM((total, depth, max(widths)), BF),
            pltpu.SemaphoreType.DMA((total,)),
            pltpu.SemaphoreType.DMA((total,)),
        ],
        compiler_params=pltpu.CompilerParams(vmem_limit_bytes=58 * 2**20),
    )(where, *flat)


def halves(place_ref, total, depth):
    first = place_ref[1] == 0
    for n in range(total.shape[0] // (2 * depth)):
        low = total[2 * n * depth : (2 * n + 1) * depth].astype(BF)
        high = total[(2 * n + 1) * depth : (2 * n + 2) * depth].astype(BF)
        yield n, jnp.where(first, low, high), jnp.where(first, high, low)


def pieces_to(place_ref, ins, widths, held, sems):
    each = len(ins) // 2
    planes, depth = ins[each - 5].shape[0] + 1, ins[each - 5].shape[1]
    half = depth // 2
    z, core, me = place_ref[0], place_ref[1], place_ref[2]
    places = [me, me + 1 - 2 * (me % 2), (me + 2) % 4, 3 - me, 3 - me]
    parts = [(0, depth), (0, depth), (0, depth), (0, half), (half, half)]
    lists, count = [], 0
    for target, wide in enumerate(widths):
        copies = []
        for flip_core in range(2):
            side = (core + flip_core) % 2
            mine = ins[flip_core * each : (flip_core + 1) * each]
            sources = [
                (mine[target].at[:, pl.ds(unit * wide, wide)], 2 * z + side, unit, 0, depth)
                for unit in range(4)
            ]
            for step in range(1, planes):
                shard = 2 * ((z + planes - step) % planes) + side
                for other, spot, part in zip(mine[each - 5 :], places, parts):
                    source = other.at[step - 1, :, pl.ds(sum(widths[:target]), wide)]
                    sources.append((source, shard, spot, *part))
            for source, shard, unit, first, size in sources:
                row = pl.multiple_of(shard * depth + first, half)
                column = pl.multiple_of(jnp.int32(unit) * wide, wide)
                spot = held[target].at[pl.ds(row, size), pl.ds(column, wide)]
                copies.append(pltpu.make_async_copy(source, spot, sems.at[count]))
                count += 1
        lists.append(copies)
    return lists


def piece_count(pieces, targets):
    return targets * 2 * (4 + pieces[0][0].shape[0] * 5)


def assembled_project(where, owns, pieces, a, bias):
    flat = [*owns[0], *pieces[0], *owns[1], *pieces[1]]
    rows, width = a.shape
    wide = owns[0][0].shape[1]
    steps = wide // TILE

    def kernel(place_ref, *refs):
        ins, refs = refs[: len(flat)], refs[len(flat) :]
        a_ref, b_ref, y_ref, qkv_ref, out_ref, qkv, out, sems, done = refs
        step = pl.program_id(0)
        qkv_copies, out_copies = pieces_to(
            place_ref, ins, [wide // 4, width // 4], [qkv, out], sems
        )
        qkv_whole = pltpu.make_async_copy(qkv, qkv_ref, done.at[0])
        out_whole = pltpu.make_async_copy(out, out_ref, done.at[1])

        @pl.when(step == 0)
        def _():
            for copy in qkv_copies + out_copies:
                copy.start()
            for copy in qkv_copies:
                copy.wait()
            qkv_whole.start()

        @pl.when(step == 1)
        def _():
            for copy in out_copies:
                copy.wait()
            out_whole.start()

        w = qkv[:, pl.ds(pl.multiple_of(step * TILE, TILE), TILE)]
        y_ref[...] = (nn(a_ref[...], w) + b_ref[...]).astype(BF)

        @pl.when(step == steps - 1)
        def _():
            qkv_whole.wait()
            out_whole.wait()

    far = pl.BlockSpec(memory_space=pltpu.HBM)
    return call(
        kernel,
        (steps,),
        [pl.BlockSpec(memory_space=pltpu.SMEM)]
        + [pl.BlockSpec(memory_space=pl.ANY)] * len(flat)
        + [whole(a), columns_of(1, TILE)],
        [columns_of(rows, TILE), far, far],
        [struct(rows, wide), struct(width, wide), struct(width, width)],
        [
            pltpu.VMEM((width, wide), BF),
            pltpu.VMEM((width, width), BF),
            pltpu.SemaphoreType.DMA((piece_count(pieces, 2),)),
            pltpu.SemaphoreType.DMA((2,)),
        ],
        (where, *flat, a, bias[None]),
    )


def assembled_middle(where, owns, pieces, o, w, x, bias, gain, shift):
    flat = [*owns[0], *pieces[0], *owns[1], *pieces[1]]
    rows, width = x.shape
    wide = owns[0][0].shape[1]
    height = rows // 4

    def kernel(place_ref, *refs):
        ins, refs = refs[: len(flat)], refs[len(flat) :]
        o_ref, w_ref, x_ref, b_ref, gain_ref, shift_ref, y_ref, a_ref, up_ref = refs[:9]
        up, sems, done = refs[9:]
        step = pl.program_id(0)
        (copies,) = pieces_to(place_ref, ins, [wide // 4], [up], sems)
        up_whole = pltpu.make_async_copy(up, up_ref, done.at[0])

        @pl.when(step == 0)
        def _():
            for copy in copies:
                copy.start()

        @pl.when(step == 1)
        def _():
            for copy in copies:
                copy.wait()
            up_whole.start()

        y = nn(o_ref[...], w_ref[...]) + x_ref[...].astype(F32) + b_ref[...]
        y_ref[...] = y
        unit, _ = normal(y)
        a_ref[...] = (unit * gain_ref[...] + shift_ref[...]).astype(BF)

        @pl.when(step == 3)
        def _():
            up_whole.wait()

    tile = rows_of(height, width)
    vectors = [bias[None], gain[None], shift[None]]
    return call(
        kernel,
        (4,),
        [pl.BlockSpec(memory_space=pltpu.SMEM)]
        + [pl.BlockSpec(memory_space=pl.ANY)] * len(flat)
        + [tile, whole(w), tile]
        + [whole(v) for v in vectors],
        [tile, tile, pl.BlockSpec(memory_space=pltpu.HBM)],
        [struct(rows, width, dtype=F32), struct(rows, width), struct(width, wide)],
        [
            pltpu.VMEM((width, wide), BF),
            pltpu.SemaphoreType.DMA((piece_count(pieces, 1),)),
            pltpu.SemaphoreType.DMA((1,)),
        ],
        (where, *flat, o, w, x, *vectors),
    )


def wgrad_call(kernel, where, grid, specs, outs, shapes, arrays, scratch=()):
    return pl.pallas_call(
        kernel,
        grid_spec=pltpu.PrefetchScalarGridSpec(
            num_scalar_prefetch=1,
            grid=grid,
            in_specs=specs,
            out_specs=outs,
            scratch_shapes=scratch,
        ),
        out_shape=[jax.ShapeDtypeStruct(shape, BF) for shape in shapes],
        compiler_params=pltpu.CompilerParams(vmem_limit_bytes=50 * 2**20),
    )(where, *arrays)


def wgrad_units(where, left, right, extra=()):
    rows, width = left.shape
    shards = lax.axis_size("fsdp")
    planes, depth, wide = shards // 2, width // shards, right.shape[1] // 4
    part = extra[1].shape[1] // 4 if extra else 0
    count = 2 + len(extra)

    def kernel(place_ref, *refs):
        ins, outs, held = refs[:count], refs[count : count + 2], refs[count + 2 :]
        step = pl.program_id(0)
        if extra:

            @pl.when(step == 0)
            def _():
                for n, mine, far in halves(place_ref, tn(ins[2][...], ins[3][...]), depth):
                    for j in range(4):
                        held[0][j, n] = mine[:, j * part : (j + 1) * part]
                        held[1][j, n] = far[:, j * part : (j + 1) * part]

        for n, mine, far in halves(place_ref, tn(ins[0][...], ins[1][...]), depth):
            outs[0][n, :, pl.ds(0, wide)] = mine
            outs[1][n, :, pl.ds(0, wide)] = far
        if extra:
            for out, kept in zip(outs, held):
                out[:, :, pl.ds(wide, part)] = kept[step]

    one = pl.BlockSpec((rows, width), lambda j, c: (0, 0), pipeline_mode=pl.Buffered(1))
    specs = [one, pl.BlockSpec((rows, wide), lambda j, c: (0, j))] + [one] * len(extra)
    out = pl.BlockSpec((None, planes, depth, wide + part), lambda j, c: (j, 0, 0, 0))
    shape = (4, planes, depth, wide + part)
    scratch = [pltpu.VMEM((4, planes, depth, part), BF)] * 2 if extra else []
    arrays = (left, right, *extra)
    return wgrad_call(kernel, where, (4,), specs, [out] * 2, [shape] * 2, arrays, scratch)


def wgrad_planes(where, left, right):
    rows, width = right.shape
    planes = lax.axis_size("fsdp") // 2
    depth, wide = left.shape[1] // (2 * planes), width // 4

    def kernel(place_ref, left_ref, right_ref, mine_ref, far_ref):
        for _, mine, far in halves(place_ref, tn(left_ref[...], right_ref[...]), depth):
            for j in range(4):
                mine_ref[j] = mine[:, j * wide : (j + 1) * wide]
                far_ref[j] = far[:, j * wide : (j + 1) * wide]

    specs = [
        pl.BlockSpec((rows, 2 * depth), lambda z, c: (0, z)),
        pl.BlockSpec((rows, width), lambda z, c: (0, 0), pipeline_mode=pl.Buffered(1)),
    ]
    out = pl.BlockSpec((4, None, depth, wide), lambda z, c: (0, z, 0, 0))
    shape = (4, planes, depth, wide)
    return wgrad_call(kernel, where, (planes,), specs, [out] * 2, [shape] * 2, (left, right))


def add(*parts):
    if len(parts) == 2:
        return parts[0] + parts[1]
    total = parts[0].astype(F32)
    for part in parts[1:]:
        total += part.astype(F32)
    return total.astype(BF)


def chip_sum(where, mine, far):
    planes, depth = mine[0].shape[1:3]
    wides = [part.shape[3] for part in mine]
    half = planes // 2

    def kernel(place_ref, *refs):
        ins, outs = refs[: 2 * len(wides)], refs[2 * len(wides) :]
        for flip, (first, second) in enumerate(((0, 2), (1, 2), (0, 3), (1, 3))):

            @pl.when(pl.program_id(0) == flip)
            def _():
                for n, wide in enumerate(wides):
                    columns = pl.ds(sum(wides[:n]), wide)
                    total = add(ins[n][...], ins[len(wides) + n][...])
                    outs[first][flip // 2, :, :, columns] = total[:half]
                    outs[second][flip % 2, :, :, columns] = total[half:]

    piece = (2, half, depth, sum(wides))
    return pl.pallas_call(
        kernel,
        grid_spec=pltpu.PrefetchScalarGridSpec(
            num_scalar_prefetch=1,
            grid=(4,),
            in_specs=[
                pl.BlockSpec((None, planes, depth, wide), lambda f, c: (c[2] ^ f, 0, 0, 0))
                for wide in wides
            ]
            * 2,
            out_specs=[pl.BlockSpec(piece, lambda f, c: (0, 0, 0, 0))] * 4,
        ),
        out_shape=[jax.ShapeDtypeStruct(piece, BF)] * 4,
        compiler_params=pltpu.CompilerParams(vmem_limit_bytes=40 * 2**20),
    )(where, *mine, *far)


def sides(chip):
    return [send(chip[1], 0, 0, 1), send(chip[3], 0, 0, 2)]


def side_sum(chip, got):
    half, depth, wide = chip[0].shape[1:]

    def kernel(a_ref, ga_ref, b_ref, gb_ref, *outs):
        for own, other, outs_of in ((a_ref, ga_ref, outs[:2]), (b_ref, gb_ref, outs[2:])):
            for n in range(2):

                @pl.when(pl.program_id(0) == n)
                def _():
                    outs_of[n][...] = add(own[...], other[...])

    return pl.pallas_call(
        kernel,
        grid=(2,),
        in_specs=[pl.BlockSpec((None, half, depth, wide), lambda n: (n, 0, 0, 0))] * 4,
        out_specs=[pl.BlockSpec((half, depth, wide), lambda n: (0, 0, 0))] * 4,
        out_shape=[jax.ShapeDtypeStruct((half, depth, wide), BF)] * 4,
        compiler_params=pltpu.CompilerParams(vmem_limit_bytes=32 * 2**20),
    )(chip[0], got[0], chip[2], got[1])


def ends(side):
    return [send(side[1], 0, 0, 2), send(side[3], 0, 0, 1)]


def plane_sum(side, got):
    half, depth, wide = side[0].shape
    parts = [side[0], got[0], side[2], got[1]]

    def kernel(*refs):
        out = refs[-1]
        for n in range(half):
            out[n] = add(refs[0][n], refs[1][n])
            out[half + n] = add(refs[2][n], refs[3][n])

    return pl.pallas_call(
        kernel,
        in_specs=[pl.BlockSpec(memory_space=pltpu.VMEM)] * 4,
        out_shape=jax.ShapeDtypeStruct((2 * half, depth, wide), BF),
        compiler_params=pltpu.CompilerParams(vmem_limit_bytes=24 * 2**20),
    )(*parts)


def plane_columns(where, side, got, last):
    half, depth, wide = side[0].shape
    planes, more = 2 * half, 16
    parts = [side[0], got[0], side[2], got[1], last]

    def kernel(place_ref, *refs):
        ins, outs = refs[:5], refs[5:]
        for step in range(planes):
            at = (place_ref[0] + step) % planes

            @pl.when(at < half)
            def _():
                outs[step][pl.ds(0, depth), :] = add(ins[0][at], ins[1][at])

            @pl.when(at >= half)
            def _():
                outs[step][pl.ds(0, depth), :] = add(ins[2][at - half], ins[3][at - half])

            outs[step][pl.ds(depth, more), :] = ins[4][at]

    return pl.pallas_call(
        kernel,
        in_specs=[pl.BlockSpec(memory_space=pltpu.SMEM)]
        + [pl.BlockSpec(memory_space=pltpu.VMEM)] * 5,
        out_shape=[jax.ShapeDtypeStruct((depth + more, wide), BF)] * planes,
        compiler_params=pltpu.CompilerParams(vmem_limit_bytes=24 * 2**20),
    )(where, *parts)


def column_parts(parts):
    return [parts[0]] + [send(part, step, 0, 0) for step, part in enumerate(parts) if step]


def column_groups():
    shards = lax.axis_size("fsdp")
    return [list(range(c, shards, 2)) for c in range(2)]


def column_sum(total):
    return lax.psum_scatter(
        total, "fsdp", scatter_dimension=0, tiled=False, axis_index_groups=column_groups()
    )


def from_plane(share):
    return lax.all_gather(share, "seq", axis=0, tiled=False)


def joined(units, widths):
    count, depth, _ = units.shape

    def kernel(in_ref, *outs):
        for n, (wide, out_ref) in enumerate(zip(widths, outs)):
            for j in range(count):
                value = in_ref[j, :, pl.ds(sum(widths[:n]), wide)].astype(F32)
                out_ref[:, pl.ds(j * wide, wide)] = value

    return pl.pallas_call(
        kernel,
        in_specs=[pl.BlockSpec(memory_space=pltpu.VMEM)],
        out_specs=[pl.BlockSpec(memory_space=pltpu.VMEM)] * len(widths),
        out_shape=[jax.ShapeDtypeStruct((depth, count * wide), F32) for wide in widths],
        compiler_params=pltpu.CompilerParams(vmem_limit_bytes=24 * 2**20),
    )(units)


def shares(total):
    return [total] + over_plane(total)


def spread(where, parts, widths, more=0):
    depth = parts[0].shape[0] - (16 if more else 0)

    def kernel(place_ref, *refs):
        ins, outs = refs[: len(parts)], refs[len(parts) :]
        me = place_ref[2]
        for spot, ref in zip([me, me + 1 - 2 * (me % 2), (me + 2) % 4, 3 - me], ins):
            for n, wide in enumerate(widths):
                column = pl.ds(pl.multiple_of(spot * wide, wide), wide)
                value = ref[pl.ds(0, depth), pl.ds(sum(widths[:n]), wide)]
                outs[n][:, column] = value.astype(F32)
        if more:
            rows = [ref[pl.ds(depth, 16), :].astype(F32) for ref in ins]
            outs[-1][...] = (rows[0] + rows[1] + rows[2] + rows[3])[:more]

    shapes = [struct(depth, 4 * wide, dtype=F32) for wide in widths]
    if more:
        shapes.append(struct(more, parts[0].shape[1], dtype=F32))
    return pl.pallas_call(
        kernel,
        in_specs=[pl.BlockSpec(memory_space=pltpu.SMEM)]
        + [pl.BlockSpec(memory_space=pltpu.VMEM)] * len(parts),
        out_shape=shapes,
        compiler_params=pltpu.CompilerParams(vmem_limit_bytes=24 * 2**20),
    )(where, *parts)


def along_z(mine):
    return [send(mine, step, 0, 0) for step in range(1, lax.axis_size("fsdp") // 2)]


def over_plane(value):
    return [send(value, 0, 0, flip) for flip in (1, 2, 3)]


def to_partner(values):
    return [send(value, 0, 1, 0) for value in values]


def column(mine):
    return lax.all_gather(
        mine, "fsdp", axis=0, tiled=False, axis_index_groups=column_groups()
    )


def others(where, whole, depth):
    planes = whole.shape[0]
    return jnp.stack(
        [pick(whole, (where[0] + planes - step) % planes)[:depth] for step in range(1, planes)]
    )


def edges(two):
    half = two[0].shape[1] // 2
    return [two[0][:, :half], two[1][:, half:]]


def across(parts):
    return [send(parts[0], 0, 0, 2), send(parts[1], 0, 0, 1)]


def plain_sum(left, right):
    share = lax.psum_scatter(tn(left, right).astype(BF), "fsdp", scatter_dimension=0, tiled=True)
    return lax.psum(share, "seq").astype(F32)


def normal(values):
    center = values - jnp.mean(values, axis=-1, keepdims=True)
    inverse = lax.rsqrt(jnp.mean(center * center, axis=-1, keepdims=True) + epsilon)
    return center * inverse, inverse


def norm_back(grad, unit, inverse, gain):
    e = grad * gain
    return inverse * (
        e
        - jnp.mean(e, axis=-1, keepdims=True)
        - unit * jnp.mean(e * unit, axis=-1, keepdims=True)
    )


def gelu_and_slope(u):
    c = 0.7978845608
    square = u * u
    t = jnp.tanh(u * (c + (0.044715 * c) * square))
    half = 0.5 + 0.5 * t
    hid = u * half
    return hid, half + hid * (1.0 - t) * (c + (3 * 0.044715 * c) * square)


def call(kernel, grid, in_specs, out_specs, out_shape, scratch, args, room=56):
    return pl.pallas_call(
        kernel,
        grid=grid,
        in_specs=in_specs,
        out_specs=out_specs,
        out_shape=out_shape,
        scratch_shapes=scratch,
        compiler_params=pltpu.CompilerParams(vmem_limit_bytes=room * 2**20),
    )(*args)


def whole(array):
    return pl.BlockSpec(array.shape, lambda *i: (0,) * array.ndim, pipeline_mode=pl.Buffered(1))


def rows_of(height, width):
    return pl.BlockSpec((height, width), lambda i: (i, 0))


def columns_of(height, width):
    return pl.BlockSpec((height, width), lambda i: (0, i))


def struct(*shape, dtype=BF):
    return jax.ShapeDtypeStruct(shape, dtype)


def project(a, w, bias):
    rows, wide = a.shape[0], w.shape[1]

    def kernel(a_ref, w_ref, b_ref, out_ref):
        out_ref[...] = (nn(a_ref[...], w_ref[...]) + b_ref[...]).astype(BF)

    return call(
        kernel,
        (wide // TILE,),
        [whole(a), columns_of(w.shape[0], TILE), columns_of(1, TILE)],
        columns_of(rows, TILE),
        struct(rows, wide),
        [],
        (a, w, bias[None]),
    )


def middle(o, w, x, bias, gain, shift):
    rows, width = x.shape
    height = rows // 4

    def kernel(o_ref, w_ref, x_ref, b_ref, gain_ref, shift_ref, y_ref, a_ref):
        y = nn(o_ref[...], w_ref[...]) + x_ref[...].astype(F32) + b_ref[...]
        y_ref[...] = y
        unit, _ = normal(y)
        a_ref[...] = (unit * gain_ref[...] + shift_ref[...]).astype(BF)

    tile = rows_of(height, width)
    vectors = [bias[None], gain[None], shift[None]]
    return call(
        kernel,
        (rows // height,),
        [tile, whole(w), tile] + [whole(v) for v in vectors],
        [tile, tile],
        [struct(rows, width, dtype=F32), struct(rows, width)],
        [],
        (o, w, x, *vectors),
    )


def expand(a, w, bias):
    rows, wide = a.shape[0], w.shape[1]

    def kernel(a_ref, w_ref, b_ref, hid_ref, slope_ref):
        for part in range(PARTS):
            at = pl.ds(part * (rows // PARTS), rows // PARTS)
            hid, slope = gelu_and_slope(nn(a_ref[at, :], w_ref[...]) + b_ref[...])
            hid_ref[at, :] = hid.astype(BF)
            slope_ref[at, :] = slope.astype(BF)

    tile = columns_of(rows, WIDE)
    return call(
        kernel,
        (wide // WIDE,),
        [whole(a), columns_of(w.shape[0], WIDE), columns_of(1, WIDE)],
        [tile, tile],
        [struct(rows, wide)] * 2,
        [],
        (a, w, bias[None]),
    )


def back_norm(total, values, gain):
    unit, inverse = normal(values)
    sums = (
        jnp.sum(total * unit, axis=0, keepdims=True),
        jnp.sum(total, axis=0, keepdims=True),
    )
    return norm_back(total, unit, inverse, gain), sums


def gather_sums(refs, sums):
    @pl.when(pl.program_id(0) == 0)
    def _():
        for ref, value in zip(refs, sums):
            ref[...] = value

    @pl.when(pl.program_id(0) > 0)
    def _():
        for ref, value in zip(refs, sums):
            ref[...] += value


def back_ffn(g, w_down, slope, w_up, y1, gain):
    rows, wide = slope.shape
    width = y1.shape[1]
    height, part = rows // HEIGHTS, wide // 4

    def kernel(g_ref, down_ref, slope_ref, up_ref, y_ref, gain_ref, *refs):
        du_ref, sum_ref, dy_ref, d1_ref, s1_ref, s2_ref, s3_ref, down, up, sems = refs
        first = pl.program_id(0) == 0

        def bring(n):
            at = pl.ds(n * part, part)
            return (
                pltpu.make_async_copy(down_ref.at[at, :], down.at[at, :], sems.at[2 * n]),
                pltpu.make_async_copy(up_ref.at[:, at], up.at[:, at], sems.at[2 * n + 1]),
            )

        @pl.when(first)
        def _():
            sum_ref[...] = jnp.zeros_like(sum_ref)
            for n in range(4):
                for copy in bring(n):
                    copy.start()

        total = None
        for n in range(4):
            at = pl.ds(n * part, part)

            @pl.when(first)
            def _():
                for copy in bring(n):
                    copy.wait()

            dh = nt(g_ref[...], down[at, :])
            du = (dh * slope_ref[:, at].astype(F32)).astype(BF)
            du_ref[:, at] = du
            sum_ref[:, at] += jnp.sum(du.astype(F32), axis=0, keepdims=True)
            more = nt(du, up[:, at])
            total = more if total is None else total + more
        back, sums = back_norm(total, y_ref[...], gain_ref[...])
        dy = g_ref[...].astype(F32) + back
        dy_ref[...] = dy
        d1 = dy.astype(BF)
        d1_ref[...] = d1
        sums += (jnp.sum(d1.astype(F32), axis=0, keepdims=True),)
        gather_sums((s1_ref, s2_ref, s3_ref), sums)

    tile, long = rows_of(height, width), rows_of(height, wide)
    row = pl.BlockSpec((1, width), lambda i: (0, 0))
    far = pl.BlockSpec(memory_space=pl.ANY)
    vector = struct(1, width, dtype=F32)
    return call(
        kernel,
        (rows // height,),
        [tile, far, long, far, tile, whole(gain[None])],
        [long, pl.BlockSpec((1, wide), lambda i: (0, 0)), tile, tile, row, row, row],
        [
            struct(rows, wide),
            struct(1, wide, dtype=F32),
            struct(rows, width, dtype=F32),
            struct(rows, width),
            vector,
            vector,
            vector,
        ],
        [
            pltpu.VMEM(w_down.shape, BF),
            pltpu.VMEM(w_up.shape, BF),
            pltpu.SemaphoreType.DMA((8,)),
        ],
        (g, w_down, slope, w_up, y1, gain[None]),
    )


def back_out(d1, w):
    rows, width = d1.shape

    def kernel(d_ref, w_ref, out_ref):
        out_ref[...] = nt(d_ref[...], w_ref[...]).astype(BF)

    return call(
        kernel,
        (width // 512,),
        [whole(d1), rows_of(512, width)],
        columns_of(rows, 512),
        struct(rows, width),
        [],
        (d1, w),
    )


def back_qkv(dqkv, w, x, dy1, gain):
    rows, wide = dqkv.shape
    width = x.shape[1]
    height = rows // HEIGHTS

    def kernel(d_ref, w_ref, x_ref, dy_ref, gain_ref, dx_ref, s1_ref, s2_ref, s3_ref):
        back, sums = back_norm(
            nt(d_ref[...], w_ref[...]), x_ref[...].astype(F32), gain_ref[...]
        )
        dx_ref[...] = (dy_ref[...] + back).astype(BF)
        sums += (jnp.sum(d_ref[...].astype(F32), axis=0, keepdims=True),)
        gather_sums((s1_ref, s2_ref, s3_ref), sums)

    row, tile = pl.BlockSpec((1, width), lambda i: (0, 0)), rows_of(height, width)
    long = pl.BlockSpec((1, wide), lambda i: (0, 0))
    vector = struct(1, width, dtype=F32)
    return call(
        kernel,
        (rows // height,),
        [rows_of(height, wide), whole(w), tile, tile, whole(gain[None])],
        [tile, row, row, long],
        [struct(rows, width), vector, vector, struct(1, wide, dtype=F32)],
        [],
        (dqkv, w, x, dy1, gain[None]),
    )


def contract(hid, w, y1, bias):
    rows, wide = hid.shape
    width = w.shape[1]
    height = rows // HEIGHTS

    def kernel(h_ref, w_ref, y_ref, b_ref, out_ref):
        out_ref[...] = (nn(h_ref[...], w_ref[...]) + y_ref[...] + b_ref[...]).astype(BF)

    tile = rows_of(height, width)
    return call(
        kernel,
        (rows // height,),
        [rows_of(height, wide), whole(w), tile, whole(bias[None])],
        tile,
        struct(rows, width),
        [],
        (hid, w, y1, bias[None]),
    )


def plainly(
    tokens, live, x, g_low, small, w_qkv, w_out, w_up, w_down
):
    gain1, shift1, bias_qkv, bias_out, gain2, shift2, bias_up, bias_down = small
    slots, width = tokens.shape[2:]
    qkv_w, out_w, up_w, down_w = [
        lax.all_gather(w, "fsdp", axis=0, tiled=True) for w in (w_qkv, w_out, w_up, w_down)
    ]
    g = g_low.astype(F32)
    unit1, inverse1 = normal(x)
    a1 = (unit1 * gain1 + shift1).astype(BF)
    qkv = (nn(a1, qkv_w) + bias_qkv).astype(BF)
    o = per_image(attention_forward, live, slots, [qkv], width)
    y1 = x + nn(o, out_w) + bias_out
    unit2, inverse2 = normal(y1)
    a2 = (unit2 * gain2 + shift2).astype(BF)
    hid, slope = gelu_and_slope(nn(a2, up_w) + bias_up)
    hid = hid.astype(BF)
    s_down = plain_sum(hid, g_low)
    du = (nt(g_low, down_w) * slope).astype(BF)
    s_up = plain_sum(a2, du)
    activations = (y1 + nn(hid, down_w) + bias_down).astype(BF)
    da2 = nt(du, up_w)
    dy1 = g + norm_back(da2, unit2, inverse2, gain2)
    d1 = dy1.astype(BF)
    s_out = plain_sum(o, d1)
    do = nt(d1, out_w).astype(BF)
    dqkv = per_image(attention_backward, live, slots, [qkv, do], 3 * width)
    s_qkv = plain_sum(a1, dqkv)
    da1 = nt(dqkv, qkv_w)
    input_grad = (dy1 + norm_back(da1, unit1, inverse1, gain1)).astype(BF)
    sums = column_sums(da1, unit1, dqkv, d1, da2, unit2, du, g)
    shards = lax.axis_size("fsdp")
    packed = jnp.concatenate([part.reshape(shards, -1) for part in sums], axis=1)
    own = pick(lax.psum(packed, ("fsdp", "seq")), lax.axis_index("fsdp"))
    return activations, input_grad, s_qkv, s_out, s_up, s_down, own_parts(own, sums)


def column_sums(da1, unit1, dqkv, d1, da2, unit2, du, g):
    width = da1.shape[1]
    sums_qkv = jnp.sum(dqkv.astype(F32), axis=0)
    return (
        jnp.sum(da1 * unit1, axis=0),
        jnp.sum(da1, axis=0),
        jnp.concatenate([sums_qkv[:width], sums_qkv[2 * width :]]),
        jnp.sum(d1.astype(F32), axis=0),
        jnp.sum(da2 * unit2, axis=0),
        jnp.sum(da2, axis=0),
        jnp.sum(du.astype(F32), axis=0),
        jnp.sum(g, axis=0),
    )


def by_parts(where, tokens, live, x, g_low, vectors, w_qkv, w_out, w_up, w_down):
    slots, width = tokens.shape[2:]
    wide = w_up.shape[1]
    me = where[2]
    x_low = tokens.reshape(x.shape)

    def unit(w):
        return lax.dynamic_slice_in_dim(w, me * (w.shape[1] // 4), w.shape[1] // 4, axis=1)

    depth = w_qkv.shape[0]
    first = jnp.concatenate([unit(w_qkv), unit(w_out)], axis=1)
    z_first = along_z(first)
    packed = jnp.pad(packed_rows(vectors), ((0, 4), (0, 0))).reshape(2, width)
    packed = jnp.pad(packed, ((0, 14), (0, 0)))
    packed = jnp.concatenate([unit(w_up), packed])
    third = unit(w_down)
    z_second = column(after(packed, z_first, third))
    z_third = column(third)
    unit1, _ = normal(x)
    sum_down = jnp.sum(g_low.astype(F32), axis=0)

    far_own = to_partner(after([w_qkv, w_out], unit1))
    col_first = jnp.stack(after(z_first, far_own))
    far_own = far_own + to_partner(after([w_up, w_down], col_first))
    two_first = [send(col_first, 0, 0, flip) for flip in (1, 2)]
    far_first = to_partner([col_first])
    two_first, far_own, far_first = after((two_first, far_own, far_first), col_first)
    edges_first = edges(two_first)
    cross_first = across(edges_first)
    far_first = far_first + to_partner(two_first)
    z_second = after(z_second, edges_first)
    small = complete(small_table(where, z_second[:, depth : depth + 2, :width], vectors), width)
    gain1, shift1, bias_qkv, bias_out, gain2, shift2, bias_up, bias_down = small
    a1 = (unit1 * gain1 + shift1).astype(BF)
    col_second = others(where, z_second, depth)
    two_second = [send(col_second, 0, 0, flip) for flip in (1, 2)]
    cross_first = after(cross_first, col_second, a1)
    near_first = [col_first] + two_first + cross_first
    far_first = far_first + to_partner(cross_first)
    far_second = to_partner(after([col_second], far_first))
    qkv, qkv_w, out_w = assembled_project(
        where, [[w_qkv, w_out], far_own[:2]], [near_first, far_first], a1, bias_qkv
    )
    two_second, far_second = after((two_second, far_second), qkv)
    cross_second = across(edges(two_second))
    far_second = far_second + to_partner(two_second)
    o = per_image(attention_forward, live, slots, [after(qkv, two_second, sum_down)], width)
    cross_second, far_second = after((cross_second, far_second), o)
    near_second = [col_second] + two_second + cross_second
    far_second = far_second + to_partner(cross_second)
    y1, a2, up_w = assembled_middle(
        where,
        [[w_up], far_own[2:3]],
        [near_second, far_second],
        o,
        out_w,
        x_low,
        bias_out,
        gain2,
        shift2,
    )
    col_third = others(where, after(z_third, far_second), w_down.shape[0])
    two_third = [send(col_third, 0, 0, flip) for flip in (1, 2)]
    far_third = to_partner([col_third])
    hid, slope = expand(after(a2, col_third), up_w, bias_up)
    two_third, far_third = after((two_third, far_third), hid)
    edges_third = edges(two_third)
    cross_third = across(edges_third)
    far_third = far_third + to_partner(two_third)

    mine_down, far_down = wgrad_planes(where, after(hid, edges_third), g_low)
    cross_third, far_third = after((cross_third, far_third), mine_down)
    near_third = [col_third] + two_third + cross_third
    far_third = far_third + to_partner(cross_third)
    got_down = send(after(far_down, far_third), 0, 1, 0)
    (down_w,) = assemble(
        where,
        [[w_down], far_own[3:]],
        [near_third, far_third],
        [(wide, width)],
    )
    chip_down = chip_sum(where, *after(([mine_down], [got_down]), down_w))
    sides_down = sides(chip_down)
    du, sum_up, dy1, d1, sum_gain2, sum_shift2, sum_out = back_ffn(
        after(g_low, chip_down), down_w, slope, up_w, y1, gain2
    )
    side_down = side_sum(chip_down, after(sides_down, dy1))
    ends_down = ends(side_down)
    mine_up, far_up = wgrad_units(where, a2, after(du, side_down), (o, d1))
    total_down = plane_sum(side_down, after(ends_down, mine_up))
    got_up = send(after(far_up, total_down), 0, 1, 0)
    share_down = column_sum(total_down)
    do = back_out(after(d1, total_down), out_w)
    chip_up = chip_sum(where, *after(([mine_up], [got_up]), do))
    sides_up = sides(chip_up)
    dqkv = per_image(attention_backward, live, slots, [qkv, after(do, chip_up)], 3 * width)
    share_down = after(share_down, dqkv)
    side_up = side_sum(chip_up, after(sides_up, share_down))
    ends_up = ends(side_up)
    mine_qkv, far_qkv = wgrad_units(where, a1, after(dqkv, side_up))
    total_up = plane_sum(side_up, after(ends_up, mine_qkv))
    got_qkv = send(after(far_qkv, total_up), 0, 1, 0)
    share_up = column_sum(total_up)
    chip_qkv = chip_sum(where, *after(([mine_qkv], [got_qkv]), total_up))
    sides_qkv = sides(chip_qkv)
    input_grad, sum_gain1, sum_shift1, sum_qkv = back_qkv(
        after(dqkv, chip_qkv), qkv_w, x_low, dy1, gain1
    )
    side_qkv = side_sum(chip_qkv, after(sides_qkv, input_grad))
    ends_qkv = ends(side_qkv)

    sum_qv = jnp.concatenate([sum_qkv[0, :width], sum_qkv[0, 2 * width :]])
    sums = (
        sum_gain1[0],
        sum_shift1[0],
        sum_qv,
        sum_out[0],
        sum_gain2[0],
        sum_shift2[0],
        sum_up[0],
        sum_down,
    )
    planes = lax.axis_size("fsdp") // 2
    rows = packed_rows([part.reshape(planes, 2, -1) for part in sums])
    rows = pick(rows, where[1], 1) + send(pick(rows, 1 - where[1], 1), 0, 1, 0)
    rows = rows.reshape(planes, 2, -1).astype(BF)
    rows = jnp.pad(rows, ((0, 0), (0, 14), (0, 0)))

    from_down = from_plane(after(share_down, chip_qkv))
    column_qkv = column_parts(plane_columns(where, side_qkv, ends_qkv, rows))
    activations = contract(after(hid, column_qkv[0]), down_w, y1, bias_down)
    shares_up = shares(after(share_up, side_qkv))
    share_qkv = add(*after(column_qkv, activations))
    shares_qkv = shares(share_qkv)
    (s_down,) = joined(after(from_down, share_qkv), [width // 4])
    s_up, s_out = spread(where, after(shares_up, s_down), [wide // 4, width // 4])
    s_qkv, own = spread(where, after(shares_qkv, s_up), [width * 3 // 4], 2)
    own = own.reshape(-1)
    return activations, input_grad, s_qkv, s_out, s_up, s_down, own_parts(own, sums)


def on_device(
    tokens,
    counts,
    ln1_gain,
    ln1_shift,
    w_qkv,
    b_qv,
    w_out,
    b_out,
    ln2_gain,
    ln2_shift,
    w_up,
    b_up,
    w_down,
    b_down,
    cotangent,
):
    where = place()
    vectors = (ln1_gain, ln1_shift, b_qv, b_out, ln2_gain, ln2_shift, b_up, b_down)
    micro, images, slots, width = tokens.shape
    rows = micro * images * slots
    own_start = lax.axis_index("seq") * images
    live = lax.dynamic_slice_in_dim(counts, own_start, images, axis=1).reshape(-1)
    x = tokens.reshape(rows, width).astype(F32)
    g_low = cotangent.reshape(rows, width)
    weights = (w_qkv, w_out, w_up, w_down)
    if by_hand():
        found = by_parts(where, tokens, live, x, g_low, vectors, *weights)
    else:
        packed = lax.all_gather(jnp.concatenate(vectors), "fsdp", axis=0, tiled=False)
        small = complete(cut(packed, vectors), width)
        found = plainly(tokens, live, x, g_low, small, *weights)
    activations, input_grad, s_qkv, s_out, s_up, s_down, sums = found
    return (
        activations.reshape(tokens.shape),
        input_grad.reshape(tokens.shape),
        sums[0],
        sums[1],
        s_qkv,
        sums[2],
        s_out,
        sums[3],
        sums[4],
        sums[5],
        s_up,
        sums[6],
        s_down,
        sums[7],
    )


def solution(mesh):
    row = P(None, ("fsdp", "seq"), None, None)
    one, two = P("fsdp"), P("fsdp", None)
    params = (one, one, two, one, two, one, one, one, two, one, two, one)
    return jax.shard_map(
        on_device,
        mesh=mesh,
        in_specs=(row, P(None, "fsdp")) + params + (row,),
        out_specs=(row, row) + params,
        check_vma=False,
    )
```
